128 devices in a mesh: dp: 16 (over y, x), tensor: 8 (over z, core).
Axes of the slice: x: 4, y: 4, z: 4, core: 2. Of those that a mesh axis runs over, the one named last changes fastest.
Arguments:
- tokens: bfloat16 [8192, 2048], P('dp'), may hold values from -6 to 6
- segments: int32 [8192], P('dp'), may hold values from 0 to 8191, as said below
- weight_qkv: float32 [2048, 3072], P('dp', 'tensor'), may hold values from -0.125 to 0.125
- weight_out: float32 [2048, 2048], P('tensor', 'dp'), may hold values from -0.5 to 0.5
- weight_gate_up: float32 [2, 2048, 8192], P(None, 'dp', 'tensor'), may hold values from -0.125 to 0.125
- weight_down: float32 [8192, 2048], P('tensor', 'dp'), may hold values from -0.0625 to 0.0625
- norm_gains: float32 [2, 2048], replicated, may hold values from 0.5 to 1.5
- head_gains: float32 [2, 64], replicated, may hold values from 1 to 2
- first_qkv: float32 [2048, 3072], P('dp', 'tensor'), may hold values from -2048 to 2048
- first_out: float32 [2048, 2048], P('tensor', 'dp'), may hold values from -320 to 320
- first_gate_up: float32 [2, 2048, 8192], P(None, 'dp', 'tensor'), may hold values from -320 to 320
- first_down: float32 [8192, 2048], P('tensor', 'dp'), may hold values from -640 to 640
- first_norm: float32 [2, 2048], replicated, may hold values from -1536 to 1536
- first_head: float32 [2, 64], replicated, may hold values from -8192 to 8192
- second_qkv: float32 [2048, 3072], P('dp', 'tensor'), may hold values from 131072 to 524288
- second_out: float32 [2048, 2048], P('tensor', 'dp'), may hold values from 2949.12 to 11796.48
- second_gate_up: float32 [2, 2048, 8192], P(None, 'dp', 'tensor'), may hold values from 2949.12 to 11796.48
- second_down: float32 [8192, 2048], P('tensor', 'dp'), may hold values from 11796.48 to 47185.92
- second_norm: float32 [2, 2048], replicated, may hold values from 73728 to 294912
- second_head: float32 [2, 64], replicated, may hold values from 2097152 to 8388608
- cotangent: bfloat16 [8192, 2048], P('dp'), may hold values from -18 to 18
Outputs:
- block_out: bfloat16 [8192, 2048], P('dp')
- input_grad: bfloat16 [8192, 2048], P('dp')
- qkv_new: float32 [2048, 3072], P('dp', 'tensor')
- out_new: float32 [2048, 2048], P('tensor', 'dp')
- gate_up_new: float32 [2, 2048, 8192], P(None, 'dp', 'tensor')
- down_new: float32 [8192, 2048], P('tensor', 'dp')
- norm_gains_new: float32 [2, 2048], replicated
- head_gains_new: float32 [2, 64], replicated
- qkv_first: float32 [2048, 3072], P('dp', 'tensor')
- out_first: float32 [2048, 2048], P('tensor', 'dp')
- gate_up_first: float32 [2, 2048, 8192], P(None, 'dp', 'tensor')
- down_first: float32 [8192, 2048], P('tensor', 'dp')
- norm_first: float32 [2, 2048], replicated
- head_first: float32 [2, 64], replicated
- qkv_second: float32 [2048, 3072], P('dp', 'tensor')
- out_second: float32 [2048, 2048], P('tensor', 'dp')
- gate_up_second: float32 [2, 2048, 8192], P(None, 'dp', 'tensor')
- down_second: float32 [8192, 2048], P('tensor', 'dp')
- norm_second: float32 [2, 2048], replicated
- head_second: float32 [2, 64], replicated
- trust_stats: float32 [3, 6], replicated
The draws below stay inside these ranges and needn't reach their ends.
Inputs may be any that keep to these rules, and one draw needn't show every extreme that they name: `segments`: segment numbers never fall and start at 0; the last document of the sequence has the number 8192 - 1; one document begins within the first 512 tokens and ends within the last 512 tokens, the others lie before or after it.
All inputs are finite; a program needn't handle non-finite values.
Results may differ from the reference program's by a relative error of at most 0.03.
Values may be sent and summed in bfloat16 or wider, within the bound.
No kernel may reach another device: no remote copies, remote signals or barrier semaphores. Data moves between devices by JAX's collectives and lax.ppermute only.
A program may use at most 576 MiB of HBM per device.

```python
import math
import jax
import jax.numpy as jnp
from jax import lax

D = 2048
H = 32
KVH = 8
HD = 64
FF = 8192
TOK_DEV = 512
STEP = 5
QPK = 4
TOKENS = 8192


def draw_segments(key, part):
    key = jax.random.fold_in(key, 7)
    key_begin, key_finish, key_cuts = jax.random.split(key, 3)
    doc_begin = jax.random.randint(key_begin, (), 1, TOK_DEV)
    finish = TOKENS - jax.random.randint(key_finish, (), 1, TOK_DEV)
    cut_flags = jax.random.randint(key_cuts, (TOKENS,), 0, 6) == 0
    position_ids = jnp.arange(TOKENS, dtype=jnp.int32)
    outside = (position_ids < doc_begin) | (position_ids >= finish)
    boundary = (position_ids == doc_begin) | (position_ids == finish) | outside & cut_flags
    boundary = boundary & (position_ids > 0)
    numbers = jnp.cumsum(boundary.astype(jnp.int32)).astype(jnp.int32)
    last_number = numbers[TOKENS - 1]
    return jnp.where(numbers == last_number, jnp.int32(TOKENS - 1), numbers).astype(jnp.int32)


def rising_rows(base, top_factor):
    fraction = jnp.arange(TOKENS, dtype=jnp.float32) / max(TOKENS - 1, 1)
    return base * (1.0 + (top_factor - 1.0) * fraction)[:, None]


def draw_cotangent(key, part):
    key = jax.random.fold_in(key, 11)
    base = jnp.clip(jax.random.normal(key, (TOKENS, D), jnp.float32), -6.0, 6.0)
    return rising_rows(base, 3.0).astype(jnp.bfloat16)


def shard_levels(key, shape, cuts, smallest, largest):
    level, own = 1.0, jax.random.fold_in(key, 6)
    for axis_at, parts in cuts:
        heights = jnp.exp(jax.random.uniform(jax.random.fold_in(own, axis_at), (parts,), jnp.float32, smallest / len(cuts), largest / len(cuts)))
        level = level * jnp.repeat(heights, shape[axis_at] // parts).reshape([-1 if axis == axis_at else 1 for axis in range(len(shape))])
    return level


def scatter_about(stream_key, extent, deviation, limit, cuts=(), kind=jnp.bfloat16):
    loudness = shard_levels(stream_key, extent, cuts, -0.22, 0.18) if cuts else 1.0
    entries = jax.random.normal(stream_key, extent, jnp.float32) * deviation * loudness
    return jnp.minimum(jnp.maximum(entries, -limit), limit).astype(kind)


def setup_inputs(seed: int = 0) -> dict:
    key_list = jax.random.split(jax.random.key(seed), 22)
    return {
        "tokens": scatter_about(key_list[0], (TOKENS, D), 1.0, 6.0, ((0, 16),)),
        "segments": draw_segments(jax.random.fold_in(key_list[21], 71), 0),
        "weight_qkv": scatter_about(key_list[2], (D, (QPK + 2) * HD * KVH), D ** -0.5, 0.125, ((0, 16), (1, 8)), jnp.float32),
        "weight_out": scatter_about(key_list[3], (H * HD, D), (H * HD // 16) ** -0.5, 0.5, ((0, 8), (1, 16)), jnp.float32),
        "weight_gate_up": scatter_about(key_list[4], (2, D, FF), D ** -0.5, 0.125, ((1, 16), (2, 8)), jnp.float32),
        "weight_down": scatter_about(key_list[5], (FF, D), FF ** -0.5, 0.0625, ((0, 8), (1, 16)), jnp.float32),
        "norm_gains": jnp.clip(1.0 + 0.1 * jax.random.normal(key_list[6], (2, D), jnp.float32), 0.5, 1.5),
        "head_gains": jnp.clip(jax.random.uniform(key_list[7], (2, HD), jnp.float32, 1.0, 2.0), 1.0, 2.0),
        "first_qkv": scatter_about(key_list[8], (D, (QPK + 2) * HD * KVH), (4.0 * TOKENS ** 0.5), 2048.0, ((0, 16), (1, 8)), jnp.float32),
        "first_out": scatter_about(key_list[9], (H * HD, D), (0.6 * TOKENS ** 0.5), 320.0, ((0, 8), (1, 16)), jnp.float32),
        "first_gate_up": scatter_about(key_list[10], (2, D, FF), (0.6 * TOKENS ** 0.5), 320.0, ((1, 16), (2, 8)), jnp.float32),
        "first_down": scatter_about(key_list[11], (FF, D), (1.2 * TOKENS ** 0.5), 640.0, ((0, 8), (1, 16)), jnp.float32),
        "first_norm": scatter_about(key_list[12], (2, D), (3.0 * TOKENS ** 0.5), 1536.0, (), jnp.float32),
        "first_head": scatter_about(key_list[13], (2, HD), (16.0 * TOKENS ** 0.5), 8192.0, (), jnp.float32),
        "second_qkv": jnp.clip(jnp.exp(math.log(524288.0) - 1.3862944 * jax.random.uniform(key_list[14], (D, (QPK + 2) * HD * KVH), jnp.float32) ** shard_levels(key_list[14], (D, (QPK + 2) * HD * KVH), ((0, 16), (1, 8)), -0.2, 0.2)), 131072.0, 524288.0),
        "second_out": jnp.clip(jnp.exp(math.log(11796.48) - 1.3862944 * jax.random.uniform(key_list[15], (H * HD, D), jnp.float32) ** shard_levels(key_list[15], (H * HD, D), ((0, 8), (1, 16)), -0.2, 0.2)), 2949.12, 11796.48),
        "second_gate_up": jnp.clip(jnp.exp(math.log(11796.48) - 1.3862944 * jax.random.uniform(key_list[16], (2, D, FF), jnp.float32) ** shard_levels(key_list[16], (2, D, FF), ((1, 16), (2, 8)), -0.2, 0.2)), 2949.12, 11796.48),
        "second_down": jnp.clip(jnp.exp(math.log(47185.92) - 1.3862944 * jax.random.uniform(key_list[17], (FF, D), jnp.float32) ** shard_levels(key_list[17], (FF, D), ((0, 8), (1, 16)), -0.2, 0.2)), 11796.48, 47185.92),
        "second_norm": jnp.clip(jnp.exp(jax.random.uniform(key_list[18], (2, D), jnp.float32, math.log(73728.0), math.log(294912.0))), 73728.0, 294912.0),
        "second_head": jnp.clip(jnp.exp(jax.random.uniform(key_list[19], (2, HD), jnp.float32, math.log(2097152), math.log(8388608))), 2097152, 8388608),
        "cotangent": draw_cotangent(jax.random.fold_in(key_list[21], 71), 0),
    }


EPS_NORM = 1e-05
ROPE_BASE = 1000000.0
BETA_ONE = 0.5
BETA_TWO = 0.5
EPS_ADAM = 1e-06
DECAY = 0.01
RATE = 0.5
MASKED = -1e+30

@jax.custom_vjp
def low(v):
    return lax.optimization_barrier(v.astype(jnp.bfloat16)).astype(jnp.float32)

@jax.custom_vjp
def low_back(v):
    return v

def low_keep(v):
    return (low(v), None)

def low_pass(kept, grad):
    return (grad,)

def back_keep(v):
    return (v, None)

def back_low(kept, grad):
    return (low(grad),)
low.defvjp(low_keep, low_pass)
low_back.defvjp(back_keep, back_low)

def inverse_rms(array_in):
    return lax.rsqrt(lax.optimization_barrier(jnp.mean(array_in * array_in, axis=-1, keepdims=True)) + EPS_NORM)

def rotary_tables(positions, width):
    half_width = width // 2
    frequency = ROPE_BASE ** (-(jnp.arange(half_width, dtype=jnp.float32) * 2.0 / width))
    angles = positions[:, None] * frequency[None, :]
    return (jnp.cos(angles), jnp.sin(angles))

def rotate(array_in, cosine, sine_table):
    half_width = array_in.shape[-1] // 2
    first_half = array_in[..., :half_width]
    second_half = array_in[..., half_width:]
    return jnp.concatenate([first_half * cosine - second_half * sine_table, second_half * cosine + first_half * sine_table], axis=-1)

def forward(inputs, weight_qkv, weight_out, weight_gate_up, weight_down, norm_gains, head_gains, segments):
    highest = lax.Precision.HIGHEST
    weight_qkv = low(weight_qkv)
    weight_out = low(weight_out)
    weight_gate_up = low(weight_gate_up)
    weight_down = low(weight_down)
    seq_total = inputs.shape[0]
    per_group = H // KVH
    attn_in = low(inputs * inverse_rms(inputs) * norm_gains[0])
    projected = low_back(jnp.dot(attn_in, weight_qkv, precision=highest))
    projected = projected.reshape(seq_total, KVH, per_group + 2, HD)
    queries = projected[:, :, :per_group]
    keys_raw = projected[:, :, per_group]
    values_raw = projected[:, :, per_group + 1]
    positions = jnp.arange(seq_total).astype(jnp.float32)
    cosine, sine_table = rotary_tables(positions, HD)
    query_rot = rotate(queries * inverse_rms(queries) * head_gains[0], cosine[:, None, None, :], sine_table[:, None, None, :])
    key_rot = rotate(keys_raw * inverse_rms(keys_raw) * head_gains[1], cosine[:, None, :], sine_table[:, None, :])
    query_low = low_back(low(query_rot))
    key_low = low_back(low(key_rot))
    value_low = low_back(low(values_raw))
    key_span = min(512, seq_total)
    key_pos = jnp.arange(seq_total, dtype=jnp.int32)
    score_scale = HD ** (-0.5)

    def attend(block_in):
        query_block, query_pos, query_seg = block_in
        scores = jnp.einsum('bgqd,ngd->gqbn', query_block, key_low, precision=highest) * score_scale
        scores = low_back(scores)
        allowed = (key_pos[None, :] <= query_pos[:, None]) & (segments[None, :] == query_seg[:, None])
        scores = jnp.where(allowed[None, None], scores, MASKED)
        running_top = lax.optimization_barrier(jnp.max(scores, axis=-1, keepdims=True))
        expon = jnp.exp(scores - running_top)
        attn_probs = low(expon / lax.optimization_barrier(jnp.sum(expon, axis=-1, keepdims=True)))
        return jnp.einsum('gqbn,ngd->bgqd', attn_probs, value_low, precision=highest)
    block_count = seq_total // key_span
    attended = lax.map(jax.checkpoint(attend), (query_low.reshape(block_count, key_span, KVH, per_group, HD), key_pos.reshape(block_count, key_span), segments.reshape(block_count, key_span)))
    mixed = low_back(low(attended.reshape(seq_total, KVH * per_group * HD)))
    attn_out = low_back(jnp.dot(mixed, weight_out, precision=highest))
    hidden_one = inputs + attn_out
    ffn_in = low(hidden_one * inverse_rms(hidden_one) * norm_gains[1])
    gate_value = low_back(jnp.dot(ffn_in, weight_gate_up[0], precision=highest))
    up_value = low_back(jnp.dot(ffn_in, weight_gate_up[1], precision=highest))
    inner_act = low(jax.nn.silu(gate_value) * up_value)
    ffn_out = low_back(jnp.dot(inner_act, weight_down, precision=highest))
    return hidden_one + ffn_out

def lamb(weight, first_old, second_old, grad_in):
    first_new = BETA_ONE * first_old + (1.0 - BETA_ONE) * grad_in
    second_new = BETA_TWO * second_old + (1.0 - BETA_TWO) * grad_in * grad_in
    direction = first_new / (1.0 - BETA_ONE ** STEP) / (jnp.sqrt(second_new / (1.0 - BETA_TWO ** STEP)) + EPS_ADAM) + DECAY * weight
    weight_norm = jnp.sqrt(jnp.sum(weight * weight))
    step_norm = jnp.sqrt(jnp.sum(direction * direction))
    ratio = weight_norm / (step_norm + EPS_ADAM)
    return (weight - RATE * ratio * direction, first_new, second_new, weight_norm, step_norm, ratio)

def reference(tokens, segments, weight_qkv, weight_out, weight_gate_up, weight_down, norm_gains, head_gains, first_qkv, first_out, first_gate_up, first_down, first_norm, first_head, second_qkv, second_out, second_gate_up, second_down, second_norm, second_head, cotangent):
    inputs = tokens.astype(jnp.float32)

    def run(inputs_in, qkv_in, out_in, gate_up_in, down_in, norm_in, head_in):
        return forward(inputs_in, qkv_in, out_in, gate_up_in, down_in, norm_in, head_in, segments)
    outputs, pullback = jax.vjp(run, inputs, weight_qkv, weight_out, weight_gate_up, weight_down, norm_gains, head_gains)
    grads = pullback(cotangent.astype(jnp.float32))
    params = (weight_qkv, weight_out, weight_gate_up, weight_down, norm_gains, head_gains)
    firsts = (first_qkv, first_out, first_gate_up, first_down, first_norm, first_head)
    seconds = (second_qkv, second_out, second_gate_up, second_down, second_norm, second_head)
    results = [lamb(params[i], firsts[i], seconds[i], grads[i + 1]) for i in range(6)]
    trust_stats = jnp.stack([jnp.stack([item[3] for item in results]), jnp.stack([item[4] for item in results]), jnp.stack([item[5] for item in results])])
    return (outputs.astype(jnp.bfloat16), grads[0].astype(jnp.bfloat16), results[0][0], results[1][0], results[2][0], results[3][0], results[4][0], results[5][0], results[0][1], results[1][1], results[2][1], results[3][1], results[4][1], results[5][1], results[0][2], results[1][2], results[2][2], results[3][2], results[4][2], results[5][2], trust_stats)
```

```python
import functools

import jax
import jax.numpy as jnp
from jax import lax
from jax.experimental import pallas as pl
from jax.experimental.pallas import tpu as pltpu
from jax.sharding import PartitionSpec as P

H = 32
KVH = 8
HD = 64
STEP = 5
D = 2048
ROWS = 512
QPK = 4
CH = 64

EPS_NORM = 1e-05
ROPE_BASE = 1000000.0
BETA_ONE = 0.5
BETA_TWO = 0.5
EPS_ADAM = 1e-06
DECAY = 0.01
RATE = 0.5
F32 = jnp.float32
BF16 = jnp.bfloat16
OFF = -1e5
VMEM_LIMIT = 50 * 1024 * 1024


def inverse_rms(array_in):
    return lax.rsqrt(jnp.mean(array_in * array_in, axis=-1, keepdims=True) + EPS_NORM)


def adapt(weight, first_old, second_old, grad_in):
    first_new = BETA_ONE * first_old + (1.0 - BETA_ONE) * grad_in
    second_new = BETA_TWO * second_old + (1.0 - BETA_TWO) * grad_in * grad_in
    direction = (
        first_new
        / (1.0 - BETA_ONE**STEP)
        / (jnp.sqrt(second_new / (1.0 - BETA_TWO**STEP)) + EPS_ADAM)
        + DECAY * weight
    )
    return (first_new, second_new, direction)


def perm_x(k):
    return [(i, (i // 4) * 4 + (i % 4 - k) % 4) for i in range(16)]


def perm_y(k):
    return [(i, ((i // 4 - k) % 4) * 4 + i % 4) for i in range(16)]


def perm_z(k):
    return [(i, ((i // 2 - k) % 4) * 2 + i % 2) for i in range(8)]


PERM_CORE = [(i, i ^ 1) for i in range(8)]


def from_x(a, k):
    return lax.ppermute(a, "dp", perm_x(k))


def from_y(a, k):
    return lax.ppermute(a, "dp", perm_y(k))


def from_z(a, k):
    return lax.ppermute(a, "tensor", perm_z(k))


def from_core(a):
    return lax.ppermute(a, "tensor", PERM_CORE)


def gather_dp(a):
    row = jnp.stack([a] + [from_x(a, k) for k in (1, 2, 3)])
    return [row] + [from_y(row, k) for k in (1, 2, 3)]


def scatter_dp(groups):
    got = [None] + [from_y(groups[k].astype(BF16), -k) for k in (1, 2, 3)]
    row = (groups[0].astype(F32) + got[2].astype(F32)) + (got[1].astype(F32) + got[3].astype(F32))
    low = row.astype(BF16)
    back = [None] + [from_x(low[k], -k) for k in (1, 2, 3)]
    return (row[0] + back[2].astype(F32)) + (back[1].astype(F32) + back[3].astype(F32))


def scatter_tensor(near, far):
    near = near.astype(F32) + from_core(far.astype(BF16)).astype(F32)
    parts = near.reshape(4, CH, near.shape[-1])
    low = parts.astype(BF16)
    got = [None] + [from_z(low[k], -k) for k in (1, 2, 3)]
    return (parts[0] + got[2].astype(F32)) + (got[1].astype(F32) + got[3].astype(F32))


def gather_tensor(a):
    near = jnp.concatenate([a] + [from_z(a, k) for k in (1, 2, 3)], axis=0)
    return near, from_core(near)


def sum_all(a):
    for step in (from_x, from_y, from_z):
        a = (a + step(a, 2)) + (step(a, 1) + step(a, 3))
    return a + from_core(a)


def params(vmem=VMEM_LIMIT):
    return pltpu.CompilerParams(vmem_limit_bytes=vmem)


def prepare_kernel(row_ref, col_ref, tok_ref, cot_ref, gain_ref, out_ref, dy_ref):
    x = tok_ref[...].astype(F32)
    scale = inverse_rms(x)
    normed = (x * scale * gain_ref[...]).astype(BF16)
    for slot in range(16):
        at = pl.multiple_of(col_ref[slot] * 128, 128)
        out_ref[:, pl.ds(at, 128)] = normed[:, slot * 128 : (slot + 1) * 128]
    dy_ref[...] = cot_ref[...]


def prepare(row_table, slot_of, tokens, cotangent, gain):
    return pl.pallas_call(
        prepare_kernel,
        grid_spec=pltpu.PrefetchScalarGridSpec(
            num_scalar_prefetch=2,
            grid=(8,),
            in_specs=[
                pl.BlockSpec((CH, D), lambda i, r, c: (r[i], 0)),
                pl.BlockSpec((CH, D), lambda i, r, c: (r[i], 0)),
                pl.BlockSpec((1, D), lambda i, r, c: (0, 0)),
            ],
            out_specs=[
                pl.BlockSpec((CH, D), lambda i, r, c: (i, 0)),
                pl.BlockSpec((CH, D), lambda i, r, c: (i, 0)),
            ],
        ),
        out_shape=[
            jax.ShapeDtypeStruct((ROWS, D), BF16),
            jax.ShapeDtypeStruct((ROWS, D), BF16),
        ],
        compiler_params=params(),
        name="prepare",
    )(row_table, slot_of, tokens, cotangent, gain)


def lane_of(shape):
    return lax.broadcasted_iota(jnp.int32, shape, len(shape) - 1)


def head_sums(a, low_half):
    left = jnp.sum(jnp.where(low_half, a, 0.0), axis=-1, keepdims=True)
    right = jnp.sum(jnp.where(low_half, 0.0, a), axis=-1, keepdims=True)
    return jnp.where(low_half, left, right)


def turn(a, first):
    return jnp.where(first, pltpu.roll(a, 96, 1), pltpu.roll(a, 32, 1))


def project_kernel(x_ref, w0, w1, w2, w3, cos_ref, sin_ref, gain_ref, proj_ref, q_ref, kv_ref):
    acc = None
    for group, ref in enumerate((w0, w1, w2, w3)):
        for j in range(4):
            slot = group * 4 + j
            term = jnp.dot(
                x_ref[:, slot * 128 : (slot + 1) * 128],
                ref[j, :128, :],
                preferred_element_type=F32,
            )
            acc = term if acc is None else acc + term
    proj_ref[...] = acc
    lane = lane_of((x_ref.shape[0], 128))
    low_half = lane < 64
    first = (lane & 63) < 32
    cosine = cos_ref[...]
    sine = jnp.where(first, -sin_ref[...], sin_ref[...])
    for pair in range(3):
        u = acc[:, pair * 128 : (pair + 1) * 128]
        scale = lax.rsqrt(head_sums(u * u, low_half) * (1.0 / HD) + EPS_NORM)
        hat = u * scale * gain_ref[pair // 2 : pair // 2 + 1, :]
        turned = hat * cosine + turn(hat, first) * sine
        if pair < 2:
            q_ref[:, pair * 128 : (pair + 1) * 128] = (turned.astype(BF16).astype(F32) * 0.125).astype(BF16)
        else:
            kv_ref[...] = jnp.where(low_half, turned, u).astype(BF16)


def project(x, w_groups, cosine, sine, gains):
    tile = 128
    wspec = pl.BlockSpec((4, 144, 384), lambda i: (0, 0, 0))
    return pl.pallas_call(
        project_kernel,
        grid=(ROWS // tile,),
        in_specs=[pl.BlockSpec((tile, D), lambda i: (i, 0))]
        + [wspec] * 4
        + [
            pl.BlockSpec((tile, 128), lambda i: (i, 0)),
            pl.BlockSpec((tile, 128), lambda i: (i, 0)),
            pl.BlockSpec((8, 128), lambda i: (0, 0)),
        ],
        out_specs=[
            pl.BlockSpec((tile, 384), lambda i: (i, 0)),
            pl.BlockSpec((tile, 256), lambda i: (i, 0)),
            pl.BlockSpec((tile, 128), lambda i: (i, 0)),
        ],
        out_shape=[
            jax.ShapeDtypeStruct((ROWS, 384), F32),
            jax.ShapeDtypeStruct((ROWS, 256), BF16),
            jax.ShapeDtypeStruct((ROWS, 128), BF16),
        ],
        compiler_params=params(),
        name="project",
    )(x, *w_groups, cosine, sine, gains)


def lane_masks():
    low = (lane_of((1, 128)) < 64).astype(F32)
    return low.astype(BF16), (1.0 - low).astype(BF16)


def allowed_keys(is_own, kinfo_ref, qinfo_ref):
    own_seg = kinfo_ref[:, 0:1]
    first_seg = kinfo_ref[:, 1:2]
    pos = kinfo_ref[:, 2:3]
    seg = jnp.where(is_own, own_seg, first_seg)
    pos = jnp.where(is_own, pos, -1)
    return (seg == qinfo_ref[0:1, :]) & (pos <= qinfo_ref[1:2, :])


def forward_kernel(
    blk_ref, q_ref, kv0, kv1, kv2, kv3, kinfo_ref, qinfo_ref, bias_ref,
    mixed_ref, out_ref, lse_ref, kv_all, q_t, acc,
):
    for group, ref in enumerate((kv0, kv1, kv2, kv3)):
        kv_all[group * 4 : (group + 1) * 4] = ref[...]
    acc[...] = jnp.zeros_like(acc)
    turned = q_ref[...].astype(F32).T
    row = lax.broadcasted_iota(jnp.int32, (64, ROWS), 0)
    bias = jnp.where(row == 0, bias_ref[...], 0.0).astype(BF16)
    for head in range(QPK):
        q_t[head, :64, :] = turned[head * 64 : (head + 1) * 64, :].astype(BF16)
        q_t[head, 64:, :] = bias
    keep_k, keep_v = lane_masks()
    me = blk_ref[16]

    def step(slot, carry):
        block = blk_ref[slot]

        def work(masked):
            kv = kv_all[slot]
            keys = kv * keep_k + (keep_v if not masked else jnp.zeros_like(keep_v))
            vals = (kv * keep_v + keep_k).astype(F32).T.astype(BF16)
            allowed = allowed_keys(block == me, kinfo_ref, qinfo_ref) if masked else None
            for head in range(QPK):
                scores = jnp.dot(keys, q_t[head], preferred_element_type=F32)
                probs = jnp.exp(scores)
                if masked:
                    probs = jnp.where(allowed, probs, 0.0)
                acc[head] += jnp.dot(vals, probs.astype(BF16), preferred_element_type=F32)

        @pl.when((block == 0) | (block == me))
        def _():
            work(True)

        @pl.when((block > 0) & (block < me))
        def _():
            work(False)

        return carry

    lax.fori_loop(0, 16, step, 0)
    heads = []
    for head in range(QPK):
        total = acc[head, 0:1, :]
        heads.append(acc[head, 64:, :] / total)
        lse_ref[head : head + 1, :] = jnp.log(total)
    lse_ref[QPK:, :] = jnp.zeros((8 - QPK, ROWS), F32)
    out = jnp.concatenate(heads, axis=0).T
    out_ref[...] = out
    mixed_ref[...] = out.astype(BF16)


def attend(blocks, q, kv_groups, kinfo, qinfo, bias):
    vm = pl.BlockSpec(memory_space=pltpu.VMEM)
    return pl.pallas_call(
        forward_kernel,
        in_specs=[pl.BlockSpec(memory_space=pltpu.SMEM)] + [vm] * 8,
        out_specs=[vm] * 3,
        out_shape=[
            jax.ShapeDtypeStruct((ROWS, 256), BF16),
            jax.ShapeDtypeStruct((ROWS, 256), F32),
            jax.ShapeDtypeStruct((8, ROWS), F32),
        ],
        scratch_shapes=[
            pltpu.VMEM((16, ROWS, 128), BF16),
            pltpu.VMEM((QPK, 128, ROWS), BF16),
            pltpu.VMEM((QPK, 128, ROWS), F32),
        ],
        compiler_params=params(),
        name="attend",
    )(blocks, q, *kv_groups, kinfo, qinfo, bias)


def three_rows(row, value, at):
    high = value.astype(BF16).astype(F32)
    rest = value - high
    middle = rest.astype(BF16).astype(F32)
    low = rest - middle
    return (
        jnp.where(row == at, high, 0.0)
        + jnp.where(row == at + 1, middle, 0.0)
        + jnp.where(row == at + 2, low, 0.0)
    )


def backward_kernel(
    blk_ref, q_ref, do_ref, out_ref, lse_ref, kv0, kv1, kv2, kv3, kinfo_ref, qinfo_ref, bias_ref,
    dq_ref, dkv_ref, kv_all, q_t, do_t, q_pad, do_pad, dq_t,
):
    for group, ref in enumerate((kv0, kv1, kv2, kv3)):
        kv_all[group * 4 : (group + 1) * 4] = ref[...]
    dq_t[...] = jnp.zeros_like(dq_t)
    q = q_ref[...].astype(F32)
    do = do_ref[...].astype(F32)
    q_turned = q.T
    do_turned = do.T
    dots = (do * out_ref[...]).T
    row = lax.broadcasted_iota(jnp.int32, (64, ROWS), 0)
    low_half = lane_of((ROWS, 128)) < 64
    for head in range(QPK):
        at = slice(head * 64, (head + 1) * 64)
        delta = jnp.sum(dots[at, :], axis=0, keepdims=True)
        extra = three_rows(row, -lse_ref[head : head + 1, :], 0)
        extra = extra + jnp.where(row == 3, bias_ref[...], 0.0)
        q_t[head, :64, :] = q_turned[at, :].astype(BF16)
        q_t[head, 64:, :] = extra.astype(BF16)
        do_t[head, :64, :] = three_rows(row, -delta, 0).astype(BF16)
        do_t[head, 64:, :] = do_turned[at, :].astype(BF16)
        pair = slice((head // 2) * 128, (head // 2 + 1) * 128)
        q_head = q[:, pair]
        do_head = do[:, pair]
        if head % 2:
            q_head = pltpu.roll(q_head, 64, 1)
        else:
            do_head = pltpu.roll(do_head, 64, 1)
        q_pad[head] = jnp.where(low_half, q_head, 0.0).astype(BF16)
        do_pad[head] = jnp.where(low_half, 0.0, do_head).astype(BF16)
    keep_k, keep_v = lane_masks()
    me = blk_ref[16]

    def step(slot, carry):
        block = blk_ref[slot]

        def work(masked):
            kv = kv_all[slot]
            keys = kv * keep_k + keep_v
            vals = kv * keep_v + keep_k
            keys_turned = kv.astype(F32).T[:64, :].astype(BF16)
            allowed = allowed_keys(block == me, kinfo_ref, qinfo_ref) if masked else None
            total = None
            for head in range(QPK):
                q_t_head = q_t[head]
                if masked:
                    q_t_head = jnp.where(
                        lax.broadcasted_iota(jnp.int32, (128, ROWS), 0) == 67, 0.0, q_t_head.astype(F32)
                    ).astype(BF16)
                scores = jnp.dot(keys, q_t_head, preferred_element_type=F32)
                probs = jnp.exp(scores)
                if masked:
                    probs = jnp.where(allowed, probs, 0.0)
                grads = jnp.dot(vals, do_t[head], preferred_element_type=F32)
                grads = (probs * grads).astype(BF16)
                term = jnp.dot(probs.astype(BF16), do_pad[head], preferred_element_type=F32)
                term = term + jnp.dot(grads, q_pad[head], preferred_element_type=F32)
                total = term if total is None else total + term
                dq_t[head * 64 : (head + 1) * 64, :] += jnp.dot(
                    keys_turned, grads, preferred_element_type=F32
                )
            dkv_ref[slot] = total.astype(BF16)

        @pl.when((block == 0) | (block == me))
        def _():
            work(True)

        @pl.when((block > 0) & (block < me))
        def _():
            work(False)

        @pl.when(block > me)
        def _():
            dkv_ref[slot] = jnp.zeros((ROWS, 128), BF16)

        return carry

    lax.fori_loop(0, 16, step, 0)
    dq_ref[...] = (dq_t[...].T * 0.125).astype(BF16)


def attend_back(blocks, q, do, out, lse, kv_groups, kinfo, qinfo, bias):
    vm = pl.BlockSpec(memory_space=pltpu.VMEM)
    return pl.pallas_call(
        backward_kernel,
        in_specs=[pl.BlockSpec(memory_space=pltpu.SMEM)] + [vm] * 11,
        out_specs=[vm] * 2,
        out_shape=[
            jax.ShapeDtypeStruct((ROWS, 256), BF16),
            jax.ShapeDtypeStruct((16, ROWS, 128), BF16),
        ],
        scratch_shapes=[
            pltpu.VMEM((16, ROWS, 128), BF16),
            pltpu.VMEM((QPK, 128, ROWS), BF16),
            pltpu.VMEM((QPK, 128, ROWS), BF16),
            pltpu.VMEM((QPK, ROWS, 128), BF16),
            pltpu.VMEM((QPK, ROWS, 128), BF16),
            pltpu.VMEM((256, ROWS), F32),
        ],
        compiler_params=params(),
        name="attend_back",
    )(blocks, q, do, out, lse, *kv_groups, kinfo, qinfo, bias)


def heads_back_kernel(proj_ref, grad_ref, cos_ref, sin_ref, gain_ref, out_ref, sum_ref):
    lane = lane_of((proj_ref.shape[0], 128))
    low_half = lane < 64
    first = (lane & 63) < 32
    cosine = cos_ref[...]
    sine = jnp.where(first, sin_ref[...], -sin_ref[...])
    sums = []
    for pair in range(3):
        at = slice(pair * 128, (pair + 1) * 128)
        u = proj_ref[:, at]
        grad = grad_ref[:, at].astype(F32)
        scale = lax.rsqrt(head_sums(u * u, low_half) * (1.0 / HD) + EPS_NORM)
        hat = u * scale
        turned = grad * cosine + turn(grad, first) * sine
        sums.append(jnp.sum(turned * hat, axis=0, keepdims=True))
        grad_hat = turned * gain_ref[pair // 2 : pair // 2 + 1, :]
        mean = head_sums(grad_hat * hat, low_half) * (1.0 / HD)
        back = scale * (grad_hat - hat * mean)
        if pair == 2:
            back = jnp.where(low_half, back, grad)
        out_ref[:, at] = back.astype(BF16)

    @pl.when(pl.program_id(0) == 0)
    def _():
        sum_ref[...] = jnp.zeros_like(sum_ref)

    sum_ref[0:1, :] += sums[0] + sums[1]
    sum_ref[1:2, :] += sums[2]


def heads_back(proj, grad, cosine, sine, gains):
    tile = 128
    return pl.pallas_call(
        heads_back_kernel,
        grid=(ROWS // tile,),
        in_specs=[
            pl.BlockSpec((tile, 384), lambda i: (i, 0)),
            pl.BlockSpec((tile, 384), lambda i: (i, 0)),
            pl.BlockSpec((tile, 128), lambda i: (i, 0)),
            pl.BlockSpec((tile, 128), lambda i: (i, 0)),
            pl.BlockSpec((8, 128), lambda i: (0, 0)),
        ],
        out_specs=[
            pl.BlockSpec((tile, 384), lambda i: (i, 0)),
            pl.BlockSpec((8, 128), lambda i: (0, 0)),
        ],
        out_shape=[
            jax.ShapeDtypeStruct((ROWS, 384), BF16),
            jax.ShapeDtypeStruct((8, 128), F32),
        ],
        compiler_params=params(),
        name="heads_back",
    )(proj, grad, cosine, sine, gains)


def norm_back(grad_in, normed, inv_scale, gain):
    grad_hat = grad_in * gain
    return inv_scale * (grad_hat - normed * jnp.mean(grad_hat * normed, axis=-1, keepdims=True))


def dot_cols(a, b):
    return lax.dot_general(a, b, (((1,), (1,)), ((), ())), preferred_element_type=F32)


def dot_rows(a, b):
    return lax.dot_general(a, b, (((0,), (0,)), ((), ())), preferred_element_type=F32)


def dot(a, b):
    return jnp.dot(a, b, preferred_element_type=F32)


def local(
    tokens,
    segments,
    weight_qkv,
    weight_out,
    weight_gate_up,
    weight_down,
    norm_gains,
    head_gains,
    first_qkv,
    first_out,
    first_gate_up,
    first_down,
    first_norm,
    first_head,
    second_qkv,
    second_out,
    second_gate_up,
    second_down,
    second_norm,
    second_head,
    cotangent,
):
    dp = lax.axis_index("dp")
    tensor = lax.axis_index("tensor")
    y, x = dp // 4, dp % 4
    z, core = tensor // 2, tensor % 2
    slots = jnp.arange(8, dtype=jnp.int32)
    row_table = 2 * ((z + slots % 4) % 4) + (core ^ (slots // 4))
    near_z = (jnp.arange(4, dtype=jnp.int32) + y) % 4
    near_x = (jnp.arange(4, dtype=jnp.int32) + x) % 4
    blocks = (near_z[:, None] * 4 + near_x[None, :]).reshape(16)
    back_y = (jnp.arange(4, dtype=jnp.int32) - y) % 4
    back_x = (jnp.arange(4, dtype=jnp.int32) - x) % 4
    slot_of = (back_y[:, None] * 4 + back_x[None, :]).reshape(16)
    token_ids = (row_table[:, None] * CH + jnp.arange(CH, dtype=jnp.int32)[None, :]).reshape(ROWS)
    seg_rows = jnp.concatenate(
        [lax.dynamic_slice_in_dim(segments, row_table[j] * CH, CH, 0) for j in range(8)]
    )

    seg_low = jnp.stack([seg_rows // 64, seg_rows % 64]).astype(BF16).reshape(4, 256)
    seg_low = jnp.pad(seg_low, ((0, 12), (0, 128)))
    qkv_groups = gather_dp(jnp.concatenate([weight_qkv.astype(BF16), seg_low], axis=0))

    full_out = lax.all_gather(weight_out.T.astype(BF16), "dp", axis=0, tiled=True)
    full_down = lax.all_gather(weight_down.T.astype(BF16), "dp", axis=0, tiled=True)
    full_gate_up = lax.all_gather(
        jnp.concatenate([weight_gate_up[0], weight_gate_up[1]], axis=1).astype(BF16),
        "dp",
        axis=0,
        tiled=True,
    )

    attn_in, dy = prepare(row_table, slot_of, tokens, cotangent, norm_gains[0:1])
    frequency = ROPE_BASE ** (-(jnp.arange(HD // 2, dtype=F32) * 2.0 / HD))
    angles = (dp * ROWS + token_ids).astype(F32)[:, None] * jnp.tile(frequency, 4)[None, :]
    cosine, sine = jnp.cos(angles), jnp.sin(angles)
    ones = jnp.ones((1, HD), F32)
    gain_rows = jnp.concatenate(
        [
            jnp.concatenate([head_gains[0:1], head_gains[0:1]], axis=1),
            jnp.concatenate([head_gains[1:2], ones], axis=1),
            jnp.zeros((6, 128), F32),
        ]
    )
    projected, queries, local_kv = project(attn_in, qkv_groups, cosine, sine, gain_rows)
    kv_groups = gather_dp(local_kv)

    qkv_slots = jnp.stack(qkv_groups)
    first_seg = lax.dynamic_slice(
        qkv_slots, (back_y[0], back_x[0], 128, 0), (1, 1, 4, 256)
    ).astype(jnp.int32).reshape(2, ROWS)
    first_seg = first_seg[0] * 64 + first_seg[1]
    pair = jnp.concatenate([qkv_slots, qkv_slots])
    pair = lax.dynamic_slice(pair, (back_y[0], 0, 0, 0), (4, 4, 128, 384))
    pair = jnp.concatenate([pair, pair], axis=1)
    full_qkv = lax.dynamic_slice(pair, (0, back_x[0], 0, 0), (4, 4, 128, 384)).reshape(D, 384)

    kinfo = jnp.stack([seg_rows, first_seg, token_ids], axis=1)
    qinfo = jnp.concatenate([seg_rows[None], token_ids[None], jnp.zeros((6, ROWS), jnp.int32)])
    bias = jnp.where(seg_rows == segments[0], 0.0, OFF).astype(F32)[None]
    block_info = jnp.concatenate([blocks, dp[None]]).astype(jnp.int32)
    mixed, attn_f, log_total = attend(block_info, queries, kv_groups, kinfo, qinfo, bias)

    far = dot_cols(mixed[256:], full_out)
    near = dot_cols(mixed[:256], full_out)
    own_tokens = lax.dynamic_slice_in_dim(tokens, tensor * CH, CH, 0).astype(F32)
    hidden_one = own_tokens + scatter_tensor(near, far)
    scale_two = inverse_rms(hidden_one)
    normed_two = hidden_one * scale_two
    ffn_in = jnp.concatenate(gather_tensor((normed_two * norm_gains[1]).astype(BF16)), axis=0)

    gate_up = dot(ffn_in, full_gate_up)
    gate_value, up_value = gate_up[:, :1024], gate_up[:, 1024:]
    sigmoid_gate = jax.nn.sigmoid(gate_value)
    activated = gate_value * sigmoid_gate
    inner_act = (activated * up_value).astype(BF16)
    grad_inner = dot(dy, full_down)
    grad_gate = (
        grad_inner * up_value * sigmoid_gate * (1.0 + gate_value * (1.0 - sigmoid_gate))
    ).astype(BF16)
    grad_up = (grad_inner * activated).astype(BF16)
    grad_both = jnp.concatenate([grad_gate, grad_up], axis=1)
    far = dot_cols(grad_both[256:], full_gate_up)
    near = dot_cols(grad_both[:256], full_gate_up)
    grad_ffn_in = scatter_tensor(near, far)

    grad_down = lax.psum_scatter(
        dot_rows(dy, inner_act).astype(BF16), "dp", scatter_dimension=0, tiled=True
    )
    grad_gate_up = lax.psum_scatter(
        dot_rows(ffn_in, grad_both).astype(BF16), "dp", scatter_dimension=0, tiled=True
    )
    ffn_part = dot_cols(inner_act, full_down).astype(BF16)
    ffn_part = jnp.concatenate(
        [ffn_part[at * CH : (at + 1) * CH] for at in range(8)]
    )

    own_dy = dy[:CH].astype(F32)
    gain_ffn = jnp.sum(grad_ffn_in * normed_two, axis=0)
    grad_hidden = own_dy + norm_back(grad_ffn_in, normed_two, scale_two, norm_gains[1])
    grad_attn = jnp.concatenate(gather_tensor(grad_hidden.astype(BF16)), axis=0)
    grad_mixed = dot(grad_attn, full_out).astype(BF16)
    grad_out_w = lax.psum_scatter(
        dot_rows(grad_attn, mixed).astype(BF16), "dp", scatter_dimension=0, tiled=True
    )
    grad_query, grad_kv = attend_back(
        block_info, queries, grad_mixed, attn_f, log_total, kv_groups, kinfo, qinfo, bias
    )
    grad_kv = scatter_dp([grad_kv[k * 4 : (k + 1) * 4] for k in range(4)]).astype(BF16)
    grad_projected, gain_heads = heads_back(
        projected, jnp.concatenate([grad_query, grad_kv], axis=1), cosine, sine, gain_rows
    )
    grad_qkv = dot_rows(attn_in, grad_projected).astype(BF16).reshape(4, 4, 128, 384)
    grad_qkv = scatter_dp([grad_qkv[k] for k in range(4)])
    far = dot_cols(grad_projected[256:], full_qkv)
    near = dot_cols(grad_projected[:256], full_qkv)
    grad_attn_in = scatter_tensor(near, far)
    scale_one = inverse_rms(own_tokens)
    normed_one = own_tokens * scale_one
    gain_attn = jnp.sum(grad_attn_in * normed_one, axis=0)
    input_grad = (
        grad_hidden + norm_back(grad_attn_in, normed_one, scale_one, norm_gains[0])
    ).astype(BF16)

    ffn_total = scatter_tensor(ffn_part[:256], ffn_part[256:])
    block_out = (hidden_one + ffn_total).astype(BF16)

    def in_place(parts):
        rows = jnp.concatenate(parts, axis=0).reshape(2, 4, CH, D)
        twice = jnp.concatenate([rows, rows], axis=1)
        rows = lax.dynamic_slice(twice, (0, (4 - z) % 4, 0, 0), (2, 4, CH, D))
        rows = jnp.where(core == 0, rows, rows[::-1])
        return rows.transpose(1, 0, 2, 3).reshape(ROWS, D)

    block_out = in_place(gather_tensor(block_out))
    input_grad = in_place(gather_tensor(input_grad))

    matrices = (
        (weight_qkv, first_qkv, second_qkv, grad_qkv),
        (weight_out, first_out, second_out, grad_out_w.astype(F32).T),
        (
            weight_gate_up,
            first_gate_up,
            second_gate_up,
            jnp.stack([grad_gate_up[:, :1024], grad_gate_up[:, 1024:]]).astype(F32),
        ),
        (weight_down, first_down, second_down, grad_down.astype(F32).T),
    )
    adapted = [adapt(*entry) for entry in matrices]
    squares = jnp.stack(
        [jnp.sum(entry[0] * entry[0]) for entry in matrices]
        + [jnp.sum(item[2] * item[2]) for item in adapted]
    )
    sums = jnp.concatenate(
        [
            gain_attn.reshape(16, 128),
            gain_ffn.reshape(16, 128),
            gain_heads,
            jnp.pad(squares, (0, 120))[None],
            jnp.zeros((7, 128), F32),
        ]
    )
    sums = sum_all(sums)
    gain_norm_grad = sums[:32].reshape(2, D)
    gain_head_grad = jnp.stack([sums[32, :HD] + sums[32, HD:], sums[33, :HD]])
    square_sums = sums[40, :8]
    weight_norms = [jnp.sqrt(square_sums[index]) for index in range(4)]
    step_norms = [jnp.sqrt(square_sums[4 + index]) for index in range(4)]
    gain_sets = (
        (norm_gains, first_norm, second_norm, gain_norm_grad),
        (head_gains, first_head, second_head, gain_head_grad),
    )
    for entry in gain_sets:
        first_new, second_new, direction = adapt(entry[0], entry[1], entry[2], entry[3])
        adapted.append((first_new, second_new, direction))
        weight_norms.append(jnp.sqrt(jnp.sum(entry[0] * entry[0])))
        step_norms.append(jnp.sqrt(jnp.sum(direction * direction)))
    params_in = (weight_qkv, weight_out, weight_gate_up, weight_down, norm_gains, head_gains)
    ratios = [weight_norms[index] / (step_norms[index] + EPS_ADAM) for index in range(6)]
    new_params = [params_in[index] - RATE * ratios[index] * adapted[index][2] for index in range(6)]
    trust_stats = jnp.stack([jnp.stack(weight_norms), jnp.stack(step_norms), jnp.stack(ratios)])
    return (
        block_out,
        input_grad,
        *new_params,
        *[item[0] for item in adapted],
        *[item[1] for item in adapted],
        trust_stats,
    )


def solution(mesh):
    matrix_specs = (P("dp", "tensor"), P("tensor", "dp"), P(None, "dp", "tensor"), P("tensor", "dp"), P(), P())
    in_specs = (P("dp", None), P("dp"), *matrix_specs, *matrix_specs, *matrix_specs, P("dp", None))
    out_specs = (P("dp", None), P("dp", None), *matrix_specs, *matrix_specs, *matrix_specs, P())
    return jax.shard_map(local, mesh=mesh, in_specs=in_specs, out_specs=out_specs, check_vma=False)
```

```python
import functools

import jax
import jax.numpy as jnp
from jax import lax
from jax.experimental import pallas as pl
from jax.experimental.pallas import tpu as pltpu
from jax.sharding import PartitionSpec as P

H = 32
KVH = 8
HD = 64
STEP = 5
D = 2048
ROWS = 512
QPK = 4
CH = 64
FLAT = 256 + 2048 + 1024

EPS_NORM = 1e-05
ROPE_BASE = 1000000.0
BETA_ONE = 0.5
BETA_TWO = 0.5
EPS_ADAM = 1e-06
DECAY = 0.01
RATE = 0.5
F32 = jnp.float32
BF16 = jnp.bfloat16
OFF = -1e5
VMEM_LIMIT = 50 * 1024 * 1024


def inverse_rms(array_in):
    return lax.rsqrt(jnp.mean(array_in * array_in, axis=-1, keepdims=True) + EPS_NORM)


def adapt(weight, first_old, second_old, grad_in):
    first_new = BETA_ONE * first_old + (1.0 - BETA_ONE) * grad_in
    second_new = BETA_TWO * second_old + (1.0 - BETA_TWO) * grad_in * grad_in
    direction = (
        first_new
        / (1.0 - BETA_ONE**STEP)
        / (jnp.sqrt(second_new / (1.0 - BETA_TWO**STEP)) + EPS_ADAM)
        + DECAY * weight
    )
    return (first_new, second_new, direction)


def perm_x(k):
    return [(i, (i // 4) * 4 + (i % 4 - k) % 4) for i in range(16)]


def perm_y(k):
    return [(i, ((i // 4 - k) % 4) * 4 + i % 4) for i in range(16)]


def perm_z(k):
    return [(i, ((i // 2 - k) % 4) * 2 + i % 2) for i in range(8)]


PERM_CORE = [(i, i ^ 1) for i in range(8)]


def from_x(a, k):
    return lax.ppermute(a, "dp", perm_x(k))


def from_y(a, k):
    return lax.ppermute(a, "dp", perm_y(k))


def from_z(a, k):
    return lax.ppermute(a, "tensor", perm_z(k))


def from_core(a):
    return lax.ppermute(a, "tensor", PERM_CORE)


def gather_both(u, v):
    row = jnp.stack([u] + [from_x(u, k) for k in (1, 2, 3)])
    column = jnp.stack([v] + [from_y(v, k) for k in (1, 2, 3)])
    return [row] + [from_y(row, k) for k in (1, 2, 3)], [column] + [from_x(column, k) for k in (1, 2, 3)]


def sum_four(own, got):
    return (own.astype(F32) + got[2].astype(F32)) + (got[1].astype(F32) + got[3].astype(F32))


def send(parts, step):
    return {k: step(parts[k], -k) for k in (2, 1, 3)}


def scatter_rest(own, got, step):
    line = sum_four(own, got)
    low = line.astype(BF16)
    return sum_four(line[0], {k: step(low[k], -k) for k in (2, 1, 3)})


def beside(arrays, work):
    return lax.optimization_barrier((arrays, work))


def scatter_tensor(near, far, work=None):
    near = near.astype(F32) + from_core(far.astype(BF16)).astype(F32)
    parts = near.reshape(4, CH, near.shape[-1])
    low = parts.astype(BF16)
    got = {k: from_z(low[k], -k) for k in (2, 1, 3)}
    if work is None:
        return sum_four(parts[0], got)
    got, work = beside(got, work)
    return sum_four(parts[0], got), work


def gather_tensor(a, work=None):
    got = {k: from_z(a, k) for k in (2, 1, 3)}
    if work is not None:
        got, work = beside(got, work)
    near = jnp.concatenate([a, got[1], got[2], got[3]], axis=0)
    halves = (near, from_core(near))
    return halves if work is None else (halves, work)


def sum_all(a):
    for step in (from_x, from_y, from_z):
        a = (a + step(a, 2)) + (step(a, 1) + step(a, 3))
    return a + from_core(a)


def params(vmem=VMEM_LIMIT):
    return pltpu.CompilerParams(vmem_limit_bytes=vmem)


def whole_specs(arrays):
    return [pl.BlockSpec(a.shape, lambda i, n=len(a.shape): (0,) * n) for a in arrays]


def prepare_kernel(row_ref, tok_ref, cot_ref, gain_ref, in_ref, across_ref, x_ref, dy_ref):
    low = tok_ref[...]
    x = low.astype(F32)
    normed = x * inverse_rms(x) * gain_ref[...]
    in_ref[...] = normed.astype(BF16)
    x_ref[...] = low
    dy_ref[...] = cot_ref[...]
    step = pl.program_id(0)
    across = normed.T.astype(BF16)

    @pl.when(step % 2 == 0)
    def _():
        across_ref[:, :CH] = across

    @pl.when(step % 2 == 1)
    def _():
        across_ref[:, CH:] = across


def prepare(row_table, tokens, cotangent, gain):
    pick = pl.BlockSpec((CH, D), lambda i, r: (r[i], 0))
    put = pl.BlockSpec((CH, D), lambda i, r: (i, 0))
    return pl.pallas_call(
        prepare_kernel,
        grid_spec=pltpu.PrefetchScalarGridSpec(
            num_scalar_prefetch=1,
            grid=(8,),
            in_specs=[pick, pick, pl.BlockSpec((1, D), lambda i, r: (0, 0))],
            out_specs=[put, pl.BlockSpec((D, 128), lambda i, r: (0, i // 2)), put, put],
        ),
        out_shape=[
            jax.ShapeDtypeStruct((ROWS, D), BF16),
            jax.ShapeDtypeStruct((D, ROWS), BF16),
            jax.ShapeDtypeStruct((ROWS, D), BF16),
            jax.ShapeDtypeStruct((ROWS, D), BF16),
        ],
        compiler_params=params(),
        name="prepare",
    )(row_table, tokens, cotangent, gain)


def lane_of(shape):
    return lax.broadcasted_iota(jnp.int32, shape, len(shape) - 1)


def head_sums(a, low_half):
    left = jnp.sum(jnp.where(low_half, a, 0.0), axis=-1, keepdims=True)
    right = jnp.sum(jnp.where(low_half, 0.0, a), axis=-1, keepdims=True)
    return jnp.where(low_half, left, right)


def turn(a, first):
    return jnp.where(first, pltpu.roll(a, 96, 1), pltpu.roll(a, 32, 1))


def vmem_specs(count):
    return [pl.BlockSpec(memory_space=pltpu.VMEM)] * count


def shape(dims, kind):
    return jax.ShapeDtypeStruct(dims, kind)


def column_squares(a):
    total = None
    for at in range(0, a.shape[-1], 128):
        part = a[:, at : at + 128]
        part = jnp.sum(part * part, axis=0, keepdims=True)
        total = part if total is None else total + part
    return total


def eight_rows(rows):
    row = lax.broadcasted_iota(jnp.int32, (8, 128), 0)
    out = jnp.zeros((8, 128), F32)
    for index, value in enumerate(rows):
        if value is not None:
            out = jnp.where(row == index, value, out)
    return out


def pack_kernel(qkv_ref, out_w_ref, gate_up_ref, down_ref, flat_ref, squares_ref):
    flat_ref[:, :256] = out_w_ref[...].T.astype(BF16)
    flat_ref[:, 256:1280] = gate_up_ref[0].astype(BF16)
    flat_ref[:, 1280:2304] = gate_up_ref[1].astype(BF16)
    flat_ref[:, 2304:] = down_ref[...].T.astype(BF16)
    squares_ref[...] = eight_rows(
        [
            column_squares(qkv_ref[...]),
            column_squares(out_w_ref[...]),
            column_squares(gate_up_ref[0]) + column_squares(gate_up_ref[1]),
            column_squares(down_ref[...]),
        ]
    )


def pack(weight_qkv, weight_out, weight_gate_up, weight_down):
    given = (weight_qkv, weight_out, weight_gate_up, weight_down)
    outs = [shape((128, FLAT), BF16), shape((8, 128), F32)]
    return pl.pallas_call(
        pack_kernel,
        grid=(1,),
        in_specs=whole_specs(given),
        out_specs=whole_specs(outs),
        out_shape=outs,
        compiler_params=params(),
        name="pack",
    )(*given)


def project_kernel(
    blk_ref, x_ref, u0, u1, u2, u3, v0, v1, v2, v3, cos_ref, sin_ref, gain_ref, bias_ref,
    proj_ref, q_ref, q_ext_ref, kv_ref, w_ref,
):
    @pl.when(pl.program_id(0) == 0)
    def _():
        for at_y in range(4):
            for at_x in range(4):
                start = pl.multiple_of(blk_ref[at_y * 4 + at_x] * 128, 128)
                w_ref[pl.ds(start, 64), :] = (u0, u1, u2, u3)[at_y][at_x, :64, :]
                w_ref[pl.ds(start + 64, 64), :] = (v0, v1, v2, v3)[at_x][at_y]

    acc = jnp.dot(x_ref[...], w_ref[...], preferred_element_type=F32)
    proj_ref[...] = acc
    rows = x_ref.shape[0]
    lane = lane_of((rows, 128))
    low_half = lane < 64
    first = (lane & 63) < 32
    cosine = cos_ref[...]
    sine = jnp.where(first, -sin_ref[...], sin_ref[...])
    bias = jnp.where(lax.broadcasted_iota(jnp.int32, (64, rows), 0) == 0, bias_ref[...], 0.0)
    for pair in range(3):
        u = acc[:, pair * 128 : (pair + 1) * 128]
        scale = lax.rsqrt(head_sums(u * u, low_half) * (1.0 / HD) + EPS_NORM)
        hat = u * scale * gain_ref[pair // 2 : pair // 2 + 1, :]
        turned = hat * cosine + turn(hat, first) * sine
        if pair < 2:
            scaled = turned.astype(BF16).astype(F32) * 0.125
            q_ref[:, pair * 128 : (pair + 1) * 128] = scaled.astype(BF16)
            across = scaled.T
            for half in range(2):
                q_ext_ref[2 * pair + half, :64, :] = across[half * 64 : (half + 1) * 64, :].astype(BF16)
                q_ext_ref[2 * pair + half, 64:, :] = bias.astype(BF16)
        else:
            kv_ref[...] = jnp.where(low_half, turned, u).astype(BF16)


def project(blocks, x, w_first, w_second, cosine, sine, gains, bias):
    tile = 128
    whole = lambda dims: pl.BlockSpec(dims, lambda i, b: (0,) * len(dims))
    row = lambda width: pl.BlockSpec((tile, width), lambda i, b: (i, 0))
    return pl.pallas_call(
        project_kernel,
        grid_spec=pltpu.PrefetchScalarGridSpec(
            num_scalar_prefetch=1,
            grid=(ROWS // tile,),
            in_specs=[row(D)]
            + [whole((4, 80, 384))] * 4
            + [whole((4, 64, 384))] * 4
            + [row(128), row(128), whole((8, 128)), pl.BlockSpec((1, tile), lambda i, b: (0, i))],
            out_specs=[
                row(384),
                row(256),
                pl.BlockSpec((QPK, 128, tile), lambda i, b: (0, 0, i)),
                row(128),
                whole((D, 384)),
            ],
        ),
        out_shape=[
            shape((ROWS, 384), F32),
            shape((ROWS, 256), BF16),
            shape((QPK, 128, ROWS), BF16),
            shape((ROWS, 128), BF16),
            shape((D, 384), BF16),
        ],
        compiler_params=params(),
        name="project",
    )(blocks, x, *w_first, *w_second, cosine, sine, gains, bias)


def lane_masks():
    low = (lane_of((1, 128)) < 64).astype(F32)
    return low.astype(BF16), (1.0 - low).astype(BF16)


def allowed_keys(is_own, half, kinfo_ref, qinfo_ref):
    info = kinfo_ref[pl.ds(pl.multiple_of(half * 256, 256), 256), :]
    seg = jnp.where(is_own, info[:, 0:1], info[:, 1:2])
    pos = jnp.where(is_own, info[:, 2:3], -1)
    return (seg == qinfo_ref[0:1, :]) & (pos <= qinfo_ref[1:2, :])


def each_block(blk_ref, work, skipped=None):
    me = blk_ref[8]

    def step(slot, carry):
        block = blk_ref[slot]

        @pl.when((block == 0) | (block == me))
        def _():
            work(slot, True, block == me)

        @pl.when((block > 0) & (block < me))
        def _():
            work(slot, False, None)

        if skipped is not None:

            @pl.when(block > me)
            def _():
                skipped(slot)

        return carry

    lax.fori_loop(0, 8, step, 0)


def forward_kernel(first, last, blk_ref, q_ref, u_ref, v_ref, kinfo_ref, qinfo_ref, *refs):
    acc, kv_all = refs[-2:]
    kv_all[:4] = u_ref[...]
    kv_all[4:] = v_ref[...]
    if first:
        acc[...] = jnp.zeros_like(acc)
    else:
        acc[...] = refs[0][...]
    keep_k, keep_v = lane_masks()

    def work(slot, masked, is_own):
        kv = kv_all[slot]
        keys = kv * keep_k + (keep_v if not masked else jnp.zeros_like(keep_v))
        vals = (kv * keep_v + keep_k).astype(F32).T.astype(BF16)
        allowed = allowed_keys(is_own, slot // 4, kinfo_ref, qinfo_ref) if masked else None
        for head in range(QPK):
            scores = jnp.dot(keys, q_ref[head], preferred_element_type=F32)
            probs = jnp.exp(scores)
            if masked:
                probs = jnp.where(allowed, probs, 0.0)
            acc[head] += jnp.dot(vals, probs.astype(BF16), preferred_element_type=F32)

    each_block(blk_ref, work)
    if last:
        mixed_ref, out_ref, lse_ref = refs[1:4]
        heads = []
        for head in range(QPK):
            total = acc[head, 0:1, :]
            heads.append(acc[head, 64:, :] / total)
            lse_ref[head : head + 1, :] = jnp.log(total)
        lse_ref[QPK:, :] = jnp.zeros((8 - QPK, ROWS), F32)
        out = jnp.concatenate(heads, axis=0).T
        out_ref[...] = out
        mixed_ref[...] = out.astype(BF16)


def attend(first, last, blocks, q, u, v, kinfo, qinfo, acc=None):
    state = shape((QPK, 128, ROWS), F32)
    ends = [shape((ROWS, 256), BF16), shape((ROWS, 256), F32), shape((8, ROWS), F32)]
    given = [q, u, v, kinfo, qinfo] + ([] if first else [acc])
    return pl.pallas_call(
        functools.partial(forward_kernel, first, last),
        in_specs=[pl.BlockSpec(memory_space=pltpu.SMEM)] + vmem_specs(len(given)),
        out_specs=vmem_specs(3) if last else vmem_specs(1)[0],
        out_shape=ends if last else state,
        scratch_shapes=([pltpu.VMEM((QPK, 128, ROWS), F32)] if last else [])
        + [pltpu.VMEM((8, 256, 128), BF16)],
        compiler_params=params(),
        name="attend",
    )(blocks, *given)


def three_rows(row, value, at):
    high = value.astype(BF16).astype(F32)
    rest = value - high
    middle = rest.astype(BF16).astype(F32)
    low = rest - middle
    return (
        jnp.where(row == at, high, 0.0)
        + jnp.where(row == at + 1, middle, 0.0)
        + jnp.where(row == at + 2, low, 0.0)
    )


def ready_kernel(near_ref, far_ref, w_ref, q_ref, q_ext_ref, out_ref, lse_ref, q_t, do_t, q_pad, do_pad):
    do = jnp.concatenate(
        [
            jnp.dot(near_ref[...], w_ref[...], preferred_element_type=F32),
            jnp.dot(far_ref[...], w_ref[...], preferred_element_type=F32),
        ],
        axis=0,
    )
    do = do.astype(BF16).astype(F32)
    q = q_ref[...].astype(F32)
    do_turned = do.T
    dots = (do * out_ref[...]).T
    row = lax.broadcasted_iota(jnp.int32, (64, ROWS), 0)
    low_half = lane_of((ROWS, 128)) < 64
    for head in range(QPK):
        at = slice(head * 64, (head + 1) * 64)
        delta = jnp.sum(dots[at, :], axis=0, keepdims=True)
        extra = three_rows(row, -lse_ref[head : head + 1, :], 0)
        extra = extra + jnp.where(row == 3, q_ext_ref[head, 64:65, :].astype(F32), 0.0)
        q_t[head, :64, :] = q_ext_ref[head, :64, :]
        q_t[head, 64:, :] = extra.astype(BF16)
        do_t[head, :64, :] = three_rows(row, -delta, 0).astype(BF16)
        do_t[head, 64:, :] = do_turned[at, :].astype(BF16)
        pair = slice((head // 2) * 128, (head // 2 + 1) * 128)
        q_head = q[:, pair]
        do_head = do[:, pair]
        if head % 2:
            q_head = pltpu.roll(q_head, 64, 1)
        else:
            do_head = pltpu.roll(do_head, 64, 1)
        q_pad[head] = jnp.where(low_half, q_head, 0.0).astype(BF16)
        do_pad[head] = jnp.where(low_half, 0.0, do_head).astype(BF16)


def ready(near, far, flat, q, q_ext, out, lse):
    whole = lambda dims: pl.BlockSpec(dims, lambda i: (0,) * len(dims))
    return pl.pallas_call(
        ready_kernel,
        grid=(1,),
        in_specs=[
            whole((256, D)),
            whole((256, D)),
            whole((D, 256)),
            whole((ROWS, 256)),
            whole((QPK, 128, ROWS)),
            whole((ROWS, 256)),
            whole((8, ROWS)),
        ],
        out_specs=[whole((QPK, 128, ROWS))] * 2 + [whole((QPK, ROWS, 128))] * 2,
        out_shape=[shape((QPK, 128, ROWS), BF16)] * 2 + [shape((QPK, ROWS, 128), BF16)] * 2,
        compiler_params=params(),
        name="ready",
    )(near, far, flat, q, q_ext, out, lse)


def backward_kernel(
    first, last, blk_ref, q_t, do_t, q_pad, do_pad, u_ref, v_ref, kinfo_ref, qinfo_ref, *refs
):
    du_ref, dv_ref, dq_t, kv_all = refs[-4:]
    kv_all[:4] = u_ref[...]
    kv_all[4:] = v_ref[...]
    if first:
        dq_t[...] = jnp.zeros_like(dq_t)
    else:
        dq_t[...] = refs[0][...]
    keep_k, keep_v = lane_masks()

    def work(slot, masked, is_own):
        kv = kv_all[slot]
        keys = kv * keep_k + keep_v
        vals = kv * keep_v + keep_k
        keys_turned = kv.astype(F32).T[:64, :].astype(BF16)
        allowed = allowed_keys(is_own, slot // 4, kinfo_ref, qinfo_ref) if masked else None
        total = None
        for head in range(QPK):
            q_t_head = q_t[head]
            if masked:
                row = lax.broadcasted_iota(jnp.int32, (128, ROWS), 0)
                q_t_head = jnp.where(row == 67, 0.0, q_t_head.astype(F32)).astype(BF16)
            scores = jnp.dot(keys, q_t_head, preferred_element_type=F32)
            probs = jnp.exp(scores)
            if masked:
                probs = jnp.where(allowed, probs, 0.0)
            grads = jnp.dot(vals, do_t[head], preferred_element_type=F32)
            grads = (probs * grads).astype(BF16)
            term = jnp.dot(probs.astype(BF16), do_pad[head], preferred_element_type=F32)
            term = term + jnp.dot(grads, q_pad[head], preferred_element_type=F32)
            total = term if total is None else total + term
            dq_t[head * 64 : (head + 1) * 64, :] += jnp.dot(
                keys_turned, grads, preferred_element_type=F32
            )
        keep(slot, total.astype(BF16))

    def keep(slot, value):
        @pl.when(slot < 4)
        def _():
            du_ref[slot] = value

        @pl.when(slot >= 4)
        def _():
            dv_ref[slot - 4] = value

    def skipped(slot):
        keep(slot, jnp.zeros((256, 128), BF16))

    each_block(blk_ref, work, skipped)
    if last:
        refs[1][...] = (dq_t[...].T * 0.125).astype(BF16)


def attend_back(first, last, blocks, operands, u, v, kinfo, qinfo, dq=None):
    given = [*operands, u, v, kinfo, qinfo] + ([] if first else [dq])
    dkv = shape((4, 256, 128), BF16)
    return pl.pallas_call(
        functools.partial(backward_kernel, first, last),
        in_specs=[pl.BlockSpec(memory_space=pltpu.SMEM)] + vmem_specs(len(given)),
        out_specs=vmem_specs(3),
        out_shape=[shape((ROWS, 256), BF16), dkv, dkv] if last else [dkv, dkv, shape((256, ROWS), F32)],
        scratch_shapes=([pltpu.VMEM((256, ROWS), F32)] if last else [])
        + [pltpu.VMEM((8, 256, 128), BF16)],
        compiler_params=params(),
        name="attend_back",
    )(blocks, *given)


def heads_back_kernel(pairs, proj_ref, grad_ref, cos_ref, sin_ref, gain_ref, out_ref, sum_ref):
    lane = lane_of((proj_ref.shape[0], 128))
    low_half = lane < 64
    first = (lane & 63) < 32
    cosine = cos_ref[...]
    sine = jnp.where(first, sin_ref[...], -sin_ref[...])
    sums = None
    for index, pair in enumerate(pairs):
        at = slice(index * 128, (index + 1) * 128)
        u = proj_ref[:, pair * 128 : (pair + 1) * 128]
        grad = grad_ref[:, at].astype(F32)
        scale = lax.rsqrt(head_sums(u * u, low_half) * (1.0 / HD) + EPS_NORM)
        hat = u * scale
        turned = grad * cosine + turn(grad, first) * sine
        part = jnp.sum(turned * hat, axis=0, keepdims=True)
        sums = part if sums is None else sums + part
        grad_hat = turned * gain_ref[pair // 2 : pair // 2 + 1, :]
        mean = head_sums(grad_hat * hat, low_half) * (1.0 / HD)
        back = scale * (grad_hat - hat * mean)
        if pair == 2:
            back = jnp.where(low_half, back, grad)
        out_ref[:, at] = back.astype(BF16)

    @pl.when(pl.program_id(0) == 0)
    def _():
        sum_ref[...] = jnp.zeros_like(sum_ref)

    sum_ref[0:1, :] += sums


def heads_back(pairs, proj, grad, cosine, sine, gains):
    tile = 128
    wide = 128 * len(pairs)
    return pl.pallas_call(
        functools.partial(heads_back_kernel, pairs),
        grid=(ROWS // tile,),
        in_specs=[
            pl.BlockSpec((tile, 384), lambda i: (i, 0)),
            pl.BlockSpec((tile, wide), lambda i: (i, 0)),
            pl.BlockSpec((tile, 128), lambda i: (i, 0)),
            pl.BlockSpec((tile, 128), lambda i: (i, 0)),
            pl.BlockSpec((8, 128), lambda i: (0, 0)),
        ],
        out_specs=[
            pl.BlockSpec((tile, wide), lambda i: (i, 0)),
            pl.BlockSpec((8, 128), lambda i: (0, 0)),
        ],
        out_shape=[shape((ROWS, wide), BF16), shape((8, 128), F32)],
        compiler_params=params(),
        name="heads_back",
    )(proj, grad, cosine, sine, gains)


def out_kernel(mixed_ref, w_ref, out_ref):
    out_ref[...] = dot_cols(mixed_ref[...], w_ref[...]).astype(out_ref.dtype)


def out_project(half, mixed, flat, kind):
    return pl.pallas_call(
        out_kernel,
        grid=(1,),
        in_specs=[
            pl.BlockSpec((256, 256), lambda i: (half, 0)),
            pl.BlockSpec((D, 256), lambda i: (0, 0)),
        ],
        out_specs=pl.BlockSpec((256, D), lambda i: (0, 0)),
        out_shape=shape((256, D), kind),
        compiler_params=params(),
        name="out_project",
    )(mixed, flat)


def ffn_kernel(near_ref, far_ref, grad_ref, gate_w, up_w, act_ref, gate_ref, up_ref, near_out, far_out, x_all, acc):
    step = pl.program_id(0)

    @pl.when(step == 0)
    def _():
        x_all[:256] = near_ref[...]
        x_all[256:] = far_ref[...]
        acc[...] = jnp.zeros_like(acc)

    x = x_all[...]
    gate = jnp.dot(x, gate_w[...], preferred_element_type=F32)
    up = jnp.dot(x, up_w[...], preferred_element_type=F32)
    inner = grad_ref[...]
    sigmoid = jax.nn.sigmoid(gate)
    activated = gate * sigmoid
    act_ref[...] = (activated * up).astype(BF16)
    grad_gate = (inner * up * sigmoid * (1.0 + gate * (1.0 - sigmoid))).astype(BF16)
    grad_up = (inner * activated).astype(BF16)
    gate_ref[...] = grad_gate
    up_ref[...] = grad_up
    acc[...] += dot_cols(grad_gate, gate_w[...]) + dot_cols(grad_up, up_w[...])

    @pl.when(step == pl.num_programs(0) - 1)
    def _():
        near_out[...] = acc[:256]
        far_out[...] = acc[256:].astype(BF16)


def feed_forward(near, far, grad_inner, flat):
    whole = lambda dims: pl.BlockSpec(dims, lambda j: (0, 0))
    tile = pl.BlockSpec((ROWS, 256), lambda j: (0, j))
    return pl.pallas_call(
        ffn_kernel,
        grid=(4,),
        in_specs=[
            whole((256, D)),
            whole((256, D)),
            tile,
            pl.BlockSpec((D, 256), lambda j: (0, 1 + j)),
            pl.BlockSpec((D, 256), lambda j: (0, 5 + j)),
        ],
        out_specs=[tile, tile, tile, whole((256, D)), whole((256, D))],
        out_shape=[shape((ROWS, 1024), BF16)] * 3 + [shape((256, D), F32), shape((256, D), BF16)],
        scratch_shapes=[pltpu.VMEM((ROWS, D), BF16), pltpu.VMEM((ROWS, D), F32)],
        compiler_params=params(),
        name="feed_forward",
    )(near, far, grad_inner, flat, flat)


def inner_grad_kernel(dy_ref, w_ref, out_ref):
    out_ref[...] = jnp.dot(dy_ref[...], w_ref[...], preferred_element_type=F32)


def inner_grad(dy, flat):
    return pl.pallas_call(
        inner_grad_kernel,
        grid=(4,),
        in_specs=[
            pl.BlockSpec((ROWS, D), lambda j: (0, 0)),
            pl.BlockSpec((D, 256), lambda j: (0, 9 + j)),
        ],
        out_specs=pl.BlockSpec((ROWS, 256), lambda j: (0, j)),
        out_shape=shape((ROWS, 1024), F32),
        compiler_params=params(),
        name="inner_grad",
    )(dy, flat)


def ffn_out_kernel(row_ref, act_ref, w_ref, out_ref, acc):
    step = pl.program_id(0)
    term = dot_cols(act_ref[...], w_ref[...])

    @pl.when(step == 0)
    def _():
        acc[...] = term

    @pl.when(step > 0)
    def _():
        acc[...] += term

    @pl.when(step == pl.num_programs(0) - 1)
    def _():
        for j in range(8):
            at = pl.multiple_of(row_ref[j] * CH, CH)
            out_ref[pl.ds(at, CH), :] = acc[j * CH : (j + 1) * CH].astype(BF16)


def ffn_out(row_table, act, flat):
    return pl.pallas_call(
        ffn_out_kernel,
        grid_spec=pltpu.PrefetchScalarGridSpec(
            num_scalar_prefetch=1,
            grid=(4,),
            in_specs=[
                pl.BlockSpec((ROWS, 256), lambda j, r: (0, j)),
                pl.BlockSpec((D, 256), lambda j, r: (0, 9 + j)),
            ],
            out_specs=pl.BlockSpec((ROWS, D), lambda j, r: (0, 0)),
            scratch_shapes=[pltpu.VMEM((ROWS, D), F32)],
        ),
        out_shape=shape((ROWS, D), BF16),
        compiler_params=params(),
        name="ffn_out",
    )(row_table, act, flat)


def qkv_grad_kernel(blk_ref, across_ref, grad_ref, out_ref):
    grad = grad_ref[...]
    for slot in range(16):
        rows = across_ref[pl.ds(pl.multiple_of(blk_ref[slot] * 128, 128), 128), :]
        out_ref[slot // 4, slot % 4] = jnp.dot(rows, grad, preferred_element_type=F32).astype(BF16)


def qkv_grad(blocks, across, grad):
    wide = grad.shape[1]
    return pl.pallas_call(
        qkv_grad_kernel,
        in_specs=[pl.BlockSpec(memory_space=pltpu.SMEM)] + vmem_specs(2),
        out_specs=vmem_specs(1)[0],
        out_shape=shape((4, 4, 128, wide), BF16),
        compiler_params=params(),
        name="qkv_grad",
    )(blocks, across, grad)


def attn_back_kernel(grad_ref, w_ref, x_ref, near_ref, far_ref, gain_ref):
    step = pl.program_id(0)
    part = dot_cols(grad_ref[...], w_ref[...])
    x = x_ref[...].astype(F32)
    sums = jnp.sum(part * (x * inverse_rms(x)), axis=0, keepdims=True)

    @pl.when(step == 0)
    def _():
        gain_ref[...] = sums

    @pl.when(step > 0)
    def _():
        gain_ref[...] += sums

    @pl.when(step < 2)
    def _():
        far_ref[...] = part.astype(BF16)

    @pl.when(step >= 2)
    def _():
        near_ref[...] = part


def attn_back(grad, w, x):
    tile = 128
    turn_rows = lambda i: ((i + 2) % 4, 0)
    return pl.pallas_call(
        attn_back_kernel,
        grid=(4,),
        in_specs=[
            pl.BlockSpec((tile, 384), turn_rows),
            pl.BlockSpec((D, 384), lambda i: (0, 0)),
            pl.BlockSpec((tile, D), turn_rows),
        ],
        out_specs=[
            pl.BlockSpec((tile, D), lambda i: (jnp.maximum(i - 2, 0), 0)),
            pl.BlockSpec((tile, D), lambda i: (jnp.minimum(i, 1), 0)),
            pl.BlockSpec((1, D), lambda i: (0, 0)),
        ],
        out_shape=[shape((256, D), F32), shape((256, D), BF16), shape((1, D), F32)],
        compiler_params=params(),
        name="attn_back",
    )(grad, w, x)


def weight_grad_kernel(parts, wide, *refs):
    lhs, rhs = refs[:parts], refs[parts : parts + len(wide)]
    out_ref, turned = refs[-2:]
    step = pl.program_id(0)

    @pl.when(step == 0)
    def _():
        rows = ROWS // parts
        for index, ref in enumerate(lhs):
            turned[:, index * rows : (index + 1) * rows] = ref[...].astype(F32).T.astype(BF16)

    start = 0
    for ref, count in zip(rhs, wide, strict=True):

        @pl.when((step >= start) & (step < start + count))
        def _(ref=ref):
            out_ref[...] = jnp.dot(turned[...], ref[...], preferred_element_type=F32).astype(BF16)

        start += count


def weight_grad(lhs, rhs, at, flat=None):
    wide = [a.shape[1] // 256 for a in rhs]
    starts = [sum(wide[:i]) for i in range(len(wide))]
    given = [*lhs, *rhs] + ([] if flat is None else [flat])
    specs = [pl.BlockSpec(a.shape, lambda i: (0, 0)) for a in lhs]
    for start, count in zip(starts, wide, strict=True):
        specs.append(
            pl.BlockSpec(
                (ROWS, 256),
                lambda i, start=start, count=count: (0, jnp.clip(i - start, 0, count - 1)),
            )
        )
    if flat is not None:
        specs.append(pl.BlockSpec(memory_space=pl.ANY))
    return pl.pallas_call(
        functools.partial(weight_grad_kernel, len(lhs), wide),
        grid=(sum(wide),),
        in_specs=specs,
        out_specs=pl.BlockSpec((D, 256), lambda i: (0, at + i)),
        out_shape=shape((D, FLAT), BF16),
        scratch_shapes=[pltpu.VMEM((D, ROWS), BF16)],
        input_output_aliases={} if flat is None else {len(given) - 1: 0},
        compiler_params=params(),
        name="weight_grad",
    )(*given)


def place_kernel(row_ref, near_ref, far_ref, out_ref):
    out_ref[...] = jnp.where(pl.program_id(0) < 4, near_ref[...], far_ref[...])


def place(row_table, halves):
    return pl.pallas_call(
        place_kernel,
        grid_spec=pltpu.PrefetchScalarGridSpec(
            num_scalar_prefetch=1,
            grid=(8,),
            in_specs=[
                pl.BlockSpec((CH, D), lambda i, r: (jnp.minimum(i, 3), 0)),
                pl.BlockSpec((CH, D), lambda i, r: (jnp.maximum(i - 4, 0), 0)),
            ],
            out_specs=pl.BlockSpec((CH, D), lambda i, r: (r[i], 0)),
        ),
        out_shape=shape((ROWS, D), BF16),
        compiler_params=params(),
        name="place",
    )(row_table, *halves)


def step_kernel(wide, *refs):
    grad_ref = refs[0]
    count = len(wide)
    squares = []
    at = 0
    for index, (columns, turned, row) in enumerate(wide):
        weight, first, second = refs[1 + 3 * index : 4 + 3 * index]
        first_out, second_out, direction_out = refs[1 + 3 * count + 3 * index : 4 + 3 * count + 3 * index]
        total = None
        for part in range(2 if len(weight.shape) == 3 else 1):
            grad = grad_ref[:, at : at + columns].astype(F32)
            at += columns
            if turned:
                grad = grad.T
            pick = (part,) if len(weight.shape) == 3 else (slice(None),)
            first_new, second_new, direction = adapt(weight[pick], first[pick], second[pick], grad)
            first_out[pick] = first_new
            second_out[pick] = second_new
            direction_out[pick] = direction
            sums = column_squares(direction)
            total = sums if total is None else total + sums
        squares.append((row, total))
    refs[-1][...] = eight_rows([dict(squares).get(row) for row in range(8)])


def take_step(grad, matrices, wide):
    given = [a for matrix in matrices for a in matrix]
    outs = [shape(matrix[0].shape, F32) for matrix in matrices for _ in range(3)]
    out = pl.pallas_call(
        functools.partial(step_kernel, wide),
        grid=(1,),
        in_specs=whole_specs([grad, *given]),
        out_specs=whole_specs(outs + [shape((8, 128), F32)]),
        out_shape=outs + [shape((8, 128), F32)],
        compiler_params=params(),
        name="take_step",
    )(grad, *given)
    return [out[3 * i : 3 * i + 3] for i in range(len(matrices))], out[-1]


def finish_kernel(*refs):
    sums = refs[0]
    weights, directions = refs[1:5], refs[5:9]
    gains = (refs[9:12], refs[12:15])
    outs = refs[15:19]
    gain_outs = (refs[19:22], refs[22:25])
    stats_ref = refs[25]
    row = lax.broadcasted_iota(jnp.int32, (3, 6), 0)
    column = lax.broadcasted_iota(jnp.int32, (3, 6), 1)
    stats = jnp.zeros((3, 6), F32)

    def total(a):
        return jnp.sum(jnp.sum(a, axis=1, keepdims=True), axis=0, keepdims=True)

    def keep(stats, index, weight_norm, step_norm):
        ratio = weight_norm / (step_norm + EPS_ADAM)
        values = jnp.where(row == 0, weight_norm, jnp.where(row == 1, step_norm, ratio))
        return jnp.where(column == index, values, stats), ratio

    for index in range(4):
        weight_norm = jnp.sqrt(total(sums[2:3, 256 + index * 128 : 384 + index * 128]))
        step_norm = jnp.sqrt(total(sums[2:3, 768 + index * 128 : 896 + index * 128]))
        stats, ratio = keep(stats, index, weight_norm, step_norm)
        weight, direction, out = weights[index], directions[index], outs[index]
        if len(weight.shape) == 3:
            for part in range(2):
                out[part] = weight[part] - RATE * ratio * direction[part]
        else:
            out[...] = weight[...] - RATE * ratio * direction[...]
    query_gain = sums[2:3, 0:64] + sums[2:3, 64:128]
    head_grad = jnp.concatenate([query_gain, sums[2:3, 128:192]], axis=0)
    for index, grad in enumerate((sums[0:2, :], head_grad)):
        weight, first, second = (ref[...] for ref in gains[index])
        first_new, second_new, direction = adapt(weight, first, second, grad)
        weight_norm = jnp.sqrt(total(weight * weight))
        step_norm = jnp.sqrt(total(direction * direction))
        stats, ratio = keep(stats, 4 + index, weight_norm, step_norm)
        new_out, first_out, second_out = gain_outs[index]
        new_out[...] = weight - RATE * ratio * direction
        first_out[...] = first_new
        second_out[...] = second_new
    stats_ref[...] = stats


def finish(sums, weights, directions, norm_set, head_set):
    outs = [shape(w.shape, F32) for w in weights]
    outs += [shape(norm_set[0].shape, F32)] * 3 + [shape(head_set[0].shape, F32)] * 3
    outs += [shape((3, 6), F32)]
    given = (sums, *weights, *directions, *norm_set, *head_set)
    return pl.pallas_call(
        finish_kernel,
        grid=(1,),
        in_specs=whole_specs(given),
        out_specs=whole_specs(outs),
        out_shape=outs,
        compiler_params=params(),
        name="finish",
    )(*given)


def norm_back(grad_in, normed, inv_scale, gain):
    grad_hat = grad_in * gain
    return inv_scale * (grad_hat - normed * jnp.mean(grad_hat * normed, axis=-1, keepdims=True))


def dot_cols(a, b):
    return lax.dot_general(a, b, (((1,), (1,)), ((), ())), preferred_element_type=F32)


def in_order(a, row_table):
    return jnp.concatenate([lax.dynamic_slice_in_dim(a, row_table[j] * CH, CH, 0) for j in range(8)])


def local(
    tokens,
    segments,
    weight_qkv,
    weight_out,
    weight_gate_up,
    weight_down,
    norm_gains,
    head_gains,
    first_qkv,
    first_out,
    first_gate_up,
    first_down,
    first_norm,
    first_head,
    second_qkv,
    second_out,
    second_gate_up,
    second_down,
    second_norm,
    second_head,
    cotangent,
):
    seg_low = jnp.concatenate([segments >> 6, segments & 63]).astype(BF16).reshape(4, 256)
    seg_low = jnp.pad(seg_low, ((0, 12), (0, 128)))
    qkv_low = weight_qkv.astype(BF16)
    w_first, w_second = gather_both(jnp.concatenate([qkv_low[:64], seg_low], axis=0), qkv_low[64:])

    dp = lax.axis_index("dp")
    tensor = lax.axis_index("tensor")
    y, x = dp >> 2, dp & 3
    z, core = tensor >> 1, tensor & 1
    slots = jnp.arange(8, dtype=jnp.int32)
    row_table = 2 * ((z + slots) & 3) + (core ^ (slots >> 2))
    sixteen = jnp.arange(16, dtype=jnp.int32)
    blocks = ((((sixteen >> 2) + y) & 3) << 2) + ((sixteen + x) & 3)
    blocks_turned = blocks.reshape(4, 4).T.reshape(16)
    zero_y, zero_x = -y & 3, -x & 3

    flat_part, weight_squares = pack(weight_qkv, weight_out, weight_gate_up, weight_down)
    flat = lax.all_gather(flat_part, "dp", axis=0, tiled=True)

    attn_in, across, x_rows, dy = prepare(row_table, tokens, cotangent, norm_gains[0:1])
    token_ids = (row_table[:, None] * CH + jnp.arange(CH, dtype=jnp.int32)[None, :]).reshape(ROWS)
    frequency = ROPE_BASE ** (-(jnp.arange(HD // 2, dtype=F32) * 2.0 / HD))
    angles = (dp * ROWS + token_ids).astype(F32)[:, None] * jnp.tile(frequency, 4)[None, :]
    cosine, sine = jnp.cos(angles), jnp.sin(angles)
    seg_rows = in_order(segments, row_table)
    bias = jnp.where(seg_rows == segments[0], 0.0, OFF).astype(F32)[None]
    gain_rows = jnp.concatenate(
        [
            jnp.concatenate([head_gains[0:1], head_gains[0:1]], axis=1),
            jnp.concatenate([head_gains[1:2], jnp.ones((1, HD), F32)], axis=1),
            jnp.zeros((6, 128), F32),
        ]
    )
    projected, queries, q_ext, local_kv, full_qkv = project(
        blocks, attn_in, w_first, w_second, cosine, sine, gain_rows, bias
    )
    kv_first, kv_second = gather_both(local_kv[:256], local_kv[256:])

    first_seg = lax.dynamic_slice(jnp.stack(w_first), (zero_y, zero_x, 64, 0), (1, 1, 4, 256))
    first_seg = first_seg.astype(jnp.int32).reshape(2, ROWS)
    first_seg = in_order(first_seg[0] * 64 + first_seg[1], row_table)
    kinfo = jnp.stack([seg_rows, first_seg, token_ids], axis=1)
    qinfo = jnp.concatenate([seg_rows[None], token_ids[None], jnp.zeros((6, ROWS), jnp.int32)])
    infos = [
        jnp.concatenate([blocks[4 * k : 4 * k + 4], blocks_turned[4 * k : 4 * k + 4], dp[None]])
        for k in range(4)
    ]

    def attend_group(k, first, last, state):
        return attend(first, last, infos[k], q_ext, kv_first[k], kv_second[k], kinfo, qinfo, state)

    state = attend_group(0, True, False, None)
    state = attend_group(1, False, False, state)
    state = attend_group(3, False, False, state)
    mixed, attn_f, log_total = attend_group(2, False, True, state)

    far = out_project(1, mixed, flat, BF16)
    near = out_project(0, mixed, flat, F32)
    own_tokens = lax.dynamic_slice_in_dim(tokens, tensor * CH, CH, 0).astype(F32)
    attn_rows, grad_inner = scatter_tensor(near, far, inner_grad(dy, flat))
    hidden_one = own_tokens + attn_rows
    scale_two = inverse_rms(hidden_one)
    normed_two = hidden_one * scale_two
    ffn_in = gather_tensor((normed_two * norm_gains[1]).astype(BF16))
    inner_act, grad_gate, grad_up, near, far = feed_forward(*ffn_in, grad_inner, flat)

    ffn_part = ffn_out(row_table, inner_act, flat)
    grads = weight_grad([dy], [inner_act], 9)
    grad_ffn_in, (grads, ffn_part) = scatter_tensor(near, far, (grads, ffn_part))
    ffn_total = lax.psum_scatter(ffn_part, "tensor", scatter_dimension=0, tiled=True).astype(F32)
    block_out = lax.all_gather((hidden_one + ffn_total).astype(BF16), "tensor", axis=0, tiled=True)
    gain_ffn = jnp.sum(grad_ffn_in * normed_two, axis=0)
    grad_hidden = dy[:CH].astype(F32) + norm_back(grad_ffn_in, normed_two, scale_two, norm_gains[1])
    grads = weight_grad(ffn_in, [grad_gate, grad_up], 1, grads)
    grad_attn, grads = gather_tensor(grad_hidden.astype(BF16), grads)
    operands = ready(*grad_attn, flat, queries, q_ext, attn_f, log_total)
    grads = weight_grad(grad_attn, [mixed], 0, grads)
    grads = lax.psum_scatter(grads, "dp", scatter_dimension=0, tiled=True)

    def back_group(k, first, last, state):
        return attend_back(
            first, last, infos[k], operands, kv_first[k], kv_second[k], kinfo, qinfo, state
        )

    du, dv = {}, {}
    du[2], dv[2], state = back_group(2, True, False, None)
    du[1], dv[1], state = back_group(1, False, False, state)
    du[3], dv[3], state = back_group(3, False, False, state)
    got_u, got_v = send(du, from_y), send(dv, from_x)
    grad_query, own_u, own_v = back_group(0, False, True, state)
    grad_query, gain_query = heads_back((0, 1), projected, grad_query, cosine, sine, gain_rows)
    query_parts = qkv_grad(blocks, across, grad_query)
    grad_kv = jnp.concatenate(
        [scatter_rest(own_u, got_u, from_x), scatter_rest(own_v, got_v, from_y)]
    ).astype(BF16)
    grad_kv, gain_key = heads_back((2,), projected, grad_kv, cosine, sine, gain_rows)
    kv_parts = qkv_grad(blocks_turned, across, grad_kv)
    query_grad = scatter_rest(query_parts[0], send(query_parts, from_y), from_x)
    kv_got = send(kv_parts, from_x)

    near, far, gain_attn = attn_back(jnp.concatenate([grad_query, grad_kv], axis=1), full_qkv, x_rows)
    grad_attn_in = scatter_tensor(near, far)
    scale_one = inverse_rms(own_tokens)
    normed_one = own_tokens * scale_one
    input_grad = (
        grad_hidden + norm_back(grad_attn_in, normed_one, scale_one, norm_gains[0])
    ).astype(BF16)
    input_grad = place(row_table, gather_tensor(input_grad))

    (out_step, gate_up_step, down_step), later_squares = take_step(
        grads,
        [
            (weight_out, first_out, second_out),
            (weight_gate_up, first_gate_up, second_gate_up),
            (weight_down, first_down, second_down),
        ],
        ((256, True, 1), (1024, False, 2), (1024, True, 3)),
    )
    kv_grad = scatter_rest(kv_parts[0], kv_got, from_y)
    (qkv_step,), qkv_squares = take_step(
        jnp.concatenate([query_grad, kv_grad], axis=1),
        [(weight_qkv, first_qkv, second_qkv)],
        ((384, False, 0),),
    )
    squares = jnp.concatenate(
        [
            gain_query[0:1],
            gain_key[0:1],
            weight_squares[:4].reshape(1, 512),
            (later_squares + qkv_squares)[:4].reshape(1, 512),
            jnp.zeros((1, D - 1280), F32),
        ],
        axis=1,
    )
    sums = sum_all(jnp.concatenate([gain_attn, gain_ffn[None], squares, jnp.zeros((5, D), F32)]))
    steps = (qkv_step, out_step, gate_up_step, down_step)
    done = finish(
        sums,
        (weight_qkv, weight_out, weight_gate_up, weight_down),
        [step[2] for step in steps],
        (norm_gains, first_norm, second_norm),
        (head_gains, first_head, second_head),
    )
    return (
        block_out,
        input_grad,
        *done[:4],
        done[4],
        done[7],
        *[step[0] for step in steps],
        done[5],
        done[8],
        *[step[1] for step in steps],
        done[6],
        done[9],
        done[10],
    )


def solution(mesh):
    matrix_specs = (P("dp", "tensor"), P("tensor", "dp"), P(None, "dp", "tensor"), P("tensor", "dp"), P(), P())
    in_specs = (P("dp", None), P("dp"), *matrix_specs, *matrix_specs, *matrix_specs, P("dp", None))
    out_specs = (P("dp", None), P("dp", None), *matrix_specs, *matrix_specs, *matrix_specs, P())
    return jax.shard_map(local, mesh=mesh, in_specs=in_specs, out_specs=out_specs, check_vma=False)
```

```python
import functools

import jax
import jax.numpy as jnp
from jax import lax
from jax.experimental import pallas as pl
from jax.experimental.pallas import tpu as pltpu
from jax.sharding import PartitionSpec as P

H = 32
KVH = 8
HD = 64
STEP = 5
D = 2048
ROWS = 512
QPK = 4
CH = 64
FLAT_GRAD = 2048 + 1024

EPS_NORM = 1e-05
ROPE_BASE = 1000000.0
BETA_ONE = 0.5
BETA_TWO = 0.5
EPS_ADAM = 1e-06
DECAY = 0.01
RATE = 0.5
F32 = jnp.float32
BF16 = jnp.bfloat16
OFF = -1e5
VMEM_LIMIT = 50 * 1024 * 1024
BACK_US = 8


def inverse_rms(array_in):
    return lax.rsqrt(jnp.mean(array_in * array_in, axis=-1, keepdims=True) + EPS_NORM)


def adapt(weight, first_old, second_old, grad_in):
    first_new = BETA_ONE * first_old + (1.0 - BETA_ONE) * grad_in
    second_new = BETA_TWO * second_old + (1.0 - BETA_TWO) * grad_in * grad_in
    direction = (
        first_new
        / (1.0 - BETA_ONE**STEP)
        / (jnp.sqrt(second_new / (1.0 - BETA_TWO**STEP)) + EPS_ADAM)
        + DECAY * weight
    )
    return (first_new, second_new, direction)


def perm_x(k):
    return [(i, (i // 4) * 4 + (i % 4 - k) % 4) for i in range(16)]


def perm_y(k):
    return [(i, ((i // 4 - k) % 4) * 4 + i % 4) for i in range(16)]


def perm_z(k):
    return [(i, ((i // 2 - k) % 4) * 2 + i % 2) for i in range(8)]


PERM_CORE = [(i, i ^ 1) for i in range(8)]
PERM_PARTNER = [(i, 15 - i) for i in range(16)]


def from_x(a, k):
    return lax.ppermute(a, "dp", perm_x(k))


def from_y(a, k):
    return lax.ppermute(a, "dp", perm_y(k))


def from_z(a, k):
    return lax.ppermute(a, "tensor", perm_z(k))


def from_core(a):
    return lax.ppermute(a, "tensor", PERM_CORE)


def from_partner(a):
    return lax.ppermute(a, "dp", PERM_PARTNER)


def beside(arrays, work):
    return lax.optimization_barrier((arrays, work))


def gather_both(u, v, later):
    row = {k: from_x(u, k) for k in (2, 1, 3)}
    column = {k: from_y(v, k) for k in (2, 1, 3)}
    (row, column), later = beside((row, column), later)
    row = jnp.stack([u, row[1], row[2], row[3]])
    column = jnp.stack([v, column[1], column[2], column[3]])
    second = {k: (from_y(row, k), from_x(column, k)) for k in (2, 1, 3)}
    first = [row] + [second[k][0] for k in (1, 2, 3)]
    return first, [column] + [second[k][1] for k in (1, 2, 3)], later


def gather_dp(a, later):
    row = {k: from_x(a, k) for k in (2, 1, 3)}
    row, later = beside(row, later)
    row = jnp.stack([a, row[1], row[2], row[3]])
    second = {k: from_y(row, k) for k in (2, 1, 3)}
    return [row] + [second[k] for k in (1, 2, 3)], later


def sum_four(own, got):
    return (own.astype(F32) + got[2].astype(F32)) + (got[1].astype(F32) + got[3].astype(F32))


def send(parts, step):
    return {k: step(parts[k], -k) for k in (2, 1, 3)}


def scatter_rest(own, got, step):
    line = sum_four(own, got)
    low = line.astype(BF16)
    return sum_four(line[0], {k: step(low[k], -k) for k in (2, 1, 3)})


def scatter_tensor(near, far, work=None):
    return scatter_ring(near.astype(F32) + from_core(far.astype(BF16)).astype(F32), work)


def scatter_ring(near, work=None):
    parts = near.reshape(4, CH, near.shape[-1])
    low = parts.astype(BF16)
    got = {k: from_z(low[k], -k) for k in (2, 1, 3)}
    if work is None:
        return sum_four(parts[0], got)
    got, work = beside(got, work)
    return sum_four(parts[0], got), work


def gather_tensor(a, work=None):
    got = {k: from_z(a, k) for k in (2, 1, 3)}
    if work is not None:
        got, work = beside(got, work)
    near = jnp.concatenate([a, got[1], got[2], got[3]], axis=0)
    halves = (near, from_core(near))
    return halves if work is None else (halves, work)


def sum_all(a):
    for step in (from_x, from_y, from_z):
        a = (a + step(a, 2)) + (step(a, 1) + step(a, 3))
    return a + from_core(a)


def params(vmem=VMEM_LIMIT):
    return pltpu.CompilerParams(vmem_limit_bytes=vmem)


def takes(us):
    return pl.CostEstimate(flops=int(us * 1.1e9), bytes_accessed=0, transcendentals=0)


def whole_specs(arrays):
    return [pl.BlockSpec(a.shape, lambda i, n=len(a.shape): (0,) * n) for a in arrays]


def prepare_kernel(row_ref, tok_ref, gain_ref, in_ref):
    x = tok_ref[...].astype(F32)
    in_ref[...] = (x * inverse_rms(x) * gain_ref[...]).astype(BF16)


def prepare(row_table, tokens, gain):
    return pl.pallas_call(
        prepare_kernel,
        grid_spec=pltpu.PrefetchScalarGridSpec(
            num_scalar_prefetch=1,
            grid=(8,),
            in_specs=[
                pl.BlockSpec((CH, D), lambda i, r: (r[i], 0)),
                pl.BlockSpec((1, D), lambda i, r: (0, 0)),
            ],
            out_specs=pl.BlockSpec((CH, D), lambda i, r: (i, 0)),
        ),
        out_shape=jax.ShapeDtypeStruct((ROWS, D), BF16),
        compiler_params=params(),
        name="prepare",
        cost_estimate=takes(4),
    )(row_table, tokens, gain)


def arrange_kernel(row_ref, tok_ref, cot_ref, in_ref, across_ref, x_ref, dy_ref):
    x_ref[...] = tok_ref[...]
    dy_ref[...] = cot_ref[...]

    @pl.when(pl.program_id(0) % 2 == 0)
    def _():
        across_ref[...] = in_ref[...].astype(F32).T.astype(BF16)


def arrange(row_table, tokens, cotangent, attn_in):
    pick = pl.BlockSpec((CH, D), lambda i, r: (r[i], 0))
    put = pl.BlockSpec((CH, D), lambda i, r: (i, 0))
    return pl.pallas_call(
        arrange_kernel,
        grid_spec=pltpu.PrefetchScalarGridSpec(
            num_scalar_prefetch=1,
            grid=(8,),
            in_specs=[pick, pick, pl.BlockSpec((128, D), lambda i, r: (i // 2, 0))],
            out_specs=[pl.BlockSpec((D, 128), lambda i, r: (0, i // 2)), put, put],
        ),
        out_shape=[
            jax.ShapeDtypeStruct((D, ROWS), BF16),
            jax.ShapeDtypeStruct((ROWS, D), BF16),
            jax.ShapeDtypeStruct((ROWS, D), BF16),
        ],
        compiler_params=params(),
        name="arrange",
        cost_estimate=takes(7),
    )(row_table, tokens, cotangent, attn_in)


def lane_of(shape):
    return lax.broadcasted_iota(jnp.int32, shape, len(shape) - 1)


def head_sums(a, low_half):
    left = jnp.sum(jnp.where(low_half, a, 0.0), axis=-1, keepdims=True)
    right = jnp.sum(jnp.where(low_half, 0.0, a), axis=-1, keepdims=True)
    return jnp.where(low_half, left, right)


def turn(a, first):
    return jnp.where(first, pltpu.roll(a, 96, 1), pltpu.roll(a, 32, 1))


def vmem_specs(count):
    return [pl.BlockSpec(memory_space=pltpu.VMEM)] * count


def shape(dims, kind):
    return jax.ShapeDtypeStruct(dims, kind)


def column_squares(a):
    total = None
    for at in range(0, a.shape[-1], 128):
        part = a[:, at : at + 128]
        part = jnp.sum(part * part, axis=0, keepdims=True)
        total = part if total is None else total + part
    return total


def eight_rows(rows):
    row = lax.broadcasted_iota(jnp.int32, (8, 128), 0)
    out = jnp.zeros((8, 128), F32)
    for index, value in enumerate(rows):
        if value is not None:
            out = jnp.where(row == index, value, out)
    return out


def pack_kernel(qkv_in, out_in, gate_up_in, down_in, first_ref, second_ref, squares_ref, qkv, out_w, gate_up, down, sems):
    pairs = ((down_in, down), (out_in, out_w), (gate_up_in, gate_up), (qkv_in, qkv))
    copies = [pltpu.make_async_copy(a, b, sems.at[i]) for i, (a, b) in enumerate(pairs)]
    for copy in copies:
        copy.start()
    copies[0].wait()
    first_ref[:, :1024] = down[...].T.astype(BF16)
    copies[1].wait()
    first_ref[:, 1024:] = out_w[...].T.astype(BF16)
    copies[2].wait()
    second_ref[:, :1024] = gate_up[0].astype(BF16)
    second_ref[:, 1024:] = gate_up[1].astype(BF16)
    copies[3].wait()
    squares_ref[...] = eight_rows(
        [
            column_squares(qkv[...]),
            column_squares(out_w[...]),
            column_squares(gate_up[0]) + column_squares(gate_up[1]),
            column_squares(down[...]),
        ]
    )


def pack(weight_qkv, weight_out, weight_gate_up, weight_down):
    given = (weight_qkv, weight_out, weight_gate_up, weight_down)
    return pl.pallas_call(
        pack_kernel,
        in_specs=[pl.BlockSpec(memory_space=pl.ANY)] * 4,
        out_specs=vmem_specs(3),
        out_shape=[shape((128, 1280), BF16), shape((128, 2048), BF16), shape((8, 128), F32)],
        scratch_shapes=[pltpu.VMEM(a.shape, F32) for a in given] + [pltpu.SemaphoreType.DMA((4,))],
        compiler_params=params(),
        name="pack",
        cost_estimate=takes(2),
    )(*given)


def project_kernel(
    blk_ref, x_ref, u0, u1, u2, u3, v0, v1, v2, v3, cos_ref, sin_ref, gain_ref,
    proj_ref, q_own_ref, q_send_ref, kv_ref, w_ref, seg_ref,
):
    @pl.when(pl.program_id(0) == 0)
    def _():
        for at_y in range(4):
            for at_x in range(4):
                slot = at_y * 4 + at_x
                start = pl.multiple_of(blk_ref[slot] * 128, 128)
                w_ref[pl.ds(start, 64), :] = (u0, u1, u2, u3)[at_y][at_x, :64, :]
                w_ref[pl.ds(start + 64, 64), :] = (v0, v1, v2, v3)[at_x][at_y]
                seg_ref[slot] = (u0, u1, u2, u3)[at_y][at_x, 64:, :]

    acc = jnp.dot(x_ref[...], w_ref[...], preferred_element_type=F32)
    proj_ref[...] = acc
    lane = lane_of((x_ref.shape[0], 128))
    low_half = lane < 64
    first = (lane & 63) < 32
    cosine = cos_ref[...]
    sine = jnp.where(first, -sin_ref[...], sin_ref[...])
    for pair in range(3):
        u = acc[:, pair * 128 : (pair + 1) * 128]
        scale = lax.rsqrt(head_sums(u * u, low_half) * (1.0 / HD) + EPS_NORM)
        hat = u * scale * gain_ref[pair // 2 : pair // 2 + 1, :]
        turned = hat * cosine + turn(hat, first) * sine
        if pair < 2:
            across = (turned.astype(BF16).astype(F32) * 0.125).T.astype(BF16)
            out = (q_own_ref, q_send_ref)[pair]
            out[0] = across[:64]
            out[1] = across[64:]
        else:
            kv_ref[...] = jnp.where(low_half, turned, u).astype(BF16)


def project(blocks, x, w_first, w_second, cosine, sine, gains):
    tile = 128
    whole = lambda dims: pl.BlockSpec(dims, lambda i, b: (0,) * len(dims))
    row = lambda width: pl.BlockSpec((tile, width), lambda i, b: (i, 0))
    pair = pl.BlockSpec((2, HD, tile), lambda i, b: (0, 0, i))
    return pl.pallas_call(
        project_kernel,
        grid_spec=pltpu.PrefetchScalarGridSpec(
            num_scalar_prefetch=1,
            grid=(ROWS // tile,),
            in_specs=[row(D)]
            + [whole((4, 80, 384))] * 4
            + [whole((4, 64, 384))] * 4
            + [row(128), row(128), whole((8, 128))],
            out_specs=[row(384), pair, pair, row(128), whole((D, 384)), whole((16, 16, 384))],
        ),
        out_shape=[
            shape((ROWS, 384), F32),
            shape((2, HD, ROWS), BF16),
            shape((2, HD, ROWS), BF16),
            shape((ROWS, 128), BF16),
            shape((D, 384), BF16),
            shape((16, 16, 384), BF16),
        ],
        compiler_params=params(),
        name="project",
        cost_estimate=takes(6),
    )(blocks, x, *w_first, *w_second, cosine, sine, gains)


def lane_masks():
    low = (lane_of((1, 128)) < 64).astype(F32)
    return low.astype(BF16), (1.0 - low).astype(BF16)


def allowed_keys(queries, is_own, at, count, kinfo_ref, qinfo_ref):
    info = kinfo_ref[pl.ds(at, count), :]
    seg = jnp.where(is_own, info[:, queries : queries + 1], info[:, 2:3])
    pos = jnp.where(is_own, info[:, 3:4], -1)
    return (seg == qinfo_ref[queries : queries + 1, :]) & (pos <= qinfo_ref[2:3, :])


def for_queries(blk_ref, slot, own_at, sets, work):
    block = blk_ref[slot]
    for queries in range(sets):
        own = blk_ref[own_at + queries]

        @pl.when((block == 0) | (block == own))
        def _(queries=queries, own=own):
            work(queries, True, block == own)

        @pl.when((block > 0) & (block < own))
        def _(queries=queries):
            work(queries, False, None)


def forward_kernel(
    blk_ref, q_first, q_second, kv0, kv1, kv2, kv3, kinfo_ref, qinfo_ref, bias_ref,
    mixed_ref, out_ref, lse_ref, send_ref, kv_all, q_t, acc,
):
    for group, ref in enumerate((kv0, kv1, kv2, kv3)):
        kv_all[group * 4 : (group + 1) * 4] = ref[...]
    acc[...] = jnp.zeros_like(acc)
    row = lax.broadcasted_iota(jnp.int32, (64, ROWS), 0)
    bias = jnp.where(row == 0, bias_ref[0:1, :], 0.0).astype(BF16)
    for head in range(QPK):
        q_t[head, :64, :] = (q_first, q_second)[head // 2][head % 2]
        q_t[head, 64:, :] = bias
    keep_k, keep_v = lane_masks()

    def step(slot, carry):
        def work(queries, masked, is_own):
            kv = kv_all[slot]
            keys = kv * keep_k + (keep_v if not masked else jnp.zeros_like(keep_v))
            vals = (kv * keep_v + keep_k).astype(F32).T.astype(BF16)[56:]
            if masked:
                allowed = allowed_keys(queries, is_own, 0, ROWS, kinfo_ref, qinfo_ref)
            for head in range(QPK):
                scores = jnp.dot(keys, q_t[head], preferred_element_type=F32)
                probs = jnp.exp(scores)
                if masked:
                    probs = jnp.where(allowed, probs, 0.0)
                acc[head] += jnp.dot(vals, probs.astype(BF16), preferred_element_type=F32)

        for_queries(blk_ref, slot, 16, 1, work)
        return carry

    lax.fori_loop(0, 16, step, 0)
    heads = []
    logs = []
    for head in range(QPK):
        total = acc[head, 0:1, :]
        heads.append(acc[head, 8:, :] / total)
        logs.append(jnp.log(total))
    mixed_ref[...] = jnp.concatenate(heads, axis=0).T.astype(BF16)
    rest = jnp.zeros((6, ROWS), F32)
    out_ref[:64], out_ref[64:] = heads[0], heads[1]
    lse_ref[...] = jnp.concatenate(logs[:2] + [rest], axis=0)
    send_ref[:64], send_ref[64:128] = heads[2], heads[3]
    send_ref[128:] = jnp.concatenate(logs[2:] + [rest], axis=0)


def attend(blocks, q_first, q_second, kv, kinfo, qinfo, bias):
    return pl.pallas_call(
        forward_kernel,
        in_specs=[pl.BlockSpec(memory_space=pltpu.SMEM)] + vmem_specs(9),
        out_specs=vmem_specs(5),
        out_shape=[
            shape((ROWS, 256), BF16),
            shape((128, ROWS), F32),
            shape((8, ROWS), F32),
            shape((136, ROWS), F32),
            shape((16, ROWS, 128), BF16),
        ],
        scratch_shapes=[
            pltpu.VMEM((QPK, 128, ROWS), BF16),
            pltpu.VMEM((QPK, 72, ROWS), F32),
        ],
        compiler_params=params(),
        name="attend",
        cost_estimate=takes(20),
    )(blocks, q_first, q_second, *kv, kinfo, qinfo, bias)


def three_rows(row, value, at):
    high = value.astype(BF16).astype(F32)
    rest = value - high
    middle = rest.astype(BF16).astype(F32)
    low = rest - middle
    return (
        jnp.where(row == at, high, 0.0)
        + jnp.where(row == at + 1, middle, 0.0)
        + jnp.where(row == at + 2, low, 0.0)
    )


def mixed_grad_kernel(near_ref, far_ref, w_ref, own_ref, send_ref):
    w = w_ref[...]
    for half, ref in enumerate((near_ref, far_ref)):
        part = jnp.dot(ref[...], w, preferred_element_type=F32).astype(BF16)
        own_ref[half * 256 : (half + 1) * 256] = part[:, :128]
        send_ref[half * 256 : (half + 1) * 256] = part[:, 128:]


def mixed_grad(near, far, down_out):
    whole = lambda dims: pl.BlockSpec(dims, lambda i: (0, 0))
    return pl.pallas_call(
        mixed_grad_kernel,
        grid=(1,),
        in_specs=[whole((256, D)), whole((256, D)), pl.BlockSpec((D, 256), lambda i: (0, 4))],
        out_specs=[whole((ROWS, 128))] * 2,
        out_shape=[shape((ROWS, 128), BF16)] * 2,
        compiler_params=params(),
        name="mixed_grad",
        cost_estimate=takes(2),
    )(near, far, down_out)


def ready_kernel(do_own, do_other, out_own, lse_own, out_other, q_own, q_other, bias_ref, q_t, do_t, q_pad, do_pad):
    row = lax.broadcasted_iota(jnp.int32, (64, ROWS), 0)
    low_half = lane_of((ROWS, 128)) < 64
    for queries in range(2):
        do = (do_own, do_other)[queries][...].astype(F32)
        q_ref = (q_own, q_other)[queries]
        q = jnp.concatenate([q_ref[0].astype(F32), q_ref[1].astype(F32)], axis=0).T
        do_turned = do.T
        dots = do_turned * (out_own, out_other)[queries][:128, :]
        for part in range(2):
            head = 2 * queries + part
            at = slice(part * 64, (part + 1) * 64)
            delta = jnp.sum(dots[at, :], axis=0, keepdims=True)
            lse = (out_other[128 + part : 129 + part, :] if queries else lse_own[part : part + 1, :])
            extra = three_rows(row, -lse, 0)
            extra = extra + jnp.where(row == 3, bias_ref[queries : queries + 1, :], 0.0)
            q_t[head, :64, :] = q_ref[part]
            q_t[head, 64:, :] = extra.astype(BF16)
            do_t[head, :64, :] = three_rows(row, -delta, 0).astype(BF16)
            do_t[head, 64:, :] = do_turned[at, :].astype(BF16)
            q_head = pltpu.roll(q, 64, 1) if part else q
            do_head = do if part else pltpu.roll(do, 64, 1)
            q_pad[head] = jnp.where(low_half, q_head, 0.0).astype(BF16)
            do_pad[head] = jnp.where(low_half, 0.0, do_head).astype(BF16)


def ready(*given):
    return pl.pallas_call(
        ready_kernel,
        in_specs=vmem_specs(len(given)),
        out_specs=vmem_specs(4),
        out_shape=[shape((QPK, 128, ROWS), BF16)] * 2 + [shape((QPK, ROWS, 128), BF16)] * 2,
        compiler_params=params(),
        name="ready",
        cost_estimate=takes(2.5),
    )(*given)


def backward_kernel(first, last, count, blk_ref, q_t, do_t, q_pad, do_pad, kv_all, kinfo_ref, qinfo_ref, *rest):
    dq_t, total = rest[-2:]
    outs = rest[-2 - count : -2]
    if first:
        dq_t[...] = jnp.zeros_like(dq_t)
    else:
        dq_t[...] = rest[0][...]
    keep_k, keep_v = lane_masks()
    keep_v_masked = jnp.where(lane_of((1, 128)) == 67, 0.0, keep_v.astype(F32)).astype(BF16)

    def step(slot, carry):
        total[...] = jnp.zeros_like(total)

        def work(queries, masked, is_own):
            kv = kv_all[blk_ref[4 * count + 2 + slot]]
            keys = kv * keep_k + (keep_v_masked if masked else keep_v)
            vals = kv * keep_v + keep_k
            keys_turned = kv.astype(F32).T[:64, :].astype(BF16)
            if masked:
                allowed = allowed_keys(queries, is_own, 0, ROWS, kinfo_ref, qinfo_ref)
            for head in (2 * queries, 2 * queries + 1):
                scores = jnp.dot(keys, q_t[head], preferred_element_type=F32)
                probs = jnp.exp(scores)
                if masked:
                    probs = jnp.where(allowed, probs, 0.0)
                grads = jnp.dot(vals, do_t[head], preferred_element_type=F32)
                grads = (probs * grads).astype(BF16)
                term = jnp.dot(probs.astype(BF16), do_pad[head], preferred_element_type=F32)
                total[...] += term + jnp.dot(grads, q_pad[head], preferred_element_type=F32)
                dq_t[head * 64 : (head + 1) * 64, :] += jnp.dot(
                    keys_turned, grads, preferred_element_type=F32
                )

        for_queries(blk_ref, slot, 4 * count, 2, work)

        for index, ref in enumerate(outs):

            @pl.when(slot // 4 == index)
            def _(index=index, ref=ref):
                ref[slot - 4 * index] = total[...].astype(BF16)

        return carry

    lax.fori_loop(0, 4 * count, step, 0)
    if last:
        dq = (dq_t[...].T * 0.125).astype(BF16)
        rest[1][...] = dq[:, :128]
        rest[2][...] = dq[:, 128:]


def attend_back(first, last, count, blocks, operands, kv, kinfo, qinfo, dq=None):
    given = [*operands, kv, kinfo, qinfo] + ([] if first else [dq])
    dkv = [shape((4, ROWS, 128), BF16)] * count
    pair = shape((ROWS, 128), BF16)
    outs = [pair, pair] + dkv if last else dkv + [shape((256, ROWS), F32)]
    return pl.pallas_call(
        functools.partial(backward_kernel, first, last, count),
        in_specs=[pl.BlockSpec(memory_space=pltpu.SMEM)] + vmem_specs(len(given)),
        out_specs=vmem_specs(len(outs)),
        out_shape=outs,
        scratch_shapes=([pltpu.VMEM((256, ROWS), F32)] if last else [])
        + [pltpu.VMEM((ROWS, 128), F32)],
        compiler_params=params(),
        name="attend_back",
        cost_estimate=takes(BACK_US * count),
    )(blocks, *given)


def heads_back_kernel(proj_ref, own_ref, other_ref, kv_ref, cos_ref, sin_ref, gain_ref, out_ref, sum_ref):
    lane = lane_of((proj_ref.shape[0], 128))
    low_half = lane < 64
    first = (lane & 63) < 32
    cosine = cos_ref[...]
    sine = jnp.where(first, sin_ref[...], -sin_ref[...])
    sums = []
    for pair in range(3):
        at = slice(pair * 128, (pair + 1) * 128)
        u = proj_ref[:, at]
        grad = (own_ref, other_ref, kv_ref)[pair][...].astype(F32)
        scale = lax.rsqrt(head_sums(u * u, low_half) * (1.0 / HD) + EPS_NORM)
        hat = u * scale
        turned = grad * cosine + turn(grad, first) * sine
        sums.append(jnp.sum(turned * hat, axis=0, keepdims=True))
        grad_hat = turned * gain_ref[pair // 2 : pair // 2 + 1, :]
        mean = head_sums(grad_hat * hat, low_half) * (1.0 / HD)
        back = scale * (grad_hat - hat * mean)
        if pair == 2:
            back = jnp.where(low_half, back, grad)
        out_ref[:, at] = back.astype(BF16)

    @pl.when(pl.program_id(0) == 0)
    def _():
        sum_ref[...] = jnp.zeros_like(sum_ref)

    sum_ref[0:1, :] += sums[0] + sums[1]
    sum_ref[1:2, :] += sums[2]


def heads_back(proj, own, other, kv, cosine, sine, gains):
    tile = 128
    row = lambda width: pl.BlockSpec((tile, width), lambda i: (i, 0))
    whole = pl.BlockSpec((8, 128), lambda i: (0, 0))
    return pl.pallas_call(
        heads_back_kernel,
        grid=(ROWS // tile,),
        in_specs=[row(384), row(128), row(128), row(128), row(128), row(128), whole],
        out_specs=[row(384), whole],
        out_shape=[shape((ROWS, 384), BF16), shape((8, 128), F32)],
        compiler_params=params(),
        name="heads_back",
        cost_estimate=takes(2),
    )(proj, own, other, kv, cosine, sine, gains)


def out_kernel(mixed_ref, w_ref, out_ref):
    out_ref[...] = dot_cols(mixed_ref[...], w_ref[...]).astype(out_ref.dtype)


def out_project(half, mixed, down_out, kind):
    return pl.pallas_call(
        out_kernel,
        grid=(1,),
        in_specs=[
            pl.BlockSpec((256, 256), lambda i: (half, 0)),
            pl.BlockSpec((D, 256), lambda i: (0, 4)),
        ],
        out_specs=pl.BlockSpec((256, D), lambda i: (0, 0)),
        out_shape=shape((256, D), kind),
        compiler_params=params(),
        name="out_project",
        cost_estimate=takes(1.8),
    )(mixed, down_out)


def ffn_kernel(
    near_ref, far_ref, grad_ref, gate_w, up_w, rows_w, act_ref, gate_ref, up_ref, near_out, far_out, x_all, both
):
    step = pl.program_id(0)

    @pl.when(step == 0)
    def _():
        x_all[:256] = near_ref[...]
        x_all[256:] = far_ref[...]

    for tile in range(4):

        @pl.when(step == tile)
        def _(tile=tile):
            x = x_all[...]
            gate = jnp.dot(x, gate_w[...], preferred_element_type=F32)
            up = jnp.dot(x, up_w[...], preferred_element_type=F32)
            inner = grad_ref[...]
            sigmoid = jax.nn.sigmoid(gate)
            activated = gate * sigmoid
            act_ref[...] = (activated * up).astype(BF16)
            grad_gate = (inner * up * sigmoid * (1.0 + gate * (1.0 - sigmoid))).astype(BF16)
            grad_up = (inner * activated).astype(BF16)
            gate_ref[...] = grad_gate
            up_ref[...] = grad_up
            both[:, tile * 256 : (tile + 1) * 256] = grad_gate
            both[:, 1024 + tile * 256 : 1024 + (tile + 1) * 256] = grad_up

    @pl.when(step >= 4)
    def _():
        part = dot_cols(both[...], rows_w[...])
        near_out[...] = part[:256]
        far_out[...] = part[256:].astype(BF16)


def feed_forward(near, far, grad_inner, gate_up):
    whole = lambda dims: pl.BlockSpec(dims, lambda j: (0, 0))
    tile = pl.BlockSpec((ROWS, 256), lambda j: (0, jnp.minimum(j, 3)))
    last = lambda j: jnp.maximum(j - 4, 0)
    return pl.pallas_call(
        ffn_kernel,
        grid=(8,),
        in_specs=[
            whole((256, D)),
            whole((256, D)),
            tile,
            pl.BlockSpec((D, 256), lambda j: (0, jnp.minimum(j, 3))),
            pl.BlockSpec((D, 256), lambda j: (0, 4 + jnp.minimum(j, 3))),
            pl.BlockSpec((512, 2048), lambda j: (last(j), 0)),
        ],
        out_specs=[tile, tile, tile]
        + [pl.BlockSpec((256, 512), lambda j: (0, last(j)))] * 2,
        out_shape=[shape((ROWS, 1024), BF16)] * 3 + [shape((256, D), F32), shape((256, D), BF16)],
        scratch_shapes=[pltpu.VMEM((ROWS, D), BF16), pltpu.VMEM((ROWS, 2048), BF16)],
        compiler_params=params(),
        name="feed_forward",
        cost_estimate=takes(13),
    )(near, far, grad_inner, gate_up, gate_up, gate_up)


def inner_grad_kernel(dy_ref, w_ref, out_ref):
    out_ref[...] = jnp.dot(dy_ref[...], w_ref[...], preferred_element_type=F32)


def inner_grad(dy, down_out):
    return pl.pallas_call(
        inner_grad_kernel,
        grid=(4,),
        in_specs=[
            pl.BlockSpec((ROWS, D), lambda j: (0, 0)),
            pl.BlockSpec((D, 256), lambda j: (0, j)),
        ],
        out_specs=pl.BlockSpec((ROWS, 256), lambda j: (0, j)),
        out_shape=shape((ROWS, 1024), F32),
        compiler_params=params(),
        name="inner_grad",
        cost_estimate=takes(5.5),
    )(dy, down_out)


def ffn_out_kernel(act_ref, w_ref, near_ref, far_ref, acc):
    step = pl.program_id(0)
    term = dot_cols(act_ref[...], w_ref[...])

    @pl.when(step == 0)
    def _():
        acc[...] = term

    @pl.when(step > 0)
    def _():
        acc[...] += term

    @pl.when(step == pl.num_programs(0) - 1)
    def _():
        near_ref[...] = acc[:256]
        far_ref[...] = acc[256:].astype(BF16)


def ffn_out(act, down_out):
    whole = lambda dims: pl.BlockSpec(dims, lambda j: (0, 0))
    return pl.pallas_call(
        ffn_out_kernel,
        grid=(4,),
        in_specs=[
            pl.BlockSpec((ROWS, 256), lambda j: (0, j)),
            pl.BlockSpec((D, 256), lambda j: (0, j)),
        ],
        out_specs=[whole((256, D)), whole((256, D))],
        out_shape=[shape((256, D), F32), shape((256, D), BF16)],
        scratch_shapes=[pltpu.VMEM((ROWS, D), F32)],
        compiler_params=params(),
        name="ffn_out",
        cost_estimate=takes(6.5),
    )(act, down_out)


def out_grad_kernel(blk_ref, near_ref, far_ref, mixed_ref, out_ref, turned):
    turned[:, :256] = near_ref[...].astype(F32).T.astype(BF16)
    turned[:, 256:] = far_ref[...].astype(F32).T.astype(BF16)
    mixed = mixed_ref[...]
    for slot in range(16):
        at = pl.ds(pl.multiple_of(blk_ref[slot] * 128, 128), 128)
        out = jnp.dot(turned[at, :], mixed, preferred_element_type=F32)
        out_ref[slot // 4, slot % 4] = out.astype(BF16)


def out_grad(blocks, near, far, mixed):
    return pl.pallas_call(
        out_grad_kernel,
        in_specs=[pl.BlockSpec(memory_space=pltpu.SMEM)] + vmem_specs(3),
        out_specs=vmem_specs(1)[0],
        out_shape=shape((4, 4, 128, 256), BF16),
        scratch_shapes=[pltpu.VMEM((D, ROWS), BF16)],
        compiler_params=params(),
        name="out_grad",
        cost_estimate=takes(2),
    )(blocks, near, far, mixed)


def qkv_out_grad_kernel(blk_ref, across_ref, grad_ref, parts_ref, u_ref, v_ref):
    grad = grad_ref[...]
    for slot in range(16):
        at_y, at_x = slot // 4, slot % 4
        at = pl.ds(pl.multiple_of(blk_ref[slot] * 128, 128), 128)
        part = jnp.dot(across_ref[at, :], grad, preferred_element_type=F32).astype(BF16)
        u_ref[at_y, at_x, :, :384] = part[:64]
        u_ref[at_y, at_x, :, 384:] = parts_ref[at_y, at_x, :64]
        v_ref[at_x, at_y, :, :384] = part[64:]
        v_ref[at_x, at_y, :, 384:] = parts_ref[at_y, at_x, 64:]


def qkv_out_grad(blocks, across, grad, out_parts):
    return pl.pallas_call(
        qkv_out_grad_kernel,
        in_specs=[pl.BlockSpec(memory_space=pltpu.SMEM)] + vmem_specs(3),
        out_specs=vmem_specs(2),
        out_shape=[shape((4, 4, 64, 640), BF16)] * 2,
        compiler_params=params(),
        name="qkv_out_grad",
        cost_estimate=takes(3),
    )(blocks, across, grad, out_parts)


def attn_back_kernel(grad_ref, w_ref, x_ref, near_ref, far_ref, gain_ref):
    step = pl.program_id(0)
    part = dot_cols(grad_ref[...], w_ref[...])
    x = x_ref[...].astype(F32)
    sums = jnp.sum(part * (x * inverse_rms(x)), axis=0, keepdims=True)

    @pl.when(step == 0)
    def _():
        gain_ref[...] = sums

    @pl.when(step > 0)
    def _():
        gain_ref[...] += sums

    @pl.when(step < 2)
    def _():
        far_ref[...] = part.astype(BF16)

    @pl.when(step >= 2)
    def _():
        near_ref[...] = part


def attn_back(grad, w, x):
    tile = 128
    turn_rows = lambda i: ((i + 2) % 4, 0)
    return pl.pallas_call(
        attn_back_kernel,
        grid=(4,),
        in_specs=[
            pl.BlockSpec((tile, 384), turn_rows),
            pl.BlockSpec((D, 384), lambda i: (0, 0)),
            pl.BlockSpec((tile, D), turn_rows),
        ],
        out_specs=[
            pl.BlockSpec((tile, D), lambda i: (jnp.maximum(i - 2, 0), 0)),
            pl.BlockSpec((tile, D), lambda i: (jnp.minimum(i, 1), 0)),
            pl.BlockSpec((1, D), lambda i: (0, 0)),
        ],
        out_shape=[shape((256, D), F32), shape((256, D), BF16), shape((1, D), F32)],
        compiler_params=params(),
        name="attn_back",
        cost_estimate=takes(6),
    )(grad, w, x)


def weight_grad_kernel(parts, wide, *refs):
    lhs, rhs = refs[:parts], refs[parts : parts + len(wide)]
    out_ref, turned = refs[-2:]
    step = pl.program_id(0)

    @pl.when(step == 0)
    def _():
        rows = ROWS // parts
        for index, ref in enumerate(lhs):
            turned[:, index * rows : (index + 1) * rows] = ref[...].astype(F32).T.astype(BF16)

    start = 0
    for ref, count in zip(rhs, wide, strict=True):

        @pl.when((step >= start) & (step < start + count))
        def _(ref=ref):
            out_ref[...] = jnp.dot(turned[...], ref[...], preferred_element_type=F32).astype(BF16)

        start += count


def weight_grad(lhs, rhs, at, flat=None):
    wide = [a.shape[1] // 256 for a in rhs]
    starts = [sum(wide[:i]) for i in range(len(wide))]
    given = [*lhs, *rhs] + ([] if flat is None else [flat])
    specs = [pl.BlockSpec(a.shape, lambda i: (0, 0)) for a in lhs]
    for start, count in zip(starts, wide, strict=True):
        specs.append(
            pl.BlockSpec(
                (ROWS, 256),
                lambda i, start=start, count=count: (0, jnp.clip(i - start, 0, count - 1)),
            )
        )
    if flat is not None:
        specs.append(pl.BlockSpec(memory_space=pl.ANY))
    return pl.pallas_call(
        functools.partial(weight_grad_kernel, len(lhs), wide),
        grid=(sum(wide),),
        in_specs=specs,
        out_specs=pl.BlockSpec((D, 256), lambda i: (0, at + i)),
        out_shape=shape((D, FLAT_GRAD), BF16),
        scratch_shapes=[pltpu.VMEM((D, ROWS), BF16)],
        input_output_aliases={} if flat is None else {len(given) - 1: 0},
        compiler_params=params(),
        name="weight_grad",
        cost_estimate=takes(1.25 * sum(wide)),
    )(*given)


def step_kernel(wide, *refs):
    count = len(wide)
    squares = []
    for index, (given, start, columns, turned, row) in enumerate(wide):
        weight, first, second = refs[at_of(wide) + 3 * index : at_of(wide) + 3 * index + 3]
        base = at_of(wide) + 3 * count + 3 * index
        first_out, second_out, direction_out = refs[base : base + 3]
        total = None
        for part in range(2 if len(weight.shape) == 3 else 1):
            grad = refs[given][:, start : start + columns].astype(F32)
            start += columns
            if turned:
                grad = grad.T
            pick = (part,) if len(weight.shape) == 3 else (slice(None),)
            first_new, second_new, direction = adapt(weight[pick], first[pick], second[pick], grad)
            first_out[pick] = first_new
            second_out[pick] = second_new
            direction_out[pick] = direction
            sums = column_squares(direction)
            total = sums if total is None else total + sums
        squares.append((row, total))
    refs[-1][...] = eight_rows([dict(squares).get(row) for row in range(8)])


def at_of(wide):
    return 1 + max(entry[0] for entry in wide)


def take_step(grads, matrices, wide):
    given = [*grads, *[a for matrix in matrices for a in matrix]]
    outs = [shape(matrix[0].shape, F32) for matrix in matrices for _ in range(3)]
    out = pl.pallas_call(
        functools.partial(step_kernel, wide),
        grid=(1,),
        in_specs=whole_specs(given),
        out_specs=whole_specs(outs + [shape((8, 128), F32)]),
        out_shape=outs + [shape((8, 128), F32)],
        compiler_params=params(),
        name="take_step",
        cost_estimate=takes(4),
    )(*given)
    return [out[3 * i : 3 * i + 3] for i in range(len(matrices))], out[-1]


def finish_kernel(*refs):
    sums = refs[0]
    weights, directions = refs[1:5], refs[5:9]
    gains = (refs[9:12], refs[12:15])
    outs = refs[15:19]
    gain_outs = (refs[19:22], refs[22:25])
    stats_ref = refs[25]
    row = lax.broadcasted_iota(jnp.int32, (3, 6), 0)
    column = lax.broadcasted_iota(jnp.int32, (3, 6), 1)
    stats = jnp.zeros((3, 6), F32)

    def total(a):
        return jnp.sum(jnp.sum(a, axis=1, keepdims=True), axis=0, keepdims=True)

    def keep(stats, index, weight_norm, step_norm):
        ratio = weight_norm / (step_norm + EPS_ADAM)
        values = jnp.where(row == 0, weight_norm, jnp.where(row == 1, step_norm, ratio))
        return jnp.where(column == index, values, stats), ratio

    for index in range(4):
        weight_norm = jnp.sqrt(total(sums[2:3, 256 + index * 128 : 384 + index * 128]))
        step_norm = jnp.sqrt(total(sums[2:3, 768 + index * 128 : 896 + index * 128]))
        stats, ratio = keep(stats, index, weight_norm, step_norm)
        weight, direction, out = weights[index], directions[index], outs[index]
        if len(weight.shape) == 3:
            for part in range(2):
                out[part] = weight[part] - RATE * ratio * direction[part]
        else:
            out[...] = weight[...] - RATE * ratio * direction[...]
    query_gain = sums[2:3, 0:64] + sums[2:3, 64:128]
    head_grad = jnp.concatenate([query_gain, sums[2:3, 128:192]], axis=0)
    for index, grad in enumerate((sums[0:2, :], head_grad)):
        weight, first, second = (ref[...] for ref in gains[index])
        first_new, second_new, direction = adapt(weight, first, second, grad)
        weight_norm = jnp.sqrt(total(weight * weight))
        step_norm = jnp.sqrt(total(direction * direction))
        stats, ratio = keep(stats, 4 + index, weight_norm, step_norm)
        new_out, first_out, second_out = gain_outs[index]
        new_out[...] = weight - RATE * ratio * direction
        first_out[...] = first_new
        second_out[...] = second_new
    stats_ref[...] = stats


def finish(sums, weights, directions, norm_set, head_set):
    outs = [shape(w.shape, F32) for w in weights]
    outs += [shape(norm_set[0].shape, F32)] * 3 + [shape(head_set[0].shape, F32)] * 3
    outs += [shape((3, 6), F32)]
    given = (sums, *weights, *directions, *norm_set, *head_set)
    return pl.pallas_call(
        finish_kernel,
        grid=(1,),
        in_specs=whole_specs(given),
        out_specs=whole_specs(outs),
        out_shape=outs,
        compiler_params=params(),
        name="finish",
        cost_estimate=takes(3),
    )(*given)


def norm_back(grad_in, normed, inv_scale, gain):
    grad_hat = grad_in * gain
    return inv_scale * (grad_hat - normed * jnp.mean(grad_hat * normed, axis=-1, keepdims=True))


def dot_cols(a, b):
    return lax.dot_general(a, b, (((1,), (1,)), ((), ())), preferred_element_type=F32)


def in_order(a, row_table):
    return jnp.concatenate([lax.dynamic_slice_in_dim(a, row_table[j] * CH, CH, 0) for j in range(8)])


def local(
    tokens,
    segments,
    weight_qkv,
    weight_out,
    weight_gate_up,
    weight_down,
    norm_gains,
    head_gains,
    first_qkv,
    first_out,
    first_gate_up,
    first_down,
    first_norm,
    first_head,
    second_qkv,
    second_out,
    second_gate_up,
    second_down,
    second_norm,
    second_head,
    cotangent,
):
    seg_low = jnp.concatenate([segments >> 6, segments & 63]).astype(BF16).reshape(4, 256)
    seg_low = jnp.pad(seg_low, ((0, 12), (0, 128)))
    qkv_low = weight_qkv.astype(BF16)
    w_first, w_second, tokens = gather_both(
        jnp.concatenate([qkv_low[:64], seg_low], axis=0), qkv_low[64:], tokens
    )

    dp = lax.axis_index("dp")
    tensor = lax.axis_index("tensor")
    y, x = dp >> 2, dp & 3
    z, core = tensor >> 1, tensor & 1
    slots = jnp.arange(8, dtype=jnp.int32)
    row_table = 2 * ((z + slots) & 3) + (core ^ (slots >> 2))
    sixteen = jnp.arange(16, dtype=jnp.int32)
    blocks = ((((sixteen >> 2) + y) & 3) << 2) + ((sixteen + x) & 3)
    blocks_turned = ((((sixteen) + y) & 3) << 2) + (((sixteen >> 2) + x) & 3)
    own_blocks = jnp.stack([dp, 15 - dp])
    zero_slot = ((-y & 3) << 2) + (-x & 3)
    partner_slot = (((3 - 2 * y) & 3) << 2) + ((3 - 2 * x) & 3)

    down_out, gate_up, weight_squares = pack(weight_qkv, weight_out, weight_gate_up, weight_down)
    down_out = lax.all_gather(down_out, "dp", axis=0, tiled=True)
    gate_up = lax.all_gather(gate_up, "dp", axis=0, tiled=True)

    attn_in = prepare(row_table, tokens, norm_gains[0:1])
    token_ids = (row_table[:, None] * CH + jnp.arange(CH, dtype=jnp.int32)[None, :]).reshape(ROWS)
    frequency = ROPE_BASE ** (-(jnp.arange(HD // 2, dtype=F32) * 2.0 / HD))
    angles = (dp * ROWS + token_ids).astype(F32)[:, None] * jnp.tile(frequency, 4)[None, :]
    cosine, sine = jnp.cos(angles), jnp.sin(angles)
    gain_rows = jnp.concatenate(
        [
            jnp.concatenate([head_gains[0:1], head_gains[0:1]], axis=1),
            jnp.concatenate([head_gains[1:2], jnp.ones((1, HD), F32)], axis=1),
            jnp.zeros((6, 128), F32),
        ]
    )
    projected, q_own, q_send, local_kv, full_qkv, all_segs = project(
        blocks, attn_in, w_first, w_second, cosine, sine, gain_rows
    )
    kv_groups, (all_segs, tokens, cotangent) = gather_dp(local_kv, (all_segs, tokens, cotangent))
    kv_groups, (across, x_rows, dy) = beside(
        kv_groups, arrange(row_table, tokens, cotangent, attn_in)
    )

    def block_segs(slot):
        got = lax.dynamic_slice(all_segs, (slot, 0, 0), (1, 4, 256)).astype(jnp.int32).reshape(2, ROWS)
        return got[0] * 64 + got[1]

    partner_segs = block_segs(partner_slot)
    seg_rows = in_order(segments, row_table)
    first_rows = in_order(block_segs(zero_slot), row_table)
    partner_rows = in_order(partner_segs, row_table)
    kinfo = jnp.stack([seg_rows, partner_rows, first_rows, token_ids], axis=1)
    qinfo = jnp.concatenate(
        [seg_rows[None], partner_rows[None], token_ids[None], jnp.zeros((5, ROWS), jnp.int32)]
    )
    bias = jnp.concatenate(
        [
            jnp.where(seg_rows == segments[0], 0.0, OFF).astype(F32)[None],
            jnp.where(partner_rows == partner_segs[0], 0.0, OFF).astype(F32)[None],
            jnp.zeros((6, ROWS), F32),
        ]
    )
    mixed, out_own, log_own, out_send, kv_all = attend(
        jnp.concatenate([blocks, own_blocks]), q_own, q_send, kv_groups, kinfo, qinfo, bias
    )

    far = out_project(1, mixed, down_out, BF16)
    near = out_project(0, mixed, down_out, F32)
    own_tokens = x_rows[:CH].astype(F32)
    attn_rows, grad_inner = scatter_tensor(near, far, inner_grad(dy, down_out))
    hidden_one = own_tokens + attn_rows
    scale_two = inverse_rms(hidden_one)
    normed_two = hidden_one * scale_two
    ffn_in, (out_other, q_other) = gather_tensor(
        (normed_two * norm_gains[1]).astype(BF16), (from_partner(out_send), from_partner(q_send))
    )
    inner_act, grad_gate, grad_up, near, far = feed_forward(*ffn_in, grad_inner, gate_up)

    grads = weight_grad([dy], [inner_act], 8)
    grads = weight_grad(ffn_in, [grad_gate, grad_up], 0, grads)
    grad_ffn_in, grads = scatter_tensor(near, far, grads)
    grads = lax.psum_scatter(grads, "dp", scatter_dimension=0, tiled=True)
    gain_ffn = jnp.sum(grad_ffn_in * normed_two, axis=0)
    grad_hidden = dy[:CH].astype(F32) + norm_back(grad_ffn_in, normed_two, scale_two, norm_gains[1])
    ffn_parts = ffn_out(inner_act, down_out)
    grad_attn, (ffn_near, ffn_far) = gather_tensor(grad_hidden.astype(BF16), ffn_parts)

    do_own, do_send = mixed_grad(*grad_attn, down_out)
    do_other = from_partner(do_send)
    out_parts = out_grad(blocks, *grad_attn, mixed)
    do_other, out_parts = beside(do_other, out_parts)
    ffn_far = from_core(ffn_far)
    operands = ready(do_own, do_other, out_own, log_own, out_other, q_own, q_other, bias)

    def back_groups(groups, first, last, state):
        info = jnp.concatenate(
            [blocks[4 * k : 4 * k + 4] for k in groups]
            + [own_blocks]
            + [sixteen[4 * k : 4 * k + 4] for k in groups]
        )
        return attend_back(first, last, len(groups), info, operands, kv_all, kinfo, qinfo, state)

    got = {}
    part, state = back_groups((2,), True, False, None)
    got[2] = from_y(part, -2)
    part, state = back_groups((1,), False, False, state)
    got[1] = from_y(part, -1)
    (got[2], ffn_far), state = beside((got[2], ffn_far), state)
    ffn_near = (ffn_near + ffn_far.astype(F32)).reshape(4, CH, D)
    ffn_low = ffn_near.astype(BF16)
    ffn_got = {k: from_z(ffn_low[k], -k) for k in (2, 1, 3)}
    part, state = back_groups((3,), False, False, state)
    got[3] = from_y(part, -3)
    (got[1], ffn_got), state = beside((got[1], ffn_got), state)
    dq_own, dq_send, own_part = back_groups((0,), False, True, state)
    dq_other = from_partner(dq_send)
    block_rows = (hidden_one + sum_four(ffn_near[0], ffn_got)).astype(BF16)
    block_out = lax.all_gather(block_rows, "tensor", axis=0, tiled=True)

    line = sum_four(own_part, got)
    low = line.astype(BF16)
    got = {k: from_x(low[k], -k) for k in (2, 1, 3)}
    got, dq_other = beside(got, dq_other)
    grad_kv = sum_four(line[0], got).astype(BF16)
    grad_projected, gain_heads = heads_back(
        projected, dq_own, dq_other, grad_kv, cosine, sine, gain_rows
    )
    parts_u, parts_v = qkv_out_grad(blocks, across, grad_projected, out_parts)
    got_u, got_v = send(parts_u, from_y), send(parts_v, from_x)

    (gate_up_step, down_step), later_squares = take_step(
        [grads],
        [(weight_gate_up, first_gate_up, second_gate_up), (weight_down, first_down, second_down)],
        ((0, 0, 1024, False, 2), (0, 2048, 1024, True, 3)),
    )
    grad_projected, _ = beside(grad_projected, (parts_u, parts_v))
    near, far, gain_attn = attn_back(grad_projected, full_qkv, x_rows)
    near = near + from_core(far).astype(F32)
    (got_u, got_v), (near, later_squares, block_out) = beside(
        (got_u, got_v), (near, later_squares, block_out)
    )
    late_grad = jnp.concatenate(
        [scatter_rest(parts_u[0], got_u, from_x), scatter_rest(parts_v[0], got_v, from_y)]
    )
    (qkv_step, out_step), qkv_squares = take_step(
        [late_grad],
        [(weight_qkv, first_qkv, second_qkv), (weight_out, first_out, second_out)],
        ((0, 0, 384, False, 0), (0, 384, 256, True, 1)),
    )
    squares = jnp.concatenate(
        [
            gain_heads[0:1],
            gain_heads[1:2],
            weight_squares[:4].reshape(1, 512),
            (later_squares + qkv_squares)[:4].reshape(1, 512),
            jnp.zeros((1, D - 1280), F32),
        ],
        axis=1,
    )
    sums = jnp.concatenate([gain_attn, gain_ffn[None], squares, jnp.zeros((1, D), F32)])
    near, _ = beside(near, sums)
    grad_attn_in = scatter_ring(near)
    scale_one = inverse_rms(own_tokens)
    normed_one = own_tokens * scale_one
    input_grad = (
        grad_hidden + norm_back(grad_attn_in, normed_one, scale_one, norm_gains[0])
    ).astype(BF16)
    input_grad = lax.all_gather(input_grad, "tensor", axis=0, tiled=True)

    sums = sum_all(sums)
    steps = (qkv_step, out_step, gate_up_step, down_step)
    done = finish(
        sums,
        (weight_qkv, weight_out, weight_gate_up, weight_down),
        [step[2] for step in steps],
        (norm_gains, first_norm, second_norm),
        (head_gains, first_head, second_head),
    )
    return (
        block_out,
        input_grad,
        *done[:4],
        done[4],
        done[7],
        *[step[0] for step in steps],
        done[5],
        done[8],
        *[step[1] for step in steps],
        done[6],
        done[9],
        done[10],
    )


def solution(mesh):
    matrix_specs = (P("dp", "tensor"), P("tensor", "dp"), P(None, "dp", "tensor"), P("tensor", "dp"), P(), P())
    in_specs = (P("dp", None), P("dp"), *matrix_specs, *matrix_specs, *matrix_specs, P("dp", None))
    out_specs = (P("dp", None), P("dp", None), *matrix_specs, *matrix_specs, *matrix_specs, P())
    return jax.shard_map(local, mesh=mesh, in_specs=in_specs, out_specs=out_specs, check_vma=False)
```

```python
import functools

import jax
import jax.numpy as jnp
from jax import lax
from jax.experimental import pallas as pl
from jax.experimental.pallas import tpu as pltpu
from jax.sharding import PartitionSpec as P

H = 32
KVH = 8
HD = 64
STEP = 5
D = 2048
ROWS = 512
QPK = 4
CH = 64
FLAT_GRAD = 2048 + 1024

EPS_NORM = 1e-05
ROPE_BASE = 1000000.0
BETA_ONE = 0.5
BETA_TWO = 0.5
EPS_ADAM = 1e-06
DECAY = 0.01
RATE = 0.5
F32 = jnp.float32
BF16 = jnp.bfloat16
OFF = -1e5
VMEM_LIMIT = 50 * 1024 * 1024


def inverse_rms(array_in):
    return lax.rsqrt(jnp.mean(array_in * array_in, axis=-1, keepdims=True) + EPS_NORM)


def adapt(weight, first_old, second_old, grad_in):
    first_new = BETA_ONE * first_old + (1.0 - BETA_ONE) * grad_in
    second_new = BETA_TWO * second_old + (1.0 - BETA_TWO) * grad_in * grad_in
    direction = (
        first_new
        / (1.0 - BETA_ONE**STEP)
        / (jnp.sqrt(second_new / (1.0 - BETA_TWO**STEP)) + EPS_ADAM)
        + DECAY * weight
    )
    return (first_new, second_new, direction)


def perm_x(k):
    return [(i, (i // 4) * 4 + (i % 4 - k) % 4) for i in range(16)]


def perm_y(k):
    return [(i, ((i // 4 - k) % 4) * 4 + i % 4) for i in range(16)]


def perm_z(k):
    return [(i, ((i // 2 - k) % 4) * 2 + i % 2) for i in range(8)]


PERM_CORE = [(i, i ^ 1) for i in range(8)]
PERM_PARTNER = [(i, 15 - i) for i in range(16)]


def from_x(a, k):
    return lax.ppermute(a, "dp", perm_x(k))


def from_y(a, k):
    return lax.ppermute(a, "dp", perm_y(k))


def from_z(a, k):
    return lax.ppermute(a, "tensor", perm_z(k))


def from_core(a):
    return lax.ppermute(a, "tensor", PERM_CORE)


def from_partner(a):
    return lax.ppermute(a, "dp", PERM_PARTNER)


def beside(arrays, work):
    return lax.optimization_barrier((arrays, work))


def gather_both(u, v):
    row = {k: from_x(u, k) for k in (2, 1, 3)}
    column = {k: from_y(v, k) for k in (2, 1, 3)}
    row = jnp.stack([u, row[1], row[2], row[3]])
    column = jnp.stack([v, column[1], column[2], column[3]])
    second = {k: (from_y(row, k), from_x(column, k)) for k in (2, 1, 3)}
    first = [row] + [second[k][0] for k in (1, 2, 3)]
    return first, [column] + [second[k][1] for k in (1, 2, 3)]


def gather_dp(a, later):
    row = {k: from_x(a, k) for k in (2, 1, 3)}
    row, later = beside(row, later)
    row = jnp.stack([a, row[1], row[2], row[3]])
    second = {k: from_y(row, k) for k in (2, 1, 3)}
    return [row] + [second[k] for k in (1, 2, 3)], later


def sum_four(own, got):
    return (own.astype(F32) + got[2].astype(F32)) + (got[1].astype(F32) + got[3].astype(F32))


def send(parts, step):
    return {k: step(parts[k], -k) for k in (2, 1, 3)}


def scatter_rest(own, got, step):
    line = sum_four(own, got)
    low = line.astype(BF16)
    return sum_four(line[0], {k: step(low[k], -k) for k in (2, 1, 3)})


def scatter_tensor(near, far, work=None):
    near = near.astype(F32) + from_core(far.astype(BF16)).astype(F32)
    parts = near.reshape(4, CH, near.shape[-1])
    low = parts.astype(BF16)
    got = {k: from_z(low[k], -k) for k in (2, 1, 3)}
    if work is None:
        return sum_four(parts[0], got)
    got, work = beside(got, work)
    return sum_four(parts[0], got), work


def gather_tensor(a, work=None):
    got = {k: from_z(a, k) for k in (2, 1, 3)}
    if work is not None:
        got, work = beside(got, work)
    near = jnp.concatenate([a, got[1], got[2], got[3]], axis=0)
    halves = (near, from_core(near))
    return halves if work is None else (halves, work)


def sum_all(a):
    for step in (from_x, from_y, from_z):
        a = (a + step(a, 2)) + (step(a, 1) + step(a, 3))
    return a + from_core(a)


def params(vmem=VMEM_LIMIT):
    return pltpu.CompilerParams(vmem_limit_bytes=vmem)


def takes(us):
    return pl.CostEstimate(flops=int(us * 1.1e9), bytes_accessed=0, transcendentals=0)


def whole_specs(arrays):
    return [pl.BlockSpec(a.shape, lambda i, n=len(a.shape): (0,) * n) for a in arrays]


def prepare_kernel(row_ref, tok_ref, gain_ref, in_ref):
    x = tok_ref[...].astype(F32)
    in_ref[...] = (x * inverse_rms(x) * gain_ref[...]).astype(BF16)


def prepare(row_table, tokens, gain):
    return pl.pallas_call(
        prepare_kernel,
        grid_spec=pltpu.PrefetchScalarGridSpec(
            num_scalar_prefetch=1,
            grid=(8,),
            in_specs=[
                pl.BlockSpec((CH, D), lambda i, r: (r[i], 0)),
                pl.BlockSpec((1, D), lambda i, r: (0, 0)),
            ],
            out_specs=pl.BlockSpec((CH, D), lambda i, r: (i, 0)),
        ),
        out_shape=jax.ShapeDtypeStruct((ROWS, D), BF16),
        compiler_params=params(),
        name="prepare",
        cost_estimate=takes(4),
    )(row_table, tokens, gain)


def arrange_kernel(row_ref, tok_ref, cot_ref, in_ref, across_ref, x_ref, dy_ref):
    x_ref[...] = tok_ref[...]
    dy_ref[...] = cot_ref[...]

    @pl.when(pl.program_id(0) % 2 == 0)
    def _():
        across_ref[...] = in_ref[...].astype(F32).T.astype(BF16)


def arrange(row_table, tokens, cotangent, attn_in):
    pick = pl.BlockSpec((CH, D), lambda i, r: (r[i], 0))
    put = pl.BlockSpec((CH, D), lambda i, r: (i, 0))
    return pl.pallas_call(
        arrange_kernel,
        grid_spec=pltpu.PrefetchScalarGridSpec(
            num_scalar_prefetch=1,
            grid=(8,),
            in_specs=[pick, pick, pl.BlockSpec((128, D), lambda i, r: (i // 2, 0))],
            out_specs=[pl.BlockSpec((D, 128), lambda i, r: (0, i // 2)), put, put],
        ),
        out_shape=[
            jax.ShapeDtypeStruct((D, ROWS), BF16),
            jax.ShapeDtypeStruct((ROWS, D), BF16),
            jax.ShapeDtypeStruct((ROWS, D), BF16),
        ],
        compiler_params=params(),
        name="arrange",
        cost_estimate=takes(7),
    )(row_table, tokens, cotangent, attn_in)


def lane_of(shape):
    return lax.broadcasted_iota(jnp.int32, shape, len(shape) - 1)


def head_sums(a, low_half):
    left = jnp.sum(jnp.where(low_half, a, 0.0), axis=-1, keepdims=True)
    right = jnp.sum(jnp.where(low_half, 0.0, a), axis=-1, keepdims=True)
    return jnp.where(low_half, left, right)


def turn(a, first):
    return jnp.where(first, pltpu.roll(a, 96, 1), pltpu.roll(a, 32, 1))


def vmem_specs(count):
    return [pl.BlockSpec(memory_space=pltpu.VMEM)] * count


def shape(dims, kind):
    return jax.ShapeDtypeStruct(dims, kind)


def column_squares(a):
    total = None
    for at in range(0, a.shape[-1], 128):
        part = a[:, at : at + 128]
        part = jnp.sum(part * part, axis=0, keepdims=True)
        total = part if total is None else total + part
    return total


def eight_rows(rows):
    row = lax.broadcasted_iota(jnp.int32, (8, 128), 0)
    out = jnp.zeros((8, 128), F32)
    for index, value in enumerate(rows):
        if value is not None:
            out = jnp.where(row == index, value, out)
    return out


def pack_kernel(qkv_in, out_in, gate_up_in, down_in, first_ref, second_ref, squares_ref, qkv, out_w, gate_up, down, sems):
    pairs = ((down_in, down), (out_in, out_w), (gate_up_in, gate_up), (qkv_in, qkv))
    copies = [pltpu.make_async_copy(a, b, sems.at[i]) for i, (a, b) in enumerate(pairs)]
    for copy in copies:
        copy.start()
    copies[0].wait()
    first_ref[:, :1024] = down[...].T.astype(BF16)
    copies[1].wait()
    first_ref[:, 1024:] = out_w[...].T.astype(BF16)
    copies[2].wait()
    second_ref[:, :1024] = gate_up[0].astype(BF16)
    second_ref[:, 1024:] = gate_up[1].astype(BF16)
    copies[3].wait()
    squares_ref[...] = eight_rows(
        [
            column_squares(qkv[...]),
            column_squares(out_w[...]),
            column_squares(gate_up[0]) + column_squares(gate_up[1]),
            column_squares(down[...]),
        ]
    )


def pack(weight_qkv, weight_out, weight_gate_up, weight_down):
    given = (weight_qkv, weight_out, weight_gate_up, weight_down)
    return pl.pallas_call(
        pack_kernel,
        in_specs=[pl.BlockSpec(memory_space=pl.ANY)] * 4,
        out_specs=vmem_specs(3),
        out_shape=[shape((128, 1280), BF16), shape((128, 2048), BF16), shape((8, 128), F32)],
        scratch_shapes=[pltpu.VMEM(a.shape, F32) for a in given] + [pltpu.SemaphoreType.DMA((4,))],
        compiler_params=params(),
        name="pack",
        cost_estimate=takes(2),
    )(*given)


def project_kernel(
    blk_ref, x_ref, u0, u1, u2, u3, v0, v1, v2, v3, cos_ref, sin_ref, gain_ref,
    proj_ref, q_own_ref, q_send_ref, kv_ref, w_ref, seg_ref,
):
    @pl.when(pl.program_id(0) == 0)
    def _():
        for at_y in range(4):
            for at_x in range(4):
                slot = at_y * 4 + at_x
                start = pl.multiple_of(blk_ref[slot] * 128, 128)
                w_ref[pl.ds(start, 64), :] = (u0, u1, u2, u3)[at_y][at_x, :64, :]
                w_ref[pl.ds(start + 64, 64), :] = (v0, v1, v2, v3)[at_x][at_y]
                seg_ref[slot] = (u0, u1, u2, u3)[at_y][at_x, 64:, :]

    acc = jnp.dot(x_ref[...], w_ref[...], preferred_element_type=F32)
    proj_ref[...] = acc
    lane = lane_of((x_ref.shape[0], 128))
    low_half = lane < 64
    first = (lane & 63) < 32
    cosine = cos_ref[...]
    sine = jnp.where(first, -sin_ref[...], sin_ref[...])
    for pair in range(3):
        u = acc[:, pair * 128 : (pair + 1) * 128]
        scale = lax.rsqrt(head_sums(u * u, low_half) * (1.0 / HD) + EPS_NORM)
        hat = u * scale * gain_ref[pair // 2 : pair // 2 + 1, :]
        turned = hat * cosine + turn(hat, first) * sine
        if pair < 2:
            across = (turned.astype(BF16).astype(F32) * 0.125).T.astype(BF16)
            out = (q_own_ref, q_send_ref)[pair]
            out[0] = across[:64]
            out[1] = across[64:]
        else:
            kv_ref[...] = jnp.where(low_half, turned, u).astype(BF16)


def project(blocks, x, w_first, w_second, cosine, sine, gains):
    tile = 128
    whole = lambda dims: pl.BlockSpec(dims, lambda i, b: (0,) * len(dims))
    row = lambda width: pl.BlockSpec((tile, width), lambda i, b: (i, 0))
    pair = pl.BlockSpec((2, HD, tile), lambda i, b: (0, 0, i))
    return pl.pallas_call(
        project_kernel,
        grid_spec=pltpu.PrefetchScalarGridSpec(
            num_scalar_prefetch=1,
            grid=(ROWS // tile,),
            in_specs=[row(D)]
            + [whole((4, 80, 384))] * 4
            + [whole((4, 64, 384))] * 4
            + [row(128), row(128), whole((8, 128))],
            out_specs=[row(384), pair, pair, row(128), whole((D, 384)), whole((16, 16, 384))],
        ),
        out_shape=[
            shape((ROWS, 384), F32),
            shape((2, HD, ROWS), BF16),
            shape((2, HD, ROWS), BF16),
            shape((ROWS, 128), BF16),
            shape((D, 384), BF16),
            shape((16, 16, 384), BF16),
        ],
        compiler_params=params(),
        name="project",
        cost_estimate=takes(6),
    )(blocks, x, *w_first, *w_second, cosine, sine, gains)


def lane_masks():
    low = (lane_of((1, 128)) < 64).astype(F32)
    return low.astype(BF16), (1.0 - low).astype(BF16)


def allowed_keys(queries, is_own, at, count, kinfo_ref, qinfo_ref):
    info = kinfo_ref[pl.ds(at, count), :]
    seg = jnp.where(is_own, info[:, queries : queries + 1], info[:, 2:3])
    pos = jnp.where(is_own, info[:, 3:4], -1)
    return (seg == qinfo_ref[queries : queries + 1, :]) & (pos <= qinfo_ref[2:3, :])


def for_queries(blk_ref, slot, own_at, sets, work):
    block = blk_ref[slot]
    for queries in range(sets):
        own = blk_ref[own_at + queries]

        @pl.when((block == 0) | (block == own))
        def _(queries=queries, own=own):
            work(queries, True, block == own)

        @pl.when((block > 0) & (block < own))
        def _(queries=queries):
            work(queries, False, None)


def forward_kernel(
    blk_ref, q_first, q_second, kv0, kv1, kv2, kv3, kinfo_ref, qinfo_ref, bias_ref,
    mixed_ref, out_ref, lse_ref, send_ref, kv_all, q_t, acc,
):
    for group, ref in enumerate((kv0, kv1, kv2, kv3)):
        kv_all[group * 4 : (group + 1) * 4] = ref[...]
    acc[...] = jnp.zeros_like(acc)
    row = lax.broadcasted_iota(jnp.int32, (64, ROWS), 0)
    bias = jnp.where(row == 0, bias_ref[0:1, :], 0.0).astype(BF16)
    for head in range(QPK):
        q_t[head, :64, :] = (q_first, q_second)[head // 2][head % 2]
        q_t[head, 64:, :] = bias
    keep_k, keep_v = lane_masks()

    def step(slot, carry):
        def work(queries, masked, is_own):
            kv = kv_all[slot]
            keys = kv * keep_k + (keep_v if not masked else jnp.zeros_like(keep_v))
            vals = (kv * keep_v + keep_k).astype(F32).T.astype(BF16)[56:]
            if masked:
                allowed = allowed_keys(queries, is_own, 0, ROWS, kinfo_ref, qinfo_ref)
            for head in range(QPK):
                scores = jnp.dot(keys, q_t[head], preferred_element_type=F32)
                probs = jnp.exp(scores)
                if masked:
                    probs = jnp.where(allowed, probs, 0.0)
                acc[head] += jnp.dot(vals, probs.astype(BF16), preferred_element_type=F32)

        for_queries(blk_ref, slot, 16, 1, work)
        return carry

    lax.fori_loop(0, 16, step, 0)
    heads = []
    logs = []
    for head in range(QPK):
        total = acc[head, 0:1, :]
        heads.append(acc[head, 8:, :] / total)
        logs.append(jnp.log(total))
    mixed_ref[...] = jnp.concatenate(heads, axis=0).T.astype(BF16)
    rest = jnp.zeros((6, ROWS), F32)
    out_ref[:64], out_ref[64:] = heads[0], heads[1]
    lse_ref[...] = jnp.concatenate(logs[:2] + [rest], axis=0)
    send_ref[:64], send_ref[64:128] = heads[2], heads[3]
    send_ref[128:] = jnp.concatenate(logs[2:] + [rest], axis=0)


def attend(blocks, q_first, q_second, kv, kinfo, qinfo, bias):
    return pl.pallas_call(
        forward_kernel,
        in_specs=[pl.BlockSpec(memory_space=pltpu.SMEM)] + vmem_specs(9),
        out_specs=vmem_specs(5),
        out_shape=[
            shape((ROWS, 256), BF16),
            shape((128, ROWS), F32),
            shape((8, ROWS), F32),
            shape((136, ROWS), F32),
            shape((16, ROWS, 128), BF16),
        ],
        scratch_shapes=[
            pltpu.VMEM((QPK, 128, ROWS), BF16),
            pltpu.VMEM((QPK, 72, ROWS), F32),
        ],
        compiler_params=params(),
        name="attend",
        cost_estimate=takes(20),
    )(blocks, q_first, q_second, *kv, kinfo, qinfo, bias)


def three_rows(row, value, at):
    high = value.astype(BF16).astype(F32)
    rest = value - high
    middle = rest.astype(BF16).astype(F32)
    low = rest - middle
    return (
        jnp.where(row == at, high, 0.0)
        + jnp.where(row == at + 1, middle, 0.0)
        + jnp.where(row == at + 2, low, 0.0)
    )


def mixed_grad_kernel(near_ref, far_ref, w_ref, own_ref, send_ref):
    w = w_ref[...]
    for half, ref in enumerate((near_ref, far_ref)):
        part = jnp.dot(ref[...], w, preferred_element_type=F32).astype(BF16)
        own_ref[half * 256 : (half + 1) * 256] = part[:, :128]
        send_ref[half * 256 : (half + 1) * 256] = part[:, 128:]


def mixed_grad(near, far, down_out):
    whole = lambda dims: pl.BlockSpec(dims, lambda i: (0, 0))
    return pl.pallas_call(
        mixed_grad_kernel,
        grid=(1,),
        in_specs=[whole((256, D)), whole((256, D)), pl.BlockSpec((D, 256), lambda i: (0, 4))],
        out_specs=[whole((ROWS, 128))] * 2,
        out_shape=[shape((ROWS, 128), BF16)] * 2,
        compiler_params=params(),
        name="mixed_grad",
        cost_estimate=takes(2),
    )(near, far, down_out)


def ready_kernel(do_own, do_other, out_own, lse_own, out_other, q_own, q_other, bias_ref, q_t, do_t, q_pad, do_pad):
    row = lax.broadcasted_iota(jnp.int32, (64, ROWS), 0)
    low_half = lane_of((ROWS, 128)) < 64
    for queries in range(2):
        do = (do_own, do_other)[queries][...].astype(F32)
        q_ref = (q_own, q_other)[queries]
        q = jnp.concatenate([q_ref[0].astype(F32), q_ref[1].astype(F32)], axis=0).T
        do_turned = do.T
        dots = do_turned * (out_own, out_other)[queries][:128, :]
        for part in range(2):
            head = 2 * queries + part
            at = slice(part * 64, (part + 1) * 64)
            delta = jnp.sum(dots[at, :], axis=0, keepdims=True)
            lse = (out_other[128 + part : 129 + part, :] if queries else lse_own[part : part + 1, :])
            extra = three_rows(row, -lse, 0)
            extra = extra + jnp.where(row == 3, bias_ref[queries : queries + 1, :], 0.0)
            q_t[head, :64, :] = q_ref[part]
            q_t[head, 64:, :] = extra.astype(BF16)
            do_t[head, :64, :] = three_rows(row, -delta, 0).astype(BF16)
            do_t[head, 64:, :] = do_turned[at, :].astype(BF16)
            q_head = pltpu.roll(q, 64, 1) if part else q
            do_head = do if part else pltpu.roll(do, 64, 1)
            q_pad[head] = jnp.where(low_half, q_head, 0.0).astype(BF16)
            do_pad[head] = jnp.where(low_half, 0.0, do_head).astype(BF16)


def ready(*given):
    return pl.pallas_call(
        ready_kernel,
        in_specs=vmem_specs(len(given)),
        out_specs=vmem_specs(4),
        out_shape=[shape((QPK, 128, ROWS), BF16)] * 2 + [shape((QPK, ROWS, 128), BF16)] * 2,
        compiler_params=params(),
        name="ready",
        cost_estimate=takes(2.5),
    )(*given)


def backward_kernel(
    blk_ref, q_t, do_t, q_pad, do_pad, kv_all, kinfo_ref, qinfo_ref, own_ref, other_ref, u_ref, v_ref, dq_t, total
):
    dq_t[...] = jnp.zeros_like(dq_t)
    keep_k, keep_v = lane_masks()
    keep_v_masked = jnp.where(lane_of((1, 128)) == 67, 0.0, keep_v.astype(F32)).astype(BF16)

    def step(slot, carry):
        total[...] = jnp.zeros_like(total)

        def work(queries, masked, is_own):
            kv = kv_all[slot]
            keys = kv * keep_k + (keep_v_masked if masked else keep_v)
            vals = kv * keep_v + keep_k
            keys_turned = kv.astype(F32).T[:64, :].astype(BF16)
            if masked:
                allowed = allowed_keys(queries, is_own, 0, ROWS, kinfo_ref, qinfo_ref)
            for head in (2 * queries, 2 * queries + 1):
                scores = jnp.dot(keys, q_t[head], preferred_element_type=F32)
                probs = jnp.exp(scores)
                if masked:
                    probs = jnp.where(allowed, probs, 0.0)
                grads = jnp.dot(vals, do_t[head], preferred_element_type=F32)
                grads = (probs * grads).astype(BF16)
                term = jnp.dot(probs.astype(BF16), do_pad[head], preferred_element_type=F32)
                total[...] += term + jnp.dot(grads, q_pad[head], preferred_element_type=F32)
                dq_t[head * 64 : (head + 1) * 64, :] += jnp.dot(
                    keys_turned, grads, preferred_element_type=F32
                )

        for_queries(blk_ref, slot, 16, 2, work)
        u_ref[slot // 4, slot % 4] = total[:256].astype(BF16)
        v_ref[slot % 4, slot // 4] = total[256:].astype(BF16)
        return carry

    lax.fori_loop(0, 16, step, 0)
    dq = (dq_t[...].T * 0.125).astype(BF16)
    own_ref[...] = dq[:, :128]
    other_ref[...] = dq[:, 128:]


def attend_back(blocks, operands, kv, kinfo, qinfo):
    pair = shape((ROWS, 128), BF16)
    half = shape((4, 4, 256, 128), BF16)
    return pl.pallas_call(
        backward_kernel,
        in_specs=[pl.BlockSpec(memory_space=pltpu.SMEM)] + vmem_specs(7),
        out_specs=vmem_specs(4),
        out_shape=[pair, pair, half, half],
        scratch_shapes=[pltpu.VMEM((256, ROWS), F32), pltpu.VMEM((ROWS, 128), F32)],
        compiler_params=params(),
        name="attend_back",
        cost_estimate=takes(36),
    )(blocks, *operands, kv, kinfo, qinfo)


def heads_back_kernel(pairs, proj_ref, *refs):
    grads = refs[: len(pairs)]
    cos_ref, sin_ref, gain_ref, out_ref, sum_ref = refs[len(pairs) :]
    lane = lane_of((proj_ref.shape[0], 128))
    low_half = lane < 64
    first = (lane & 63) < 32
    cosine = cos_ref[...]
    sine = jnp.where(first, sin_ref[...], -sin_ref[...])
    sums = None
    for index, pair in enumerate(pairs):
        u = proj_ref[:, pair * 128 : (pair + 1) * 128]
        grad = grads[index][...].astype(F32)
        scale = lax.rsqrt(head_sums(u * u, low_half) * (1.0 / HD) + EPS_NORM)
        hat = u * scale
        turned = grad * cosine + turn(grad, first) * sine
        part = jnp.sum(turned * hat, axis=0, keepdims=True)
        sums = part if sums is None else sums + part
        grad_hat = turned * gain_ref[pair // 2 : pair // 2 + 1, :]
        mean = head_sums(grad_hat * hat, low_half) * (1.0 / HD)
        back = scale * (grad_hat - hat * mean)
        if pair == 2:
            back = jnp.where(low_half, back, grad)
        out_ref[:, index * 128 : (index + 1) * 128] = back.astype(BF16)

    @pl.when(pl.program_id(0) == 0)
    def _():
        sum_ref[...] = jnp.zeros_like(sum_ref)

    sum_ref[0:1, :] += sums


def heads_back(pairs, proj, grads, cosine, sine, gains):
    tile = 128
    row = lambda width: pl.BlockSpec((tile, width), lambda i: (i, 0))
    whole = pl.BlockSpec((8, 128), lambda i: (0, 0))
    wide = 128 * len(pairs)
    return pl.pallas_call(
        functools.partial(heads_back_kernel, pairs),
        grid=(ROWS // tile,),
        in_specs=[row(384)] + [row(128)] * (len(pairs) + 2) + [whole],
        out_specs=[row(wide), whole],
        out_shape=[shape((ROWS, wide), BF16), shape((8, 128), F32)],
        compiler_params=params(),
        name="heads_back",
        cost_estimate=takes(len(pairs)),
    )(proj, *grads, cosine, sine, gains)


def out_kernel(mixed_ref, w_ref, out_ref):
    out_ref[...] = dot_cols(mixed_ref[...], w_ref[...]).astype(out_ref.dtype)


def out_project(half, mixed, down_out, kind):
    return pl.pallas_call(
        out_kernel,
        grid=(1,),
        in_specs=[
            pl.BlockSpec((256, 256), lambda i: (half, 0)),
            pl.BlockSpec((D, 256), lambda i: (0, 4)),
        ],
        out_specs=pl.BlockSpec((256, D), lambda i: (0, 0)),
        out_shape=shape((256, D), kind),
        compiler_params=params(),
        name="out_project",
        cost_estimate=takes(1.8),
    )(mixed, down_out)


def ffn_kernel(
    near_ref, far_ref, grad_ref, w_in, act_ref, gate_ref, up_ref, near_out, far_out, w, x_all, both, sems
):
    tiles = []
    for tile in range(4):
        at = (slice(tile * 256, (tile + 1) * 256), slice(1024 + tile * 256, 1024 + (tile + 1) * 256))
        pair = [
            pltpu.make_async_copy(w_in.at[:, part], w.at[:, part], sems.at[2 * tile + i])
            for i, part in enumerate(at)
        ]
        for copy in pair:
            copy.start()
        tiles.append((at, pair))
    x_all[:256] = near_ref[...]
    x_all[256:] = far_ref[...]
    for (gate_at, up_at), pair in tiles:
        for copy in pair:
            copy.wait()
        x = x_all[...]
        gate = jnp.dot(x, w[:, gate_at], preferred_element_type=F32)
        up = jnp.dot(x, w[:, up_at], preferred_element_type=F32)
        inner = grad_ref[:, gate_at]
        sigmoid = jax.nn.sigmoid(gate)
        activated = gate * sigmoid
        act_ref[:, gate_at] = (activated * up).astype(BF16)
        grad_gate = (inner * up * sigmoid * (1.0 + gate * (1.0 - sigmoid))).astype(BF16)
        grad_up = (inner * activated).astype(BF16)
        gate_ref[:, gate_at] = grad_gate
        up_ref[:, gate_at] = grad_up
        both[:, gate_at] = grad_gate
        both[:, up_at] = grad_up
    for tile in range(4):
        at = slice(tile * 512, (tile + 1) * 512)
        part = dot_cols(both[...], w[at, :])
        near_out[:, at] = part[:256]
        far_out[:, at] = part[256:].astype(BF16)


def feed_forward(near, far, grad_inner, gate_up):
    return pl.pallas_call(
        ffn_kernel,
        in_specs=vmem_specs(3) + [pl.BlockSpec(memory_space=pl.ANY)],
        out_specs=vmem_specs(5),
        out_shape=[shape((ROWS, 1024), BF16)] * 3 + [shape((256, D), F32), shape((256, D), BF16)],
        scratch_shapes=[
            pltpu.VMEM((D, 2048), BF16),
            pltpu.VMEM((ROWS, D), BF16),
            pltpu.VMEM((ROWS, 2048), BF16),
            pltpu.SemaphoreType.DMA((8,)),
        ],
        compiler_params=params(),
        name="feed_forward",
        cost_estimate=takes(13),
    )(near, far, grad_inner, gate_up)


def inner_grad_kernel(dy_ref, w_ref, out_ref):
    out_ref[...] = jnp.dot(dy_ref[...], w_ref[...], preferred_element_type=F32)


def inner_grad(dy, down_out):
    return pl.pallas_call(
        inner_grad_kernel,
        grid=(4,),
        in_specs=[
            pl.BlockSpec((ROWS, D), lambda j: (0, 0)),
            pl.BlockSpec((D, 256), lambda j: (0, j)),
        ],
        out_specs=pl.BlockSpec((ROWS, 256), lambda j: (0, j)),
        out_shape=shape((ROWS, 1024), F32),
        compiler_params=params(),
        name="inner_grad",
        cost_estimate=takes(5.5),
    )(dy, down_out)


def ffn_out_kernel(act_ref, w_ref, near_ref, far_ref, acc):
    step = pl.program_id(0)
    term = dot_cols(act_ref[...], w_ref[...])

    @pl.when(step == 0)
    def _():
        acc[...] = term

    @pl.when(step > 0)
    def _():
        acc[...] += term

    @pl.when(step == pl.num_programs(0) - 1)
    def _():
        near_ref[...] = acc[:256]
        far_ref[...] = acc[256:].astype(BF16)


def ffn_out(act, down_out):
    whole = lambda dims: pl.BlockSpec(dims, lambda j: (0, 0))
    return pl.pallas_call(
        ffn_out_kernel,
        grid=(4,),
        in_specs=[
            pl.BlockSpec((ROWS, 256), lambda j: (0, j)),
            pl.BlockSpec((D, 256), lambda j: (0, j)),
        ],
        out_specs=[whole((256, D)), whole((256, D))],
        out_shape=[shape((256, D), F32), shape((256, D), BF16)],
        scratch_shapes=[pltpu.VMEM((ROWS, D), F32)],
        compiler_params=params(),
        name="ffn_out",
        cost_estimate=takes(6.5),
    )(act, down_out)


def out_grad_kernel(blk_ref, near_ref, far_ref, mixed_ref, out_ref, turned):
    turned[:, :256] = near_ref[...].astype(F32).T.astype(BF16)
    turned[:, 256:] = far_ref[...].astype(F32).T.astype(BF16)
    mixed = mixed_ref[...]
    for slot in range(16):
        at = pl.ds(pl.multiple_of(blk_ref[slot] * 128, 128), 128)
        out = jnp.dot(turned[at, :], mixed, preferred_element_type=F32)
        out_ref[slot // 4, slot % 4] = out.astype(BF16)


def out_grad(blocks, near, far, mixed):
    return pl.pallas_call(
        out_grad_kernel,
        in_specs=[pl.BlockSpec(memory_space=pltpu.SMEM)] + vmem_specs(3),
        out_specs=vmem_specs(1)[0],
        out_shape=shape((4, 4, 128, 256), BF16),
        scratch_shapes=[pltpu.VMEM((D, ROWS), BF16)],
        compiler_params=params(),
        name="out_grad",
        cost_estimate=takes(2),
    )(blocks, near, far, mixed)


def query_out_grad_kernel(blk_ref, across_ref, grad_ref, parts_ref, out_ref):
    grad = grad_ref[...]
    for slot in range(16):
        at = pl.ds(pl.multiple_of(blk_ref[slot] * 128, 128), 128)
        part = jnp.dot(across_ref[at, :], grad, preferred_element_type=F32)
        out_ref[slot // 4, slot % 4, :, :256] = part.astype(BF16)
        out_ref[slot // 4, slot % 4, :, 256:] = parts_ref[slot // 4, slot % 4]


def query_out_grad(blocks, across, grad, out_parts):
    return pl.pallas_call(
        query_out_grad_kernel,
        in_specs=[pl.BlockSpec(memory_space=pltpu.SMEM)] + vmem_specs(3),
        out_specs=vmem_specs(1)[0],
        out_shape=shape((4, 4, 128, 512), BF16),
        compiler_params=params(),
        name="query_out_grad",
        cost_estimate=takes(2),
    )(blocks, across, grad, out_parts)


def key_grad_kernel(blk_ref, across_ref, grad_ref, parts_ref, u_ref, v_ref):
    grad = grad_ref[...]
    for slot in range(16):
        at_y, at_x = slot // 4, slot % 4
        at = pl.ds(pl.multiple_of(blk_ref[slot] * 128, 128), 128)
        part = jnp.dot(across_ref[at, :], grad, preferred_element_type=F32).astype(BF16)
        u_ref[at_y, at_x, :, :512] = parts_ref[at_y, at_x, :64]
        u_ref[at_y, at_x, :, 512:] = part[:64]
        v_ref[at_x, at_y, :, :512] = parts_ref[at_y, at_x, 64:]
        v_ref[at_x, at_y, :, 512:] = part[64:]


def key_grad(blocks, across, grad, parts):
    return pl.pallas_call(
        key_grad_kernel,
        in_specs=[pl.BlockSpec(memory_space=pltpu.SMEM)] + vmem_specs(3),
        out_specs=vmem_specs(2),
        out_shape=[shape((4, 4, 64, 640), BF16)] * 2,
        compiler_params=params(),
        name="key_grad",
        cost_estimate=takes(2),
    )(blocks, across, grad, parts)


def attn_back_kernel(grad_ref, w_ref, x_ref, part_ref, gain_ref):
    step = pl.program_id(0)
    part = dot_cols(grad_ref[...], w_ref[...])
    part_ref[...] = part.astype(BF16)
    x = x_ref[...].astype(F32)
    sums = jnp.sum(part * (x * inverse_rms(x)), axis=0, keepdims=True)

    @pl.when(step == 0)
    def _():
        gain_ref[...] = sums

    @pl.when(step > 0)
    def _():
        gain_ref[...] += sums


def attn_back(grad, w, x):
    tile = 128
    row = lambda width: pl.BlockSpec((tile, width), lambda i: (i, 0))
    return pl.pallas_call(
        attn_back_kernel,
        grid=(4,),
        in_specs=[row(256), pl.BlockSpec((D, 256), lambda i: (0, 0)), row(D)],
        out_specs=[row(D), pl.BlockSpec((1, D), lambda i: (0, 0))],
        out_shape=[shape((ROWS, D), BF16), shape((1, D), F32)],
        compiler_params=params(),
        name="attn_back",
        cost_estimate=takes(5),
    )(grad, w, x)


def attn_back_rest_kernel(row_ref, grad_ref, w_ref, x_ref, part_ref, out_ref, gain_ref):
    step = pl.program_id(0)
    part = dot_cols(grad_ref[...], w_ref[...])
    x = x_ref[...].astype(F32)
    sums = jnp.sum(part * (x * inverse_rms(x)), axis=0, keepdims=True)
    part = (part + part_ref[...].astype(F32)).astype(BF16)

    @pl.when(step == 0)
    def _():
        gain_ref[...] = sums

    @pl.when(step > 0)
    def _():
        gain_ref[...] += sums

    for half in range(2):
        at = pl.multiple_of(row_ref[2 * step + half] * CH, CH)
        out_ref[pl.ds(at, CH), :] = part[half * CH : (half + 1) * CH]


def attn_back_rest(row_table, grad, w, x, part):
    tile = 128
    row = lambda width: pl.BlockSpec((tile, width), lambda i, r: (i, 0))
    return pl.pallas_call(
        attn_back_rest_kernel,
        grid_spec=pltpu.PrefetchScalarGridSpec(
            num_scalar_prefetch=1,
            grid=(4,),
            in_specs=[row(128), pl.BlockSpec((D, 128), lambda i, r: (0, 2)), row(D), row(D)],
            out_specs=[
                pl.BlockSpec((ROWS, D), lambda i, r: (0, 0)),
                pl.BlockSpec((1, D), lambda i, r: (0, 0)),
            ],
        ),
        out_shape=[shape((ROWS, D), BF16), shape((1, D), F32)],
        compiler_params=params(),
        name="attn_back_rest",
        cost_estimate=takes(4),
    )(row_table, grad, w, x, part)


def weight_grad_kernel(parts, wide, *refs):
    lhs, rhs = refs[:parts], refs[parts : parts + len(wide)]
    out_ref, turned = refs[-2:]
    step = pl.program_id(0)

    @pl.when(step == 0)
    def _():
        rows = ROWS // parts
        for index, ref in enumerate(lhs):
            turned[:, index * rows : (index + 1) * rows] = ref[...].astype(F32).T.astype(BF16)

    start = 0
    for ref, count in zip(rhs, wide, strict=True):

        @pl.when((step >= start) & (step < start + count))
        def _(ref=ref):
            out_ref[...] = jnp.dot(turned[...], ref[...], preferred_element_type=F32).astype(BF16)

        start += count


def weight_grad(lhs, rhs, at, flat=None):
    wide = [a.shape[1] // 256 for a in rhs]
    starts = [sum(wide[:i]) for i in range(len(wide))]
    given = [*lhs, *rhs] + ([] if flat is None else [flat])
    specs = [pl.BlockSpec(a.shape, lambda i: (0, 0)) for a in lhs]
    for start, count in zip(starts, wide, strict=True):
        specs.append(
            pl.BlockSpec(
                (ROWS, 256),
                lambda i, start=start, count=count: (0, jnp.clip(i - start, 0, count - 1)),
            )
        )
    if flat is not None:
        specs.append(pl.BlockSpec(memory_space=pl.ANY))
    return pl.pallas_call(
        functools.partial(weight_grad_kernel, len(lhs), wide),
        grid=(sum(wide),),
        in_specs=specs,
        out_specs=pl.BlockSpec((D, 256), lambda i: (0, at + i)),
        out_shape=shape((D, FLAT_GRAD), BF16),
        scratch_shapes=[pltpu.VMEM((D, ROWS), BF16)],
        input_output_aliases={} if flat is None else {len(given) - 1: 0},
        compiler_params=params(),
        name="weight_grad",
        cost_estimate=takes(1.25 * sum(wide)),
    )(*given)


def keep_kernel(in_ref, out_ref):
    out_ref[...] = in_ref[...]


def keep(a):
    block = pl.BlockSpec((128, D), lambda i: (i, 0))
    return pl.pallas_call(
        keep_kernel,
        grid=(4,),
        in_specs=[block],
        out_specs=block,
        out_shape=shape((ROWS, D), BF16),
        compiler_params=params(),
        name="keep",
        cost_estimate=takes(2),
    )(a)


def step_kernel(wide, *refs):
    count = len(wide)
    squares = []
    for index, (given, start, columns, turned, row) in enumerate(wide):
        weight, first, second = refs[at_of(wide) + 3 * index : at_of(wide) + 3 * index + 3]
        base = at_of(wide) + 3 * count + 3 * index
        first_out, second_out, direction_out = refs[base : base + 3]
        total = None
        for part in range(2 if len(weight.shape) == 3 else 1):
            grad = refs[given][:, start : start + columns].astype(F32)
            start += columns
            if turned:
                grad = grad.T
            pick = (part,) if len(weight.shape) == 3 else (slice(None),)
            first_new, second_new, direction = adapt(weight[pick], first[pick], second[pick], grad)
            first_out[pick] = first_new
            second_out[pick] = second_new
            direction_out[pick] = direction
            sums = column_squares(direction)
            total = sums if total is None else total + sums
        squares.append((row, total))
    refs[-1][...] = eight_rows([dict(squares).get(row) for row in range(8)])


def at_of(wide):
    return 1 + max(entry[0] for entry in wide)


def take_step(grads, matrices, wide):
    given = [*grads, *[a for matrix in matrices for a in matrix]]
    outs = [shape(matrix[0].shape, F32) for matrix in matrices for _ in range(3)]
    out = pl.pallas_call(
        functools.partial(step_kernel, wide),
        grid=(1,),
        in_specs=whole_specs(given),
        out_specs=whole_specs(outs + [shape((8, 128), F32)]),
        out_shape=outs + [shape((8, 128), F32)],
        compiler_params=params(),
        name="take_step",
        cost_estimate=takes(4),
    )(*given)
    return [out[3 * i : 3 * i + 3] for i in range(len(matrices))], out[-1]


def finish_kernel(*refs):
    sums = refs[0]
    weights, directions = refs[1:5], refs[5:9]
    gains = (refs[9:12], refs[12:15])
    outs = refs[15:19]
    gain_outs = (refs[19:22], refs[22:25])
    stats_ref = refs[25]
    row = lax.broadcasted_iota(jnp.int32, (3, 6), 0)
    column = lax.broadcasted_iota(jnp.int32, (3, 6), 1)
    stats = jnp.zeros((3, 6), F32)

    def total(a):
        return jnp.sum(jnp.sum(a, axis=1, keepdims=True), axis=0, keepdims=True)

    def keep(stats, index, weight_norm, step_norm):
        ratio = weight_norm / (step_norm + EPS_ADAM)
        values = jnp.where(row == 0, weight_norm, jnp.where(row == 1, step_norm, ratio))
        return jnp.where(column == index, values, stats), ratio

    for index in range(4):
        weight_norm = jnp.sqrt(total(sums[2:3, 256 + index * 128 : 384 + index * 128]))
        step_norm = jnp.sqrt(total(sums[2:3, 768 + index * 128 : 896 + index * 128]))
        stats, ratio = keep(stats, index, weight_norm, step_norm)
        weight, direction, out = weights[index], directions[index], outs[index]
        if len(weight.shape) == 3:
            for part in range(2):
                out[part] = weight[part] - RATE * ratio * direction[part]
        else:
            out[...] = weight[...] - RATE * ratio * direction[...]
    query_gain = sums[2:3, 0:64] + sums[2:3, 64:128]
    head_grad = jnp.concatenate([query_gain, sums[2:3, 128:192]], axis=0)
    for index, grad in enumerate((sums[0:2, :], head_grad)):
        weight, first, second = (ref[...] for ref in gains[index])
        first_new, second_new, direction = adapt(weight, first, second, grad)
        weight_norm = jnp.sqrt(total(weight * weight))
        step_norm = jnp.sqrt(total(direction * direction))
        stats, ratio = keep(stats, 4 + index, weight_norm, step_norm)
        new_out, first_out, second_out = gain_outs[index]
        new_out[...] = weight - RATE * ratio * direction
        first_out[...] = first_new
        second_out[...] = second_new
    stats_ref[...] = stats


def finish(sums, weights, directions, norm_set, head_set):
    outs = [shape(w.shape, F32) for w in weights]
    outs += [shape(norm_set[0].shape, F32)] * 3 + [shape(head_set[0].shape, F32)] * 3
    outs += [shape((3, 6), F32)]
    given = (sums, *weights, *directions, *norm_set, *head_set)
    return pl.pallas_call(
        finish_kernel,
        grid=(1,),
        in_specs=whole_specs(given),
        out_specs=whole_specs(outs),
        out_shape=outs,
        compiler_params=params(),
        name="finish",
        cost_estimate=takes(3),
    )(*given)


def norm_back(grad_in, normed, inv_scale, gain):
    grad_hat = grad_in * gain
    return inv_scale * (grad_hat - normed * jnp.mean(grad_hat * normed, axis=-1, keepdims=True))


def dot_cols(a, b):
    return lax.dot_general(a, b, (((1,), (1,)), ((), ())), preferred_element_type=F32)


def in_order(a, row_table):
    chunks = a.reshape(8, CH)
    pick = row_table[:, None, None] == jnp.arange(8, dtype=jnp.int32)[None, :, None]
    return jnp.sum(jnp.where(pick, chunks[None], 0), axis=1).reshape(ROWS)


def local(
    tokens,
    segments,
    weight_qkv,
    weight_out,
    weight_gate_up,
    weight_down,
    norm_gains,
    head_gains,
    first_qkv,
    first_out,
    first_gate_up,
    first_down,
    first_norm,
    first_head,
    second_qkv,
    second_out,
    second_gate_up,
    second_down,
    second_norm,
    second_head,
    cotangent,
):
    seg_low = jnp.concatenate([segments >> 6, segments & 63]).astype(BF16).reshape(4, 256)
    seg_low = jnp.pad(seg_low, ((0, 12), (0, 128)))
    qkv_low = weight_qkv.astype(BF16)
    w_first, w_second = gather_both(jnp.concatenate([qkv_low[:64], seg_low], axis=0), qkv_low[64:])

    dp = lax.axis_index("dp")
    tensor = lax.axis_index("tensor")
    y, x = dp >> 2, dp & 3
    z, core = tensor >> 1, tensor & 1
    slots = jnp.arange(8, dtype=jnp.int32)
    row_table = 2 * ((z + slots) & 3) + (core ^ (slots >> 2))
    sixteen = jnp.arange(16, dtype=jnp.int32)
    blocks = ((((sixteen >> 2) + y) & 3) << 2) + ((sixteen + x) & 3)
    blocks_turned = ((((sixteen) + y) & 3) << 2) + (((sixteen >> 2) + x) & 3)
    own_blocks = jnp.stack([dp, 15 - dp])
    zero_slot = ((-y & 3) << 2) + (-x & 3)
    partner_slot = (((3 - 2 * y) & 3) << 2) + ((3 - 2 * x) & 3)

    down_out, gate_up, weight_squares = pack(weight_qkv, weight_out, weight_gate_up, weight_down)
    down_out = lax.all_gather(down_out, "dp", axis=0, tiled=True)
    gate_up = lax.all_gather(gate_up, "dp", axis=0, tiled=True)

    attn_in = prepare(row_table, tokens, norm_gains[0:1])
    token_ids = (row_table[:, None] * CH + jnp.arange(CH, dtype=jnp.int32)[None, :]).reshape(ROWS)
    frequency = ROPE_BASE ** (-(jnp.arange(HD // 2, dtype=F32) * 2.0 / HD))
    angles = (dp * ROWS + token_ids).astype(F32)[:, None] * jnp.tile(frequency, 4)[None, :]
    cosine, sine = jnp.cos(angles), jnp.sin(angles)
    gain_rows = jnp.concatenate(
        [
            jnp.concatenate([head_gains[0:1], head_gains[0:1]], axis=1),
            jnp.concatenate([head_gains[1:2], jnp.ones((1, HD), F32)], axis=1),
            jnp.zeros((6, 128), F32),
        ]
    )
    projected, q_own, q_send, local_kv, full_qkv, all_segs = project(
        blocks, attn_in, w_first, w_second, cosine, sine, gain_rows
    )
    kv_groups, (all_segs, tokens, cotangent) = gather_dp(local_kv, (all_segs, tokens, cotangent))
    kv_groups, (across, x_rows, dy) = beside(
        kv_groups, arrange(row_table, tokens, cotangent, attn_in)
    )

    def block_segs(slot):
        pick = (sixteen == slot)[:, None, None]
        got = jnp.sum(jnp.where(pick, all_segs[:, :4, :256].astype(jnp.int32), 0), axis=0)
        got = got.reshape(2, ROWS)
        return got[0] * 64 + got[1]

    partner_segs = block_segs(partner_slot)
    seg_rows = in_order(segments, row_table)
    first_rows = in_order(block_segs(zero_slot), row_table)
    partner_rows = in_order(partner_segs, row_table)
    kinfo = jnp.stack([seg_rows, partner_rows, first_rows, token_ids], axis=1)
    qinfo = jnp.concatenate(
        [seg_rows[None], partner_rows[None], token_ids[None], jnp.zeros((5, ROWS), jnp.int32)]
    )
    bias = jnp.concatenate(
        [
            jnp.where(seg_rows == segments[0], 0.0, OFF).astype(F32)[None],
            jnp.where(partner_rows == partner_segs[0], 0.0, OFF).astype(F32)[None],
            jnp.zeros((6, ROWS), F32),
        ]
    )
    block_info = jnp.concatenate([blocks, own_blocks])
    mixed, out_own, log_own, out_send, kv_all = attend(
        block_info, q_own, q_send, kv_groups, kinfo, qinfo, bias
    )

    far = out_project(1, mixed, down_out, BF16)
    near = out_project(0, mixed, down_out, F32)
    own_tokens = x_rows[:CH].astype(F32)
    attn_rows, grad_inner = scatter_tensor(near, far, inner_grad(dy, down_out))
    hidden_one = own_tokens + attn_rows
    scale_two = inverse_rms(hidden_one)
    normed_two = hidden_one * scale_two
    ffn_in, (out_other, q_other) = gather_tensor(
        (normed_two * norm_gains[1]).astype(BF16), (from_partner(out_send), from_partner(q_send))
    )
    inner_act, grad_gate, grad_up, near, far = feed_forward(*ffn_in, grad_inner, gate_up)

    grads = weight_grad([dy], [inner_act], 8)
    grads = weight_grad(ffn_in, [grad_gate, grad_up], 0, grads)
    grad_ffn_in, grads = scatter_tensor(near, far, grads)
    grads = lax.psum_scatter(grads, "dp", scatter_dimension=0, tiled=True)
    gain_ffn = jnp.sum(grad_ffn_in * normed_two, axis=0)
    grad_hidden = dy[:CH].astype(F32) + norm_back(grad_ffn_in, normed_two, scale_two, norm_gains[1])
    ffn_parts = ffn_out(inner_act, down_out)
    grad_attn, (ffn_near, ffn_far) = gather_tensor(grad_hidden.astype(BF16), ffn_parts)

    do_own, do_send = mixed_grad(*grad_attn, down_out)
    do_other = from_partner(do_send)
    out_parts = out_grad(blocks, *grad_attn, mixed)
    (do_other, ffn_far), out_parts = beside((do_other, from_core(ffn_far)), out_parts)
    ffn_near = (ffn_near + ffn_far.astype(F32)).reshape(4, CH, D)
    ffn_low = ffn_near.astype(BF16)
    ffn_got = {k: from_z(ffn_low[k], -k) for k in (2, 1, 3)}
    operands = ready(do_own, do_other, out_own, log_own, out_other, q_own, q_other, bias)
    dq_own, dq_send, part_u, part_v = attend_back(block_info, operands, kv_all, kinfo, qinfo)
    dq_send, ffn_got = beside(dq_send, ffn_got)
    dq_other = from_partner(dq_send)
    part_v, dq_other = beside(part_v, dq_other)
    got_u, got_v = send(part_u, from_y), send(part_v, from_x)
    grad_query, gain_query = heads_back(
        (0, 1), projected, [dq_own, dq_other], cosine, sine, gain_rows
    )
    parts = query_out_grad(blocks, across, grad_query, out_parts)
    attn_part, gain_attn = attn_back(grad_query, full_qkv, x_rows)
    (got_u, got_v), (parts, attn_part) = beside((got_u, got_v), (parts, attn_part))
    block_rows = (hidden_one + sum_four(ffn_near[0], ffn_got)).astype(BF16)
    line_u, line_v = sum_four(part_u[0], got_u), sum_four(part_v[0], got_v)
    low_u, low_v = line_u.astype(BF16), line_v.astype(BF16)
    got_u = {k: from_x(low_u[k], -k) for k in (2, 1, 3)}
    got_v = {k: from_y(low_v[k], -k) for k in (2, 1, 3)}
    grad_kv = jnp.concatenate([sum_four(line_u[0], got_u), sum_four(line_v[0], got_v)]).astype(BF16)
    grad_kv, gain_key = heads_back((2,), projected, [grad_kv], cosine, sine, gain_rows)
    parts_u, parts_v = key_grad(blocks, across, grad_kv, parts)
    got_u, got_v = send(parts_u, from_y), send(parts_v, from_x)

    grad_kv, _ = beside(grad_kv, (parts_u, parts_v))
    block_out = keep(lax.all_gather(block_rows, "tensor", axis=0, tiled=True))
    partial, gain_rest = attn_back_rest(row_table, grad_kv, full_qkv, x_rows, attn_part)
    partial, grads = beside(partial, grads)
    grad_attn_in = lax.psum_scatter(partial, "tensor", scatter_dimension=0, tiled=True).astype(F32)
    (gate_up_step, down_step), later_squares = take_step(
        [grads],
        [(weight_gate_up, first_gate_up, second_gate_up), (weight_down, first_down, second_down)],
        ((0, 0, 1024, False, 2), (0, 2048, 1024, True, 3)),
    )
    (got_u, got_v), (later_squares, block_out) = beside((got_u, got_v), (later_squares, block_out))
    late_u = scatter_rest(parts_u[0], got_u, from_x)
    late_v = scatter_rest(parts_v[0], got_v, from_y)
    grad_attn_in, _ = beside(grad_attn_in, (late_u, late_v))
    late_grad = jnp.concatenate([late_u, late_v])
    scale_one = inverse_rms(own_tokens)
    normed_one = own_tokens * scale_one
    input_grad = (
        grad_hidden + norm_back(grad_attn_in, normed_one, scale_one, norm_gains[0])
    ).astype(BF16)
    input_grad = lax.all_gather(input_grad, "tensor", axis=0, tiled=True)

    (qkv_step, out_step), qkv_squares = take_step(
        [jnp.concatenate([late_grad[:, :256], late_grad[:, 512:]], axis=1), late_grad],
        [(weight_qkv, first_qkv, second_qkv), (weight_out, first_out, second_out)],
        ((0, 0, 384, False, 0), (1, 256, 256, True, 1)),
    )
    squares = jnp.concatenate(
        [
            gain_query[0:1],
            gain_key[0:1],
            weight_squares[:4].reshape(1, 512),
            (later_squares + qkv_squares)[:4].reshape(1, 512),
            jnp.zeros((1, D - 1280), F32),
        ],
        axis=1,
    )
    sums = jnp.concatenate([gain_attn + gain_rest, gain_ffn[None], squares, jnp.zeros((1, D), F32)])
    sums = sum_all(sums)
    steps = (qkv_step, out_step, gate_up_step, down_step)
    done = finish(
        sums,
        (weight_qkv, weight_out, weight_gate_up, weight_down),
        [step[2] for step in steps],
        (norm_gains, first_norm, second_norm),
        (head_gains, first_head, second_head),
    )
    return (
        block_out,
        input_grad,
        *done[:4],
        done[4],
        done[7],
        *[step[0] for step in steps],
        done[5],
        done[8],
        *[step[1] for step in steps],
        done[6],
        done[9],
        done[10],
    )


def solution(mesh):
    matrix_specs = (P("dp", "tensor"), P("tensor", "dp"), P(None, "dp", "tensor"), P("tensor", "dp"), P(), P())
    in_specs = (P("dp", None), P("dp"), *matrix_specs, *matrix_specs, *matrix_specs, P("dp", None))
    out_specs = (P("dp", None), P("dp", None), *matrix_specs, *matrix_specs, *matrix_specs, P())
    return jax.shard_map(local, mesh=mesh, in_specs=in_specs, out_specs=out_specs, check_vma=False)
```

```python
import functools

import jax
import jax.numpy as jnp
from jax import lax
from jax.experimental import pallas as pl
from jax.experimental.pallas import tpu as pltpu
from jax.sharding import PartitionSpec as P

H = 32
KVH = 8
HD = 64
STEP = 5
D = 2048
ROWS = 512
QPK = 4
CH = 64
FLAT_GRAD = 2048 + 1024

EPS_NORM = 1e-05
ROPE_BASE = 1000000.0
BETA_ONE = 0.5
BETA_TWO = 0.5
EPS_ADAM = 1e-06
DECAY = 0.01
RATE = 0.5
F32 = jnp.float32
BF16 = jnp.bfloat16
OFF = -1e5
VMEM_LIMIT = 24 * 1024 * 1024
VMEM_LARGE = 44 * 1024 * 1024


def inverse_rms(array_in):
    return lax.rsqrt(jnp.mean(array_in * array_in, axis=-1, keepdims=True) + EPS_NORM)


def adapt(weight, first_old, second_old, grad_in):
    first_new = BETA_ONE * first_old + (1.0 - BETA_ONE) * grad_in
    second_new = BETA_TWO * second_old + (1.0 - BETA_TWO) * grad_in * grad_in
    direction = (
        first_new
        / (1.0 - BETA_ONE**STEP)
        / (jnp.sqrt(second_new / (1.0 - BETA_TWO**STEP)) + EPS_ADAM)
        + DECAY * weight
    )
    return (first_new, second_new, direction)


def perm_x(k):
    return [(i, (i // 4) * 4 + (i % 4 - k) % 4) for i in range(16)]


def perm_y(k):
    return [(i, ((i // 4 - k) % 4) * 4 + i % 4) for i in range(16)]


def perm_z(k):
    return [(i, ((i // 2 - k) % 4) * 2 + i % 2) for i in range(8)]


PERM_CORE = [(i, i ^ 1) for i in range(8)]
PERM_PARTNER = [(i, 15 - i) for i in range(16)]


def from_x(a, k):
    return lax.ppermute(a, "dp", perm_x(k))


def from_y(a, k):
    return lax.ppermute(a, "dp", perm_y(k))


def from_z(a, k):
    return lax.ppermute(a, "tensor", perm_z(k))


def from_core(a):
    return lax.ppermute(a, "tensor", PERM_CORE)


def from_partner(a):
    return lax.ppermute(a, "dp", PERM_PARTNER)


def beside(arrays, work):
    return lax.optimization_barrier((arrays, work))


def gather_both(u, v):
    row = {k: from_x(u, k) for k in (2, 1, 3)}
    column = {k: from_y(v, k) for k in (2, 1, 3)}
    row = jnp.stack([u, row[1], row[2], row[3]])
    column = jnp.stack([v, column[1], column[2], column[3]])
    second = {k: (from_y(row, k), from_x(column, k)) for k in (2, 1, 3)}
    first = [row] + [second[k][0] for k in (1, 2, 3)]
    return first, [column] + [second[k][1] for k in (1, 2, 3)]


def gather_dp(a, later):
    row = {k: from_x(a, k) for k in (2, 1, 3)}
    row, later = beside(row, later)
    row = jnp.stack([a, row[1], row[2], row[3]])
    second = {k: from_y(row, k) for k in (2, 1, 3)}
    return [row] + [second[k] for k in (1, 2, 3)], later


def sum_four(own, got):
    return (own.astype(F32) + got[2].astype(F32)) + (got[1].astype(F32) + got[3].astype(F32))


def send(parts, step):
    return {k: step(parts[k], -k) for k in (2, 1, 3)}


def scatter_rest(own, got, step):
    line = sum_four(own, got)
    low = line.astype(BF16)
    return sum_four(line[0], {k: step(low[k], -k) for k in (2, 1, 3)})


def scatter_tensor(near, far, work=None):
    near = near.astype(F32) + from_core(far.astype(BF16)).astype(F32)
    parts = near.reshape(4, CH, near.shape[-1])
    low = parts.astype(BF16)
    got = {k: from_z(low[k], -k) for k in (2, 1, 3)}
    if work is None:
        return sum_four(parts[0], got)
    got, work = beside(got, work)
    return sum_four(parts[0], got), work


def gather_tensor(a, work=None):
    got = {k: from_z(a, k) for k in (2, 1, 3)}
    if work is not None:
        got, work = beside(got, work)
    near = jnp.concatenate([a, got[1], got[2], got[3]], axis=0)
    halves = (near, from_core(near))
    return halves if work is None else (halves, work)


def sum_all(a):
    for step in (from_x, from_y, from_z):
        a = (a + step(a, 2)) + (step(a, 1) + step(a, 3))
    return a + from_core(a)


def params(vmem=VMEM_LIMIT):
    return pltpu.CompilerParams(vmem_limit_bytes=vmem)


def takes(us):
    return pl.CostEstimate(flops=int(us * 1.1e9), bytes_accessed=0, transcendentals=0)


def whole_specs(arrays):
    return [pl.BlockSpec(a.shape, lambda i, n=len(a.shape): (0,) * n) for a in arrays]


def prepare_kernel(row_ref, tok_ref, gain_ref, in_ref):
    x = tok_ref[...].astype(F32)
    in_ref[...] = (x * inverse_rms(x) * gain_ref[...]).astype(BF16)


def prepare(row_table, tokens, gain):
    return pl.pallas_call(
        prepare_kernel,
        grid_spec=pltpu.PrefetchScalarGridSpec(
            num_scalar_prefetch=1,
            grid=(8,),
            in_specs=[
                pl.BlockSpec((CH, D), lambda i, r: (r[i], 0)),
                pl.BlockSpec((1, D), lambda i, r: (0, 0)),
            ],
            out_specs=pl.BlockSpec((CH, D), lambda i, r: (i, 0)),
        ),
        out_shape=jax.ShapeDtypeStruct((ROWS, D), BF16),
        compiler_params=params(),
        name="prepare",
        cost_estimate=takes(4),
    )(row_table, tokens, gain)


def arrange_kernel(row_ref, tok_ref, cot_ref, in_ref, across_ref, x_ref, dy_ref):
    x_ref[...] = tok_ref[...]
    dy_ref[...] = cot_ref[...]

    @pl.when(pl.program_id(0) % 2 == 0)
    def _():
        across_ref[...] = in_ref[...].astype(F32).T.astype(BF16)


def arrange(row_table, tokens, cotangent, attn_in):
    pick = pl.BlockSpec((CH, D), lambda i, r: (r[i], 0))
    put = pl.BlockSpec((CH, D), lambda i, r: (i, 0))
    return pl.pallas_call(
        arrange_kernel,
        grid_spec=pltpu.PrefetchScalarGridSpec(
            num_scalar_prefetch=1,
            grid=(8,),
            in_specs=[pick, pick, pl.BlockSpec((128, D), lambda i, r: (i // 2, 0))],
            out_specs=[pl.BlockSpec((D, 128), lambda i, r: (0, i // 2)), put, put],
        ),
        out_shape=[
            jax.ShapeDtypeStruct((D, ROWS), BF16),
            jax.ShapeDtypeStruct((ROWS, D), BF16),
            jax.ShapeDtypeStruct((ROWS, D), BF16),
        ],
        compiler_params=params(),
        name="arrange",
        cost_estimate=takes(7),
    )(row_table, tokens, cotangent, attn_in)


def lane_of(shape):
    return lax.broadcasted_iota(jnp.int32, shape, len(shape) - 1)


def head_sums(a, low_half):
    left = jnp.sum(jnp.where(low_half, a, 0.0), axis=-1, keepdims=True)
    right = jnp.sum(jnp.where(low_half, 0.0, a), axis=-1, keepdims=True)
    return jnp.where(low_half, left, right)


def turn(a, first):
    return jnp.where(first, pltpu.roll(a, 96, 1), pltpu.roll(a, 32, 1))


def vmem_specs(count):
    return [pl.BlockSpec(memory_space=pltpu.VMEM)] * count


def shape(dims, kind):
    return jax.ShapeDtypeStruct(dims, kind)


def column_squares(a):
    total = None
    for at in range(0, a.shape[-1], 128):
        part = a[:, at : at + 128]
        part = jnp.sum(part * part, axis=0, keepdims=True)
        total = part if total is None else total + part
    return total


def eight_rows(rows):
    row = lax.broadcasted_iota(jnp.int32, (8, 128), 0)
    out = jnp.zeros((8, 128), F32)
    for index, value in enumerate(rows):
        if value is not None:
            out = jnp.where(row == index, value, out)
    return out


def pack_kernel(qkv_in, out_in, gate_up_in, down_in, first_ref, second_ref, squares_ref, qkv, out_w, gate_up, down, sems):
    pairs = ((down_in, down), (out_in, out_w), (gate_up_in, gate_up), (qkv_in, qkv))
    copies = [pltpu.make_async_copy(a, b, sems.at[i]) for i, (a, b) in enumerate(pairs)]
    for copy in copies:
        copy.start()
    copies[0].wait()
    first_ref[:, :1024] = down[...].T.astype(BF16)
    copies[1].wait()
    first_ref[:, 1024:] = out_w[...].T.astype(BF16)
    copies[2].wait()
    second_ref[:, :1024] = gate_up[0].astype(BF16)
    second_ref[:, 1024:] = gate_up[1].astype(BF16)
    copies[3].wait()
    squares_ref[...] = eight_rows(
        [
            column_squares(qkv[...]),
            column_squares(out_w[...]),
            column_squares(gate_up[0]) + column_squares(gate_up[1]),
            column_squares(down[...]),
        ]
    )


def pack(weight_qkv, weight_out, weight_gate_up, weight_down):
    given = (weight_qkv, weight_out, weight_gate_up, weight_down)
    return pl.pallas_call(
        pack_kernel,
        in_specs=[pl.BlockSpec(memory_space=pl.ANY)] * 4,
        out_specs=vmem_specs(3),
        out_shape=[shape((128, 1280), BF16), shape((128, 2048), BF16), shape((8, 128), F32)],
        scratch_shapes=[pltpu.VMEM(a.shape, F32) for a in given] + [pltpu.SemaphoreType.DMA((4,))],
        compiler_params=params(60 * 1024 * 1024),
        name="pack",
        cost_estimate=takes(2),
    )(*given)


def project_kernel(
    blk_ref, x_ref, u0, u1, u2, u3, v0, v1, v2, v3, cos_ref, sin_ref, gain_ref,
    proj_ref, q_own_ref, q_send_ref, kv_ref, w_ref, seg_ref,
):
    @pl.when(pl.program_id(0) == 0)
    def _():
        for at_y in range(4):
            for at_x in range(4):
                slot = at_y * 4 + at_x
                start = pl.multiple_of(blk_ref[slot] * 128, 128)
                w_ref[pl.ds(start, 64), :] = (u0, u1, u2, u3)[at_y][at_x, :64, :]
                w_ref[pl.ds(start + 64, 64), :] = (v0, v1, v2, v3)[at_x][at_y]
                seg_ref[slot] = (u0, u1, u2, u3)[at_y][at_x, 64:, :]

    acc = jnp.dot(x_ref[...], w_ref[...], preferred_element_type=F32)
    proj_ref[...] = acc
    lane = lane_of((x_ref.shape[0], 128))
    low_half = lane < 64
    first = (lane & 63) < 32
    cosine = cos_ref[...]
    sine = jnp.where(first, -sin_ref[...], sin_ref[...])
    for pair in range(3):
        u = acc[:, pair * 128 : (pair + 1) * 128]
        scale = lax.rsqrt(head_sums(u * u, low_half) * (1.0 / HD) + EPS_NORM)
        hat = u * scale * gain_ref[pair // 2 : pair // 2 + 1, :]
        turned = hat * cosine + turn(hat, first) * sine
        if pair < 2:
            across = (turned.astype(BF16).astype(F32) * 0.125).T.astype(BF16)
            out = (q_own_ref, q_send_ref)[pair]
            out[0] = across[:64]
            out[1] = across[64:]
        else:
            kv_ref[...] = jnp.where(low_half, turned, u).astype(BF16)


def project(blocks, x, w_first, w_second, cosine, sine, gains):
    tile = 128
    whole = lambda dims: pl.BlockSpec(dims, lambda i, b: (0,) * len(dims))
    row = lambda width: pl.BlockSpec((tile, width), lambda i, b: (i, 0))
    pair = pl.BlockSpec((2, HD, tile), lambda i, b: (0, 0, i))
    return pl.pallas_call(
        project_kernel,
        grid_spec=pltpu.PrefetchScalarGridSpec(
            num_scalar_prefetch=1,
            grid=(ROWS // tile,),
            in_specs=[row(D)]
            + [whole((4, 80, 384))] * 4
            + [whole((4, 64, 384))] * 4
            + [row(128), row(128), whole((8, 128))],
            out_specs=[row(384), pair, pair, row(128), whole((D, 384)), whole((16, 16, 384))],
        ),
        out_shape=[
            shape((ROWS, 384), F32),
            shape((2, HD, ROWS), BF16),
            shape((2, HD, ROWS), BF16),
            shape((ROWS, 128), BF16),
            shape((D, 384), BF16),
            shape((16, 16, 384), BF16),
        ],
        compiler_params=params(),
        name="project",
        cost_estimate=takes(6),
    )(blocks, x, *w_first, *w_second, cosine, sine, gains)


def lane_masks():
    low = (lane_of((1, 128)) < 64).astype(F32)
    return low.astype(BF16), (1.0 - low).astype(BF16)


def allowed_keys(queries, is_own, at, count, kinfo_ref, qinfo_ref):
    info = kinfo_ref[pl.ds(at, count), :]
    seg = jnp.where(is_own, info[:, queries : queries + 1], info[:, 2:3])
    pos = jnp.where(is_own, info[:, 3:4], -1)
    return (seg == qinfo_ref[queries : queries + 1, :]) & (pos <= qinfo_ref[2:3, :])


def for_queries(blk_ref, slot, own_at, sets, work):
    block = blk_ref[slot]
    for queries in range(sets):
        own = blk_ref[own_at + queries]

        @pl.when((block == 0) | (block == own))
        def _(queries=queries, own=own):
            work(queries, True, block == own)

        @pl.when((block > 0) & (block < own))
        def _(queries=queries):
            work(queries, False, None)


def forward_kernel(
    blk_ref, q_first, q_second, kv0, kv1, kv2, kv3, kinfo_ref, qinfo_ref, bias_ref,
    mixed_ref, out_ref, lse_ref, send_ref, kv_all, q_t, acc,
):
    for group, ref in enumerate((kv0, kv1, kv2, kv3)):
        kv_all[group * 4 : (group + 1) * 4] = ref[...]
    acc[...] = jnp.zeros_like(acc)
    row = lax.broadcasted_iota(jnp.int32, (64, ROWS), 0)
    bias = jnp.where(row == 0, bias_ref[0:1, :], 0.0).astype(BF16)
    for head in range(QPK):
        q_t[head, :64, :] = (q_first, q_second)[head // 2][head % 2]
        q_t[head, 64:, :] = bias
    keep_k, keep_v = lane_masks()

    def step(slot, carry):
        def work(queries, masked, is_own):
            kv = kv_all[slot]
            keys = kv * keep_k + (keep_v if not masked else jnp.zeros_like(keep_v))
            vals = (kv * keep_v + keep_k).astype(F32).T.astype(BF16)[56:]
            if masked:
                allowed = allowed_keys(queries, is_own, 0, ROWS, kinfo_ref, qinfo_ref)
            for head in range(QPK):
                scores = jnp.dot(keys, q_t[head], preferred_element_type=F32)
                probs = jnp.exp(scores)
                if masked:
                    probs = jnp.where(allowed, probs, 0.0)
                acc[head] += jnp.dot(vals, probs.astype(BF16), preferred_element_type=F32)

        for_queries(blk_ref, slot, 16, 1, work)
        return carry

    lax.fori_loop(0, 16, step, 0)
    heads = []
    logs = []
    for head in range(QPK):
        total = acc[head, 0:1, :]
        heads.append(acc[head, 8:, :] / total)
        logs.append(jnp.log(total))
    mixed_ref[...] = jnp.concatenate(heads, axis=0).T.astype(BF16)
    rest = jnp.zeros((6, ROWS), F32)
    out_ref[:64], out_ref[64:] = heads[0], heads[1]
    lse_ref[...] = jnp.concatenate(logs[:2] + [rest], axis=0)
    send_ref[:64], send_ref[64:128] = heads[2], heads[3]
    send_ref[128:] = jnp.concatenate(logs[2:] + [rest], axis=0)


def attend(blocks, q_first, q_second, kv, kinfo, qinfo, bias):
    return pl.pallas_call(
        forward_kernel,
        in_specs=[pl.BlockSpec(memory_space=pltpu.SMEM)] + vmem_specs(9),
        out_specs=vmem_specs(5),
        out_shape=[
            shape((ROWS, 256), BF16),
            shape((128, ROWS), F32),
            shape((8, ROWS), F32),
            shape((136, ROWS), F32),
            shape((16, ROWS, 128), BF16),
        ],
        scratch_shapes=[
            pltpu.VMEM((QPK, 128, ROWS), BF16),
            pltpu.VMEM((QPK, 72, ROWS), F32),
        ],
        compiler_params=params(VMEM_LARGE),
        name="attend",
        cost_estimate=takes(20),
    )(blocks, q_first, q_second, *kv, kinfo, qinfo, bias)


def three_rows(row, value, at):
    high = value.astype(BF16).astype(F32)
    rest = value - high
    middle = rest.astype(BF16).astype(F32)
    low = rest - middle
    return (
        jnp.where(row == at, high, 0.0)
        + jnp.where(row == at + 1, middle, 0.0)
        + jnp.where(row == at + 2, low, 0.0)
    )


def mixed_grad_kernel(near_ref, far_ref, w_ref, own_ref, send_ref):
    w = w_ref[...]
    for half, ref in enumerate((near_ref, far_ref)):
        part = jnp.dot(ref[...], w, preferred_element_type=F32).astype(BF16)
        own_ref[half * 256 : (half + 1) * 256] = part[:, :128]
        send_ref[half * 256 : (half + 1) * 256] = part[:, 128:]


def mixed_grad(near, far, down_out):
    whole = lambda dims: pl.BlockSpec(dims, lambda i: (0, 0))
    return pl.pallas_call(
        mixed_grad_kernel,
        grid=(1,),
        in_specs=[whole((256, D)), whole((256, D)), pl.BlockSpec((D, 256), lambda i: (0, 4))],
        out_specs=[whole((ROWS, 128))] * 2,
        out_shape=[shape((ROWS, 128), BF16)] * 2,
        compiler_params=params(),
        name="mixed_grad",
        cost_estimate=takes(2),
    )(near, far, down_out)


def ready_kernel(do_own, do_other, out_own, lse_own, out_other, q_own, q_other, bias_ref, q_t, do_t, q_pad, do_pad):
    row = lax.broadcasted_iota(jnp.int32, (64, ROWS), 0)
    low_half = lane_of((ROWS, 128)) < 64
    for queries in range(2):
        do = (do_own, do_other)[queries][...].astype(F32)
        q_ref = (q_own, q_other)[queries]
        q = jnp.concatenate([q_ref[0].astype(F32), q_ref[1].astype(F32)], axis=0).T
        do_turned = do.T
        dots = do_turned * (out_own, out_other)[queries][:128, :]
        for part in range(2):
            head = 2 * queries + part
            at = slice(part * 64, (part + 1) * 64)
            delta = jnp.sum(dots[at, :], axis=0, keepdims=True)
            lse = (out_other[128 + part : 129 + part, :] if queries else lse_own[part : part + 1, :])
            extra = three_rows(row, -lse, 0)
            extra = extra + jnp.where(row == 3, bias_ref[queries : queries + 1, :], 0.0)
            q_t[head, :64, :] = q_ref[part]
            q_t[head, 64:, :] = extra.astype(BF16)
            do_t[head, :64, :] = three_rows(row, -delta, 0).astype(BF16)
            do_t[head, 64:, :] = do_turned[at, :].astype(BF16)
            q_head = pltpu.roll(q, 64, 1) if part else q
            do_head = do if part else pltpu.roll(do, 64, 1)
            q_pad[head] = jnp.where(low_half, q_head, 0.0).astype(BF16)
            do_pad[head] = jnp.where(low_half, 0.0, do_head).astype(BF16)


def ready(*given):
    return pl.pallas_call(
        ready_kernel,
        in_specs=vmem_specs(len(given)),
        out_specs=vmem_specs(4),
        out_shape=[shape((QPK, 128, ROWS), BF16)] * 2 + [shape((QPK, ROWS, 128), BF16)] * 2,
        compiler_params=params(),
        name="ready",
        cost_estimate=takes(2.5),
    )(*given)


def backward_kernel(
    blk_ref, q_t, do_t, q_pad, do_pad, kv_all, kinfo_ref, qinfo_ref, own_ref, other_ref, u_ref, v_ref, dq_t, total
):
    dq_t[...] = jnp.zeros_like(dq_t)
    keep_k, keep_v = lane_masks()
    keep_v_masked = jnp.where(lane_of((1, 128)) == 67, 0.0, keep_v.astype(F32)).astype(BF16)

    def step(slot, carry):
        total[...] = jnp.zeros_like(total)

        def work(queries, masked, is_own):
            kv = kv_all[slot]
            keys = kv * keep_k + (keep_v_masked if masked else keep_v)
            vals = kv * keep_v + keep_k
            keys_turned = kv.astype(F32).T[:64, :].astype(BF16)
            if masked:
                allowed = allowed_keys(queries, is_own, 0, ROWS, kinfo_ref, qinfo_ref)
            for head in (2 * queries, 2 * queries + 1):
                scores = jnp.dot(keys, q_t[head], preferred_element_type=F32)
                probs = jnp.exp(scores)
                if masked:
                    probs = jnp.where(allowed, probs, 0.0)
                grads = jnp.dot(vals, do_t[head], preferred_element_type=F32)
                grads = (probs * grads).astype(BF16)
                term = jnp.dot(probs.astype(BF16), do_pad[head], preferred_element_type=F32)
                total[...] += term + jnp.dot(grads, q_pad[head], preferred_element_type=F32)
                dq_t[head * 64 : (head + 1) * 64, :] += jnp.dot(
                    keys_turned, grads, preferred_element_type=F32
                )

        for_queries(blk_ref, slot, 16, 2, work)
        u_ref[slot // 4, slot % 4] = total[:256].astype(BF16)
        v_ref[slot % 4, slot // 4] = total[256:].astype(BF16)
        return carry

    lax.fori_loop(0, 16, step, 0)
    dq = (dq_t[...].T * 0.125).astype(BF16)
    own_ref[...] = dq[:, :128]
    other_ref[...] = dq[:, 128:]


def attend_back(blocks, operands, kv, kinfo, qinfo):
    pair = shape((ROWS, 128), BF16)
    half = shape((4, 4, 256, 128), BF16)
    return pl.pallas_call(
        backward_kernel,
        in_specs=[pl.BlockSpec(memory_space=pltpu.SMEM)] + vmem_specs(7),
        out_specs=vmem_specs(4),
        out_shape=[pair, pair, half, half],
        scratch_shapes=[pltpu.VMEM((256, ROWS), F32), pltpu.VMEM((ROWS, 128), F32)],
        compiler_params=params(VMEM_LARGE),
        name="attend_back",
        cost_estimate=takes(36),
    )(blocks, *operands, kv, kinfo, qinfo)


def heads_back_kernel(pairs, proj_ref, *refs):
    grads = refs[: len(pairs)]
    cos_ref, sin_ref, gain_ref, out_ref, sum_ref = refs[len(pairs) :]
    lane = lane_of((proj_ref.shape[0], 128))
    low_half = lane < 64
    first = (lane & 63) < 32
    cosine = cos_ref[...]
    sine = jnp.where(first, sin_ref[...], -sin_ref[...])
    sums = None
    for index, pair in enumerate(pairs):
        u = proj_ref[:, pair * 128 : (pair + 1) * 128]
        grad = grads[index][...].astype(F32)
        scale = lax.rsqrt(head_sums(u * u, low_half) * (1.0 / HD) + EPS_NORM)
        hat = u * scale
        turned = grad * cosine + turn(grad, first) * sine
        part = jnp.sum(turned * hat, axis=0, keepdims=True)
        sums = part if sums is None else sums + part
        grad_hat = turned * gain_ref[pair // 2 : pair // 2 + 1, :]
        mean = head_sums(grad_hat * hat, low_half) * (1.0 / HD)
        back = scale * (grad_hat - hat * mean)
        if pair == 2:
            back = jnp.where(low_half, back, grad)
        out_ref[:, index * 128 : (index + 1) * 128] = back.astype(BF16)

    @pl.when(pl.program_id(0) == 0)
    def _():
        sum_ref[...] = jnp.zeros_like(sum_ref)

    sum_ref[0:1, :] += sums


def heads_back(pairs, proj, grads, cosine, sine, gains):
    tile = 128
    row = lambda width: pl.BlockSpec((tile, width), lambda i: (i, 0))
    whole = pl.BlockSpec((8, 128), lambda i: (0, 0))
    wide = 128 * len(pairs)
    return pl.pallas_call(
        functools.partial(heads_back_kernel, pairs),
        grid=(ROWS // tile,),
        in_specs=[row(384)] + [row(128)] * (len(pairs) + 2) + [whole],
        out_specs=[row(wide), whole],
        out_shape=[shape((ROWS, wide), BF16), shape((8, 128), F32)],
        compiler_params=params(),
        name="heads_back",
        cost_estimate=takes(len(pairs)),
    )(proj, *grads, cosine, sine, gains)


def out_kernel(mixed_ref, w_ref, out_ref):
    out_ref[...] = dot_cols(mixed_ref[...], w_ref[...]).astype(out_ref.dtype)


def out_project(half, mixed, down_out, kind):
    return pl.pallas_call(
        out_kernel,
        grid=(1,),
        in_specs=[
            pl.BlockSpec((256, 256), lambda i: (half, 0)),
            pl.BlockSpec((D, 256), lambda i: (0, 4)),
        ],
        out_specs=pl.BlockSpec((256, D), lambda i: (0, 0)),
        out_shape=shape((256, D), kind),
        compiler_params=params(),
        name="out_project",
        cost_estimate=takes(1.8),
    )(mixed, down_out)


def ffn_kernel(
    near_ref, far_ref, grad_ref, w_in, act_ref, gate_ref, up_ref, near_out, far_out, w, x_all, both, sems
):
    tiles = []
    for tile in range(4):
        at = (slice(tile * 256, (tile + 1) * 256), slice(1024 + tile * 256, 1024 + (tile + 1) * 256))
        pair = [
            pltpu.make_async_copy(w_in.at[:, part], w.at[:, part], sems.at[2 * tile + i])
            for i, part in enumerate(at)
        ]
        for copy in pair:
            copy.start()
        tiles.append((at, pair))
    x_all[:256] = near_ref[...]
    x_all[256:] = far_ref[...]
    for (gate_at, up_at), pair in tiles:
        for copy in pair:
            copy.wait()
        x = x_all[...]
        gate = jnp.dot(x, w[:, gate_at], preferred_element_type=F32)
        up = jnp.dot(x, w[:, up_at], preferred_element_type=F32)
        inner = grad_ref[:, gate_at]
        sigmoid = jax.nn.sigmoid(gate)
        activated = gate * sigmoid
        act_ref[:, gate_at] = (activated * up).astype(BF16)
        grad_gate = (inner * up * sigmoid * (1.0 + gate * (1.0 - sigmoid))).astype(BF16)
        grad_up = (inner * activated).astype(BF16)
        gate_ref[:, gate_at] = grad_gate
        up_ref[:, gate_at] = grad_up
        both[:, gate_at] = grad_gate
        both[:, up_at] = grad_up
    for tile in range(4):
        at = slice(tile * 512, (tile + 1) * 512)
        part = dot_cols(both[...], w[at, :])
        near_out[:, at] = part[:256]
        far_out[:, at] = part[256:].astype(BF16)


def feed_forward(near, far, grad_inner, gate_up):
    return pl.pallas_call(
        ffn_kernel,
        in_specs=vmem_specs(3) + [pl.BlockSpec(memory_space=pl.ANY)],
        out_specs=vmem_specs(5),
        out_shape=[shape((ROWS, 1024), BF16)] * 3 + [shape((256, D), F32), shape((256, D), BF16)],
        scratch_shapes=[
            pltpu.VMEM((D, 2048), BF16),
            pltpu.VMEM((ROWS, D), BF16),
            pltpu.VMEM((ROWS, 2048), BF16),
            pltpu.SemaphoreType.DMA((8,)),
        ],
        compiler_params=params(VMEM_LARGE),
        name="feed_forward",
        cost_estimate=takes(13),
    )(near, far, grad_inner, gate_up)


def inner_grad_kernel(dy_ref, w_ref, out_ref):
    out_ref[...] = jnp.dot(dy_ref[...], w_ref[...], preferred_element_type=F32)


def inner_grad(dy, down_out):
    return pl.pallas_call(
        inner_grad_kernel,
        grid=(4,),
        in_specs=[
            pl.BlockSpec((ROWS, D), lambda j: (0, 0)),
            pl.BlockSpec((D, 256), lambda j: (0, j)),
        ],
        out_specs=pl.BlockSpec((ROWS, 256), lambda j: (0, j)),
        out_shape=shape((ROWS, 1024), F32),
        compiler_params=params(),
        name="inner_grad",
        cost_estimate=takes(5.5),
    )(dy, down_out)


def ffn_out_kernel(act_ref, w_ref, near_ref, far_ref, acc):
    step = pl.program_id(0)
    term = dot_cols(act_ref[...], w_ref[...])

    @pl.when(step == 0)
    def _():
        acc[...] = term

    @pl.when(step > 0)
    def _():
        acc[...] += term

    @pl.when(step == pl.num_programs(0) - 1)
    def _():
        near_ref[...] = acc[:256]
        far_ref[...] = acc[256:].astype(BF16)


def ffn_out(act, down_out):
    whole = lambda dims: pl.BlockSpec(dims, lambda j: (0, 0))
    return pl.pallas_call(
        ffn_out_kernel,
        grid=(4,),
        in_specs=[
            pl.BlockSpec((ROWS, 256), lambda j: (0, j)),
            pl.BlockSpec((D, 256), lambda j: (0, j)),
        ],
        out_specs=[whole((256, D)), whole((256, D))],
        out_shape=[shape((256, D), F32), shape((256, D), BF16)],
        scratch_shapes=[pltpu.VMEM((ROWS, D), F32)],
        compiler_params=params(),
        name="ffn_out",
        cost_estimate=takes(6.5),
    )(act, down_out)


def out_grad_kernel(blk_ref, near_ref, far_ref, mixed_ref, out_ref, turned):
    turned[:, :256] = near_ref[...].astype(F32).T.astype(BF16)
    turned[:, 256:] = far_ref[...].astype(F32).T.astype(BF16)
    mixed = mixed_ref[...]
    for slot in range(16):
        at = pl.ds(pl.multiple_of(blk_ref[slot] * 128, 128), 128)
        out = jnp.dot(turned[at, :], mixed, preferred_element_type=F32)
        out_ref[slot // 4, slot % 4] = out.astype(BF16)


def out_grad(blocks, near, far, mixed):
    return pl.pallas_call(
        out_grad_kernel,
        in_specs=[pl.BlockSpec(memory_space=pltpu.SMEM)] + vmem_specs(3),
        out_specs=vmem_specs(1)[0],
        out_shape=shape((4, 4, 128, 256), BF16),
        scratch_shapes=[pltpu.VMEM((D, ROWS), BF16)],
        compiler_params=params(),
        name="out_grad",
        cost_estimate=takes(2),
    )(blocks, near, far, mixed)


def query_out_grad_kernel(blk_ref, across_ref, grad_ref, parts_ref, out_ref):
    grad = grad_ref[...]
    for slot in range(16):
        at = pl.ds(pl.multiple_of(blk_ref[slot] * 128, 128), 128)
        part = jnp.dot(across_ref[at, :], grad, preferred_element_type=F32)
        out_ref[slot // 4, slot % 4, :, :256] = part.astype(BF16)
        out_ref[slot // 4, slot % 4, :, 256:] = parts_ref[slot // 4, slot % 4]


def query_out_grad(blocks, across, grad, out_parts):
    return pl.pallas_call(
        query_out_grad_kernel,
        in_specs=[pl.BlockSpec(memory_space=pltpu.SMEM)] + vmem_specs(3),
        out_specs=vmem_specs(1)[0],
        out_shape=shape((4, 4, 128, 512), BF16),
        compiler_params=params(),
        name="query_out_grad",
        cost_estimate=takes(2),
    )(blocks, across, grad, out_parts)


def key_grad_kernel(blk_ref, across_ref, grad_ref, parts_ref, u_ref, v_ref):
    grad = grad_ref[...]
    for slot in range(16):
        at_y, at_x = slot // 4, slot % 4
        at = pl.ds(pl.multiple_of(blk_ref[slot] * 128, 128), 128)
        part = jnp.dot(across_ref[at, :], grad, preferred_element_type=F32).astype(BF16)
        u_ref[at_y, at_x, :, :512] = parts_ref[at_y, at_x, :64]
        u_ref[at_y, at_x, :, 512:] = part[:64]
        v_ref[at_x, at_y, :, :512] = parts_ref[at_y, at_x, 64:]
        v_ref[at_x, at_y, :, 512:] = part[64:]


def key_grad(blocks, across, grad, parts):
    return pl.pallas_call(
        key_grad_kernel,
        in_specs=[pl.BlockSpec(memory_space=pltpu.SMEM)] + vmem_specs(3),
        out_specs=vmem_specs(2),
        out_shape=[shape((4, 4, 64, 640), BF16)] * 2,
        compiler_params=params(),
        name="key_grad",
        cost_estimate=takes(2),
    )(blocks, across, grad, parts)


def attn_back_kernel(grad_ref, w_ref, x_ref, part_ref, gain_ref):
    step = pl.program_id(0)
    part = dot_cols(grad_ref[...], w_ref[...])
    part_ref[...] = part.astype(BF16)
    x = x_ref[...].astype(F32)
    sums = jnp.sum(part * (x * inverse_rms(x)), axis=0, keepdims=True)

    @pl.when(step == 0)
    def _():
        gain_ref[...] = sums

    @pl.when(step > 0)
    def _():
        gain_ref[...] += sums


def attn_back(grad, w, x):
    tile = 128
    row = lambda width: pl.BlockSpec((tile, width), lambda i: (i, 0))
    return pl.pallas_call(
        attn_back_kernel,
        grid=(4,),
        in_specs=[row(256), pl.BlockSpec((D, 256), lambda i: (0, 0)), row(D)],
        out_specs=[row(D), pl.BlockSpec((1, D), lambda i: (0, 0))],
        out_shape=[shape((ROWS, D), BF16), shape((1, D), F32)],
        compiler_params=params(),
        name="attn_back",
        cost_estimate=takes(5),
    )(grad, w, x)


def attn_back_rest_kernel(row_ref, grad_ref, w_ref, x_ref, part_ref, out_ref, gain_ref):
    step = pl.program_id(0)
    part = dot_cols(grad_ref[...], w_ref[...])
    x = x_ref[...].astype(F32)
    sums = jnp.sum(part * (x * inverse_rms(x)), axis=0, keepdims=True)
    part = (part + part_ref[...].astype(F32)).astype(BF16)

    @pl.when(step == 0)
    def _():
        gain_ref[...] = sums

    @pl.when(step > 0)
    def _():
        gain_ref[...] += sums

    for half in range(2):
        at = pl.multiple_of(row_ref[2 * step + half] * CH, CH)
        out_ref[pl.ds(at, CH), :] = part[half * CH : (half + 1) * CH]


def attn_back_rest(row_table, grad, w, x, part):
    tile = 128
    row = lambda width: pl.BlockSpec((tile, width), lambda i, r: (i, 0))
    return pl.pallas_call(
        attn_back_rest_kernel,
        grid_spec=pltpu.PrefetchScalarGridSpec(
            num_scalar_prefetch=1,
            grid=(4,),
            in_specs=[row(128), pl.BlockSpec((D, 128), lambda i, r: (0, 2)), row(D), row(D)],
            out_specs=[
                pl.BlockSpec((ROWS, D), lambda i, r: (0, 0)),
                pl.BlockSpec((1, D), lambda i, r: (0, 0)),
            ],
        ),
        out_shape=[shape((ROWS, D), BF16), shape((1, D), F32)],
        compiler_params=params(),
        name="attn_back_rest",
        cost_estimate=takes(4),
    )(row_table, grad, w, x, part)


def weight_grad_kernel(parts, wide, *refs):
    lhs, rhs = refs[:parts], refs[parts : parts + len(wide)]
    out_ref, turned = refs[-2:]
    step = pl.program_id(0)

    @pl.when(step == 0)
    def _():
        rows = ROWS // parts
        for index, ref in enumerate(lhs):
            turned[:, index * rows : (index + 1) * rows] = ref[...].astype(F32).T.astype(BF16)

    start = 0
    for ref, count in zip(rhs, wide, strict=True):

        @pl.when((step >= start) & (step < start + count))
        def _(ref=ref):
            out_ref[...] = jnp.dot(turned[...], ref[...], preferred_element_type=F32).astype(BF16)

        start += count


def weight_grad(lhs, rhs, at, flat=None):
    wide = [a.shape[1] // 256 for a in rhs]
    starts = [sum(wide[:i]) for i in range(len(wide))]
    given = [*lhs, *rhs] + ([] if flat is None else [flat])
    specs = [pl.BlockSpec(a.shape, lambda i: (0, 0)) for a in lhs]
    for start, count in zip(starts, wide, strict=True):
        specs.append(
            pl.BlockSpec(
                (ROWS, 256),
                lambda i, start=start, count=count: (0, jnp.clip(i - start, 0, count - 1)),
            )
        )
    if flat is not None:
        specs.append(pl.BlockSpec(memory_space=pl.ANY))
    return pl.pallas_call(
        functools.partial(weight_grad_kernel, len(lhs), wide),
        grid=(sum(wide),),
        in_specs=specs,
        out_specs=pl.BlockSpec((D, 256), lambda i: (0, at + i)),
        out_shape=shape((D, FLAT_GRAD), BF16),
        scratch_shapes=[pltpu.VMEM((D, ROWS), BF16)],
        input_output_aliases={} if flat is None else {len(given) - 1: 0},
        compiler_params=params(),
        name="weight_grad",
        cost_estimate=takes(1.25 * sum(wide)),
    )(*given)


def keep_kernel(in_ref, out_ref):
    out_ref[...] = in_ref[...]


def keep(a):
    block = pl.BlockSpec((128, D), lambda i: (i, 0))
    return pl.pallas_call(
        keep_kernel,
        grid=(4,),
        in_specs=[block],
        out_specs=block,
        out_shape=shape((ROWS, D), BF16),
        compiler_params=params(),
        name="keep",
        cost_estimate=takes(2),
    )(a)


def step_kernel(wide, *refs):
    count = len(wide)
    squares = []
    for index, (given, start, columns, turned, row) in enumerate(wide):
        weight, first, second = refs[at_of(wide) + 3 * index : at_of(wide) + 3 * index + 3]
        base = at_of(wide) + 3 * count + 3 * index
        first_out, second_out, direction_out = refs[base : base + 3]
        total = None
        for part in range(2 if len(weight.shape) == 3 else 1):
            grad = refs[given][:, start : start + columns].astype(F32)
            start += columns
            if turned:
                grad = grad.T
            pick = (part,) if len(weight.shape) == 3 else (slice(None),)
            first_new, second_new, direction = adapt(weight[pick], first[pick], second[pick], grad)
            first_out[pick] = first_new
            second_out[pick] = second_new
            direction_out[pick] = direction
            sums = column_squares(direction)
            total = sums if total is None else total + sums
        squares.append((row, total))
    refs[-1][...] = eight_rows([dict(squares).get(row) for row in range(8)])


def at_of(wide):
    return 1 + max(entry[0] for entry in wide)


def take_step(grads, matrices, wide):
    given = [*grads, *[a for matrix in matrices for a in matrix]]
    outs = [shape(matrix[0].shape, F32) for matrix in matrices for _ in range(3)]
    out = pl.pallas_call(
        functools.partial(step_kernel, wide),
        grid=(1,),
        in_specs=whole_specs(given),
        out_specs=whole_specs(outs + [shape((8, 128), F32)]),
        out_shape=outs + [shape((8, 128), F32)],
        compiler_params=params(),
        name="take_step",
        cost_estimate=takes(4),
    )(*given)
    return [out[3 * i : 3 * i + 3] for i in range(len(matrices))], out[-1]


def finish_kernel(*refs):
    sums = refs[0]
    weights, directions = refs[1:5], refs[5:9]
    gains = (refs[9:12], refs[12:15])
    outs = refs[15:19]
    gain_outs = (refs[19:22], refs[22:25])
    stats_ref = refs[25]
    row = lax.broadcasted_iota(jnp.int32, (3, 6), 0)
    column = lax.broadcasted_iota(jnp.int32, (3, 6), 1)
    stats = jnp.zeros((3, 6), F32)

    def total(a):
        return jnp.sum(jnp.sum(a, axis=1, keepdims=True), axis=0, keepdims=True)

    def keep(stats, index, weight_norm, step_norm):
        ratio = weight_norm / (step_norm + EPS_ADAM)
        values = jnp.where(row == 0, weight_norm, jnp.where(row == 1, step_norm, ratio))
        return jnp.where(column == index, values, stats), ratio

    for index in range(4):
        weight_norm = jnp.sqrt(total(sums[2:3, 256 + index * 128 : 384 + index * 128]))
        step_norm = jnp.sqrt(total(sums[2:3, 768 + index * 128 : 896 + index * 128]))
        stats, ratio = keep(stats, index, weight_norm, step_norm)
        weight, direction, out = weights[index], directions[index], outs[index]
        if len(weight.shape) == 3:
            for part in range(2):
                out[part] = weight[part] - RATE * ratio * direction[part]
        else:
            out[...] = weight[...] - RATE * ratio * direction[...]
    query_gain = sums[2:3, 0:64] + sums[2:3, 64:128]
    head_grad = jnp.concatenate([query_gain, sums[2:3, 128:192]], axis=0)
    for index, grad in enumerate((sums[0:2, :], head_grad)):
        weight, first, second = (ref[...] for ref in gains[index])
        first_new, second_new, direction = adapt(weight, first, second, grad)
        weight_norm = jnp.sqrt(total(weight * weight))
        step_norm = jnp.sqrt(total(direction * direction))
        stats, ratio = keep(stats, 4 + index, weight_norm, step_norm)
        new_out, first_out, second_out = gain_outs[index]
        new_out[...] = weight - RATE * ratio * direction
        first_out[...] = first_new
        second_out[...] = second_new
    stats_ref[...] = stats


def finish(sums, weights, directions, norm_set, head_set):
    outs = [shape(w.shape, F32) for w in weights]
    outs += [shape(norm_set[0].shape, F32)] * 3 + [shape(head_set[0].shape, F32)] * 3
    outs += [shape((3, 6), F32)]
    given = (sums, *weights, *directions, *norm_set, *head_set)
    return pl.pallas_call(
        finish_kernel,
        grid=(1,),
        in_specs=whole_specs(given),
        out_specs=whole_specs(outs),
        out_shape=outs,
        compiler_params=params(),
        name="finish",
        cost_estimate=takes(3),
    )(*given)


def norm_back(grad_in, normed, inv_scale, gain):
    grad_hat = grad_in * gain
    return inv_scale * (grad_hat - normed * jnp.mean(grad_hat * normed, axis=-1, keepdims=True))


def dot_cols(a, b):
    return lax.dot_general(a, b, (((1,), (1,)), ((), ())), preferred_element_type=F32)


def in_order(a, row_table):
    chunks = a.reshape(8, CH)
    pick = row_table[:, None, None] == jnp.arange(8, dtype=jnp.int32)[None, :, None]
    return jnp.sum(jnp.where(pick, chunks[None], 0), axis=1).reshape(ROWS)


def local(
    tokens,
    segments,
    weight_qkv,
    weight_out,
    weight_gate_up,
    weight_down,
    norm_gains,
    head_gains,
    first_qkv,
    first_out,
    first_gate_up,
    first_down,
    first_norm,
    first_head,
    second_qkv,
    second_out,
    second_gate_up,
    second_down,
    second_norm,
    second_head,
    cotangent,
):
    seg_low = jnp.concatenate([segments >> 6, segments & 63]).astype(BF16).reshape(4, 256)
    seg_low = jnp.pad(seg_low, ((0, 12), (0, 128)))
    qkv_low = weight_qkv.astype(BF16)
    w_first, w_second = gather_both(jnp.concatenate([qkv_low[:64], seg_low], axis=0), qkv_low[64:])

    dp = lax.axis_index("dp")
    tensor = lax.axis_index("tensor")
    y, x = dp >> 2, dp & 3
    z, core = tensor >> 1, tensor & 1
    slots = jnp.arange(8, dtype=jnp.int32)
    row_table = 2 * ((z + slots) & 3) + (core ^ (slots >> 2))
    sixteen = jnp.arange(16, dtype=jnp.int32)
    blocks = ((((sixteen >> 2) + y) & 3) << 2) + ((sixteen + x) & 3)
    blocks_turned = ((((sixteen) + y) & 3) << 2) + (((sixteen >> 2) + x) & 3)
    own_blocks = jnp.stack([dp, 15 - dp])
    zero_slot = ((-y & 3) << 2) + (-x & 3)
    partner_slot = (((3 - 2 * y) & 3) << 2) + ((3 - 2 * x) & 3)

    down_out, gate_up, weight_squares = pack(weight_qkv, weight_out, weight_gate_up, weight_down)
    down_out = lax.all_gather(down_out, "dp", axis=0, tiled=True)
    gate_up = lax.all_gather(gate_up, "dp", axis=0, tiled=True)

    attn_in = prepare(row_table, tokens, norm_gains[0:1])
    token_ids = (row_table[:, None] * CH + jnp.arange(CH, dtype=jnp.int32)[None, :]).reshape(ROWS)
    frequency = ROPE_BASE ** (-(jnp.arange(HD // 2, dtype=F32) * 2.0 / HD))
    angles = (dp * ROWS + token_ids).astype(F32)[:, None] * jnp.tile(frequency, 4)[None, :]
    cosine, sine = jnp.cos(angles), jnp.sin(angles)
    gain_rows = jnp.concatenate(
        [
            jnp.concatenate([head_gains[0:1], head_gains[0:1]], axis=1),
            jnp.concatenate([head_gains[1:2], jnp.ones((1, HD), F32)], axis=1),
            jnp.zeros((6, 128), F32),
        ]
    )
    projected, q_own, q_send, local_kv, full_qkv, all_segs = project(
        blocks, attn_in, w_first, w_second, cosine, sine, gain_rows
    )
    kv_groups, (all_segs, tokens, cotangent) = gather_dp(local_kv, (all_segs, tokens, cotangent))
    kv_groups, (across, x_rows, dy) = beside(
        kv_groups, arrange(row_table, tokens, cotangent, attn_in)
    )

    def block_segs(slot):
        pick = (sixteen == slot)[:, None, None]
        got = jnp.sum(jnp.where(pick, all_segs[:, :4, :256].astype(jnp.int32), 0), axis=0)
        got = got.reshape(2, ROWS)
        return got[0] * 64 + got[1]

    partner_segs = block_segs(partner_slot)
    seg_rows = in_order(segments, row_table)
    first_rows = in_order(block_segs(zero_slot), row_table)
    partner_rows = in_order(partner_segs, row_table)
    kinfo = jnp.stack([seg_rows, partner_rows, first_rows, token_ids], axis=1)
    qinfo = jnp.concatenate(
        [seg_rows[None], partner_rows[None], token_ids[None], jnp.zeros((5, ROWS), jnp.int32)]
    )
    bias = jnp.concatenate(
        [
            jnp.where(seg_rows == segments[0], 0.0, OFF).astype(F32)[None],
            jnp.where(partner_rows == partner_segs[0], 0.0, OFF).astype(F32)[None],
            jnp.zeros((6, ROWS), F32),
        ]
    )
    block_info = jnp.concatenate([blocks, own_blocks])
    mixed, out_own, log_own, out_send, kv_all = attend(
        block_info, q_own, q_send, kv_groups, kinfo, qinfo, bias
    )

    far = out_project(1, mixed, down_out, BF16)
    near = out_project(0, mixed, down_out, F32)
    own_tokens = x_rows[:CH].astype(F32)
    attn_rows, grad_inner = scatter_tensor(near, far, inner_grad(dy, down_out))
    hidden_one = own_tokens + attn_rows
    scale_two = inverse_rms(hidden_one)
    normed_two = hidden_one * scale_two
    ffn_in, (out_other, q_other) = gather_tensor(
        (normed_two * norm_gains[1]).astype(BF16), (from_partner(out_send), from_partner(q_send))
    )
    inner_act, grad_gate, grad_up, near, far = feed_forward(*ffn_in, grad_inner, gate_up)

    grads = weight_grad([dy], [inner_act], 8)
    grads = weight_grad(ffn_in, [grad_gate, grad_up], 0, grads)
    grad_ffn_in, grads = scatter_tensor(near, far, grads)
    grads = lax.psum_scatter(grads, "dp", scatter_dimension=0, tiled=True)
    gain_ffn = jnp.sum(grad_ffn_in * normed_two, axis=0)
    grad_hidden = dy[:CH].astype(F32) + norm_back(grad_ffn_in, normed_two, scale_two, norm_gains[1])
    ffn_parts = ffn_out(inner_act, down_out)
    grad_attn, (ffn_near, ffn_far) = gather_tensor(grad_hidden.astype(BF16), ffn_parts)

    do_own, do_send = mixed_grad(*grad_attn, down_out)
    do_other = from_partner(do_send)
    out_parts = out_grad(blocks, *grad_attn, mixed)
    (do_other, ffn_far), out_parts = beside((do_other, from_core(ffn_far)), out_parts)
    ffn_near = (ffn_near + ffn_far.astype(F32)).reshape(4, CH, D)
    ffn_low = ffn_near.astype(BF16)
    ffn_got = {k: from_z(ffn_low[k], -k) for k in (2, 1, 3)}
    operands = ready(do_own, do_other, out_own, log_own, out_other, q_own, q_other, bias)
    dq_own, dq_send, part_u, part_v = attend_back(block_info, operands, kv_all, kinfo, qinfo)
    dq_send, ffn_got = beside(dq_send, ffn_got)
    dq_other = from_partner(dq_send)
    part_v, dq_other = beside(part_v, dq_other)
    got_u, got_v = send(part_u, from_y), send(part_v, from_x)
    grad_query, gain_query = heads_back(
        (0, 1), projected, [dq_own, dq_other], cosine, sine, gain_rows
    )
    parts = query_out_grad(blocks, across, grad_query, out_parts)
    attn_part, gain_attn = attn_back(grad_query, full_qkv, x_rows)
    (got_u, got_v), (parts, attn_part) = beside((got_u, got_v), (parts, attn_part))
    block_rows = (hidden_one + sum_four(ffn_near[0], ffn_got)).astype(BF16)
    line_u, line_v = sum_four(part_u[0], got_u), sum_four(part_v[0], got_v)
    low_u, low_v = line_u.astype(BF16), line_v.astype(BF16)
    got_u = {k: from_x(low_u[k], -k) for k in (2, 1, 3)}
    got_v = {k: from_y(low_v[k], -k) for k in (2, 1, 3)}
    grad_kv = jnp.concatenate([sum_four(line_u[0], got_u), sum_four(line_v[0], got_v)]).astype(BF16)
    grad_kv, gain_key = heads_back((2,), projected, [grad_kv], cosine, sine, gain_rows)
    parts_u, parts_v = key_grad(blocks, across, grad_kv, parts)
    got_u, got_v = send(parts_u, from_y), send(parts_v, from_x)

    grad_kv, _ = beside(grad_kv, (parts_u, parts_v))
    block_out = keep(lax.all_gather(block_rows, "tensor", axis=0, tiled=True))
    partial, gain_rest = attn_back_rest(row_table, grad_kv, full_qkv, x_rows, attn_part)
    partial, grads = beside(partial, grads)
    grad_attn_in = lax.psum_scatter(partial, "tensor", scatter_dimension=0, tiled=True).astype(F32)
    (gate_up_step, down_step), later_squares = take_step(
        [grads],
        [(weight_gate_up, first_gate_up, second_gate_up), (weight_down, first_down, second_down)],
        ((0, 0, 1024, False, 2), (0, 2048, 1024, True, 3)),
    )
    (got_u, got_v), (later_squares, block_out) = beside((got_u, got_v), (later_squares, block_out))
    late_u = scatter_rest(parts_u[0], got_u, from_x)
    late_v = scatter_rest(parts_v[0], got_v, from_y)
    grad_attn_in, _ = beside(grad_attn_in, (late_u, late_v))
    late_grad = jnp.concatenate([late_u, late_v])
    scale_one = inverse_rms(own_tokens)
    normed_one = own_tokens * scale_one
    input_grad = (
        grad_hidden + norm_back(grad_attn_in, normed_one, scale_one, norm_gains[0])
    ).astype(BF16)
    input_grad = lax.all_gather(input_grad, "tensor", axis=0, tiled=True)

    (qkv_step, out_step), qkv_squares = take_step(
        [jnp.concatenate([late_grad[:, :256], late_grad[:, 512:]], axis=1), late_grad],
        [(weight_qkv, first_qkv, second_qkv), (weight_out, first_out, second_out)],
        ((0, 0, 384, False, 0), (1, 256, 256, True, 1)),
    )
    squares = jnp.concatenate(
        [
            gain_query[0:1],
            gain_key[0:1],
            weight_squares[:4].reshape(1, 512),
            (later_squares + qkv_squares)[:4].reshape(1, 512),
            jnp.zeros((1, D - 1280), F32),
        ],
        axis=1,
    )
    sums = jnp.concatenate([gain_attn + gain_rest, gain_ffn[None], squares, jnp.zeros((1, D), F32)])
    sums = sum_all(sums)
    steps = (qkv_step, out_step, gate_up_step, down_step)
    done = finish(
        sums,
        (weight_qkv, weight_out, weight_gate_up, weight_down),
        [step[2] for step in steps],
        (norm_gains, first_norm, second_norm),
        (head_gains, first_head, second_head),
    )
    return (
        block_out,
        input_grad,
        *done[:4],
        done[4],
        done[7],
        *[step[0] for step in steps],
        done[5],
        done[8],
        *[step[1] for step in steps],
        done[6],
        done[9],
        done[10],
    )


def solution(mesh):
    matrix_specs = (P("dp", "tensor"), P("tensor", "dp"), P(None, "dp", "tensor"), P("tensor", "dp"), P(), P())
    in_specs = (P("dp", None), P("dp"), *matrix_specs, *matrix_specs, *matrix_specs, P("dp", None))
    out_specs = (P("dp", None), P("dp", None), *matrix_specs, *matrix_specs, *matrix_specs, P())
    return jax.shard_map(local, mesh=mesh, in_specs=in_specs, out_specs=out_specs, check_vma=False)
```

```python
import functools

import jax
import jax.numpy as jnp
from jax import lax
from jax.experimental import pallas as pl
from jax.experimental.pallas import tpu as pltpu
from jax.sharding import PartitionSpec as P

H = 32
KVH = 8
HD = 64
STEP = 5
D = 2048
ROWS = 512
QPK = 4
CH = 64
FLAT_GRAD = 2048 + 1024

EPS_NORM = 1e-05
ROPE_BASE = 1000000.0
BETA_ONE = 0.5
BETA_TWO = 0.5
EPS_ADAM = 1e-06
DECAY = 0.01
RATE = 0.5
F32 = jnp.float32
BF16 = jnp.bfloat16
OFF = -1e5
VMEM_LIMIT = 24 * 1024 * 1024
VMEM_LARGE = 44 * 1024 * 1024


def inverse_rms(array_in):
    return lax.rsqrt(jnp.mean(array_in * array_in, axis=-1, keepdims=True) + EPS_NORM)


def adapt(weight, first_old, second_old, grad_in):
    first_new = BETA_ONE * first_old + (1.0 - BETA_ONE) * grad_in
    second_new = BETA_TWO * second_old + (1.0 - BETA_TWO) * grad_in * grad_in
    direction = (
        first_new
        / (1.0 - BETA_ONE**STEP)
        / (jnp.sqrt(second_new / (1.0 - BETA_TWO**STEP)) + EPS_ADAM)
        + DECAY * weight
    )
    return (first_new, second_new, direction)


def perm_x(k):
    return [(i, (i // 4) * 4 + (i % 4 - k) % 4) for i in range(16)]


def perm_y(k):
    return [(i, ((i // 4 - k) % 4) * 4 + i % 4) for i in range(16)]


def perm_z(k):
    return [(i, ((i // 2 - k) % 4) * 2 + i % 2) for i in range(8)]


PERM_CORE = [(i, i ^ 1) for i in range(8)]
PERM_PARTNER = [(i, 15 - i) for i in range(16)]


def from_x(a, k):
    return lax.ppermute(a, "dp", perm_x(k))


def from_y(a, k):
    return lax.ppermute(a, "dp", perm_y(k))


def from_z(a, k):
    return lax.ppermute(a, "tensor", perm_z(k))


def from_core(a):
    return lax.ppermute(a, "tensor", PERM_CORE)


def from_partner(a):
    return lax.ppermute(a, "dp", PERM_PARTNER)


def beside(arrays, work):
    return lax.optimization_barrier((arrays, work))


def gather_both(u, v):
    row = {k: from_x(u, k) for k in (2, 1, 3)}
    column = {k: from_y(v, k) for k in (2, 1, 3)}
    row = jnp.stack([u, row[1], row[2], row[3]])
    column = jnp.stack([v, column[1], column[2], column[3]])
    second = {k: (from_y(row, k), from_x(column, k)) for k in (2, 1, 3)}
    first = [row] + [second[k][0] for k in (1, 2, 3)]
    return first, [column] + [second[k][1] for k in (1, 2, 3)]


def gather_dp(a, later):
    row = {k: from_x(a, k) for k in (2, 1, 3)}
    row, later = beside(row, later)
    row = jnp.stack([a, row[1], row[2], row[3]])
    second = {k: from_y(row, k) for k in (2, 1, 3)}
    return [row] + [second[k] for k in (1, 2, 3)], later


def sum_four(own, got):
    return (own.astype(F32) + got[2].astype(F32)) + (got[1].astype(F32) + got[3].astype(F32))


def send(parts, step):
    return {k: step(parts[k], -k) for k in (2, 1, 3)}


def scatter_rest(own, got, step):
    line = sum_four(own, got)
    low = line.astype(BF16)
    return sum_four(line[0], {k: step(low[k], -k) for k in (2, 1, 3)})


def scatter_tensor(near, far, work=None):
    near = near.astype(F32) + from_core(far.astype(BF16)).astype(F32)
    parts = near.reshape(4, CH, near.shape[-1])
    low = parts.astype(BF16)
    got = {k: from_z(low[k], -k) for k in (2, 1, 3)}
    if work is None:
        return sum_four(parts[0], got)
    got, work = beside(got, work)
    return sum_four(parts[0], got), work


def gather_tensor(a, work=None):
    got = {k: from_z(a, k) for k in (2, 1, 3)}
    if work is not None:
        got, work = beside(got, work)
    near = jnp.concatenate([a, got[1], got[2], got[3]], axis=0)
    halves = (near, from_core(near))
    return halves if work is None else (halves, work)


def sum_all(a):
    for step in (from_x, from_y, from_z):
        a = (a + step(a, 2)) + (step(a, 1) + step(a, 3))
    return a + from_core(a)


def params(vmem=VMEM_LIMIT):
    return pltpu.CompilerParams(vmem_limit_bytes=vmem)


def takes(us):
    return pl.CostEstimate(flops=int(us * 1.1e9), bytes_accessed=0, transcendentals=0)


def whole_specs(arrays):
    return [pl.BlockSpec(a.shape, lambda i, n=len(a.shape): (0,) * n) for a in arrays]


def prepare_kernel(row_ref, tok_ref, gain_ref, in_ref):
    x = tok_ref[...].astype(F32)
    in_ref[...] = (x * inverse_rms(x) * gain_ref[...]).astype(BF16)


def prepare(row_table, tokens, gain):
    return pl.pallas_call(
        prepare_kernel,
        grid_spec=pltpu.PrefetchScalarGridSpec(
            num_scalar_prefetch=1,
            grid=(8,),
            in_specs=[
                pl.BlockSpec((CH, D), lambda i, r: (r[i], 0)),
                pl.BlockSpec((1, D), lambda i, r: (0, 0)),
            ],
            out_specs=pl.BlockSpec((CH, D), lambda i, r: (i, 0)),
        ),
        out_shape=jax.ShapeDtypeStruct((ROWS, D), BF16),
        compiler_params=params(),
        name="prepare",
        cost_estimate=takes(4),
    )(row_table, tokens, gain)


def arrange_kernel(row_ref, tok_ref, cot_ref, in_ref, across_ref, x_ref, dy_ref):
    x_ref[...] = tok_ref[...]
    dy_ref[...] = cot_ref[...]

    @pl.when(pl.program_id(0) % 2 == 0)
    def _():
        across_ref[...] = in_ref[...].astype(F32).T.astype(BF16)


def arrange(row_table, tokens, cotangent, attn_in):
    pick = pl.BlockSpec((CH, D), lambda i, r: (r[i], 0))
    put = pl.BlockSpec((CH, D), lambda i, r: (i, 0))
    return pl.pallas_call(
        arrange_kernel,
        grid_spec=pltpu.PrefetchScalarGridSpec(
            num_scalar_prefetch=1,
            grid=(8,),
            in_specs=[pick, pick, pl.BlockSpec((128, D), lambda i, r: (i // 2, 0))],
            out_specs=[pl.BlockSpec((D, 128), lambda i, r: (0, i // 2)), put, put],
        ),
        out_shape=[
            jax.ShapeDtypeStruct((D, ROWS), BF16),
            jax.ShapeDtypeStruct((ROWS, D), BF16),
            jax.ShapeDtypeStruct((ROWS, D), BF16),
        ],
        compiler_params=params(),
        name="arrange",
        cost_estimate=takes(7),
    )(row_table, tokens, cotangent, attn_in)


def lane_of(shape):
    return lax.broadcasted_iota(jnp.int32, shape, len(shape) - 1)


def head_sums(a, low_half):
    left = jnp.sum(jnp.where(low_half, a, 0.0), axis=-1, keepdims=True)
    right = jnp.sum(jnp.where(low_half, 0.0, a), axis=-1, keepdims=True)
    return jnp.where(low_half, left, right)


def turn(a, first):
    return jnp.where(first, pltpu.roll(a, 96, 1), pltpu.roll(a, 32, 1))


def vmem_specs(count):
    return [pl.BlockSpec(memory_space=pltpu.VMEM)] * count


def shape(dims, kind):
    return jax.ShapeDtypeStruct(dims, kind)


def column_squares(a):
    total = None
    for at in range(0, a.shape[-1], 128):
        part = a[:, at : at + 128]
        part = jnp.sum(part * part, axis=0, keepdims=True)
        total = part if total is None else total + part
    return total


def eight_rows(rows):
    row = lax.broadcasted_iota(jnp.int32, (8, 128), 0)
    out = jnp.zeros((8, 128), F32)
    for index, value in enumerate(rows):
        if value is not None:
            out = jnp.where(row == index, value, out)
    return out


def pack_kernel(qkv_in, out_in, gate_up_in, down_in, first_ref, second_ref, squares_ref, qkv, out_w, gate_up, down, sems):
    pairs = ((down_in, down), (out_in, out_w), (gate_up_in, gate_up), (qkv_in, qkv))
    copies = [pltpu.make_async_copy(a, b, sems.at[i]) for i, (a, b) in enumerate(pairs)]
    for copy in copies:
        copy.start()
    copies[0].wait()
    first_ref[:, :1024] = down[...].T.astype(BF16)
    copies[1].wait()
    first_ref[:, 1024:] = out_w[...].T.astype(BF16)
    copies[2].wait()
    second_ref[:, :1024] = gate_up[0].astype(BF16)
    second_ref[:, 1024:] = gate_up[1].astype(BF16)
    copies[3].wait()
    squares_ref[...] = eight_rows(
        [
            column_squares(qkv[...]),
            column_squares(out_w[...]),
            column_squares(gate_up[0]) + column_squares(gate_up[1]),
            column_squares(down[...]),
        ]
    )


def pack(weight_qkv, weight_out, weight_gate_up, weight_down):
    given = (weight_qkv, weight_out, weight_gate_up, weight_down)
    return pl.pallas_call(
        pack_kernel,
        in_specs=[pl.BlockSpec(memory_space=pl.ANY)] * 4,
        out_specs=vmem_specs(3),
        out_shape=[shape((128, 1280), BF16), shape((128, 2048), BF16), shape((8, 128), F32)],
        scratch_shapes=[pltpu.VMEM(a.shape, F32) for a in given] + [pltpu.SemaphoreType.DMA((4,))],
        compiler_params=params(60 * 1024 * 1024),
        name="pack",
        cost_estimate=takes(2),
    )(*given)


def project_kernel(
    blk_ref, x_ref, u0, u1, u2, u3, v0, v1, v2, v3, cos_ref, sin_ref, gain_ref,
    proj_ref, q_own_ref, q_send_ref, kv_ref, w_ref, seg_ref,
):
    @pl.when(pl.program_id(0) == 0)
    def _():
        for at_y in range(4):
            for at_x in range(4):
                slot = at_y * 4 + at_x
                start = pl.multiple_of(blk_ref[slot] * 128, 128)
                w_ref[pl.ds(start, 64), :] = (u0, u1, u2, u3)[at_y][at_x, :64, :]
                w_ref[pl.ds(start + 64, 64), :] = (v0, v1, v2, v3)[at_x][at_y]
                seg_ref[slot] = (u0, u1, u2, u3)[at_y][at_x, 64:, :]

    acc = jnp.dot(x_ref[...], w_ref[...], preferred_element_type=F32)
    proj_ref[...] = acc
    lane = lane_of((x_ref.shape[0], 128))
    low_half = lane < 64
    first = (lane & 63) < 32
    cosine = cos_ref[...]
    sine = jnp.where(first, -sin_ref[...], sin_ref[...])
    for pair in range(3):
        u = acc[:, pair * 128 : (pair + 1) * 128]
        scale = lax.rsqrt(head_sums(u * u, low_half) * (1.0 / HD) + EPS_NORM)
        hat = u * scale * gain_ref[pair // 2 : pair // 2 + 1, :]
        turned = hat * cosine + turn(hat, first) * sine
        if pair < 2:
            across = (turned.astype(BF16).astype(F32) * 0.125).T.astype(BF16)
            out = (q_own_ref, q_send_ref)[pair]
            out[0] = across[:64]
            out[1] = across[64:]
        else:
            kv_ref[...] = jnp.where(low_half, turned, u).astype(BF16)


def project(blocks, x, w_first, w_second, cosine, sine, gains):
    tile = 128
    whole = lambda dims: pl.BlockSpec(dims, lambda i, b: (0,) * len(dims))
    row = lambda width: pl.BlockSpec((tile, width), lambda i, b: (i, 0))
    pair = pl.BlockSpec((2, HD, tile), lambda i, b: (0, 0, i))
    return pl.pallas_call(
        project_kernel,
        grid_spec=pltpu.PrefetchScalarGridSpec(
            num_scalar_prefetch=1,
            grid=(ROWS // tile,),
            in_specs=[row(D)]
            + [whole((4, 80, 384))] * 4
            + [whole((4, 64, 384))] * 4
            + [row(128), row(128), whole((8, 128))],
            out_specs=[row(384), pair, pair, row(128), whole((D, 384)), whole((16, 16, 384))],
        ),
        out_shape=[
            shape((ROWS, 384), F32),
            shape((2, HD, ROWS), BF16),
            shape((2, HD, ROWS), BF16),
            shape((ROWS, 128), BF16),
            shape((D, 384), BF16),
            shape((16, 16, 384), BF16),
        ],
        compiler_params=params(),
        name="project",
        cost_estimate=takes(6),
    )(blocks, x, *w_first, *w_second, cosine, sine, gains)


def lane_masks():
    low = (lane_of((1, 128)) < 64).astype(F32)
    return low.astype(BF16), (1.0 - low).astype(BF16)


def allowed_keys(queries, is_own, at, count, kinfo_ref, qinfo_ref):
    info = kinfo_ref[pl.ds(at, count), :]
    seg = jnp.where(is_own, info[:, queries : queries + 1], info[:, 2:3])
    pos = jnp.where(is_own, info[:, 3:4], -1)
    return (seg == qinfo_ref[queries : queries + 1, :]) & (pos <= qinfo_ref[2:3, :])


def for_queries(blk_ref, slot, own_at, sets, work):
    block = blk_ref[slot]
    for queries in range(sets):
        own = blk_ref[own_at + queries]

        @pl.when((block == 0) | (block == own))
        def _(queries=queries, own=own):
            work(queries, True, block == own)

        @pl.when((block > 0) & (block < own))
        def _(queries=queries):
            work(queries, False, None)


def forward_kernel(
    blk_ref, q_first, q_second, kv0, kv1, kv2, kv3, kinfo_ref, qinfo_ref, bias_ref,
    mixed_ref, out_ref, lse_ref, send_ref, kv_all, q_t, acc,
):
    for group, ref in enumerate((kv0, kv1, kv2, kv3)):
        kv_all[group * 4 : (group + 1) * 4] = ref[...]
    acc[...] = jnp.zeros_like(acc)
    row = lax.broadcasted_iota(jnp.int32, (64, ROWS), 0)
    bias = jnp.where(row == 0, bias_ref[0:1, :], 0.0).astype(BF16)
    for head in range(QPK):
        q_t[head, :64, :] = (q_first, q_second)[head // 2][head % 2]
        q_t[head, 64:, :] = bias
    keep_k, keep_v = lane_masks()

    def step(slot, carry):
        def work(queries, masked, is_own):
            kv = kv_all[slot]
            keys = kv * keep_k + (keep_v if not masked else jnp.zeros_like(keep_v))
            vals = (kv * keep_v + keep_k).astype(F32).T.astype(BF16)[56:]
            if masked:
                allowed = allowed_keys(queries, is_own, 0, ROWS, kinfo_ref, qinfo_ref)
            for head in range(QPK):
                scores = jnp.dot(keys, q_t[head], preferred_element_type=F32)
                probs = jnp.exp(scores)
                if masked:
                    probs = jnp.where(allowed, probs, 0.0)
                acc[head] += jnp.dot(vals, probs.astype(BF16), preferred_element_type=F32)

        for_queries(blk_ref, slot, 16, 1, work)
        return carry

    lax.fori_loop(0, 16, step, 0)
    heads = []
    logs = []
    for head in range(QPK):
        total = acc[head, 0:1, :]
        heads.append(acc[head, 8:, :] / total)
        logs.append(jnp.log(total))
    mixed_ref[...] = jnp.concatenate(heads, axis=0).T.astype(BF16)
    rest = jnp.zeros((6, ROWS), F32)
    out_ref[:64], out_ref[64:] = heads[0], heads[1]
    lse_ref[...] = jnp.concatenate(logs[:2] + [rest], axis=0)
    send_ref[:64], send_ref[64:128] = heads[2], heads[3]
    send_ref[128:136] = jnp.concatenate(logs[2:] + [rest], axis=0)
    send_ref[136:200], send_ref[200:] = q_second[0].astype(F32), q_second[1].astype(F32)


def attend(blocks, q_first, q_second, kv, kinfo, qinfo, bias):
    return pl.pallas_call(
        forward_kernel,
        in_specs=[pl.BlockSpec(memory_space=pltpu.SMEM)] + vmem_specs(9),
        out_specs=vmem_specs(5),
        out_shape=[
            shape((ROWS, 256), BF16),
            shape((128, ROWS), F32),
            shape((8, ROWS), F32),
            shape((264, ROWS), F32),
            shape((16, ROWS, 128), BF16),
        ],
        scratch_shapes=[
            pltpu.VMEM((QPK, 128, ROWS), BF16),
            pltpu.VMEM((QPK, 72, ROWS), F32),
        ],
        compiler_params=params(VMEM_LARGE),
        name="attend",
        cost_estimate=takes(20),
    )(blocks, q_first, q_second, *kv, kinfo, qinfo, bias)


def three_rows(row, value, at):
    high = value.astype(BF16).astype(F32)
    rest = value - high
    middle = rest.astype(BF16).astype(F32)
    low = rest - middle
    return (
        jnp.where(row == at, high, 0.0)
        + jnp.where(row == at + 1, middle, 0.0)
        + jnp.where(row == at + 2, low, 0.0)
    )


def mixed_grad_kernel(near_ref, far_ref, w_ref, own_ref, send_ref):
    w = w_ref[...]
    for half, ref in enumerate((near_ref, far_ref)):
        part = jnp.dot(ref[...], w, preferred_element_type=F32).astype(BF16)
        own_ref[half * 256 : (half + 1) * 256] = part[:, :128]
        send_ref[half * 256 : (half + 1) * 256] = part[:, 128:]


def mixed_grad(near, far, down_out):
    whole = lambda dims: pl.BlockSpec(dims, lambda i: (0, 0))
    return pl.pallas_call(
        mixed_grad_kernel,
        grid=(1,),
        in_specs=[whole((256, D)), whole((256, D)), pl.BlockSpec((D, 256), lambda i: (0, 4))],
        out_specs=[whole((ROWS, 128))] * 2,
        out_shape=[shape((ROWS, 128), BF16)] * 2,
        compiler_params=params(),
        name="mixed_grad",
        cost_estimate=takes(2),
    )(near, far, down_out)


def ready_kernel(do_own, do_other, out_own, lse_own, out_other, q_own, bias_ref, q_t, do_t, q_pad, do_pad):
    row = lax.broadcasted_iota(jnp.int32, (64, ROWS), 0)
    low_half = lane_of((ROWS, 128)) < 64
    for queries in range(2):
        do = (do_own, do_other)[queries][...].astype(F32)
        if queries:
            across = out_other[136:264, :]
        else:
            across = jnp.concatenate([q_own[0].astype(F32), q_own[1].astype(F32)], axis=0)
        q = across.T
        do_turned = do.T
        dots = do_turned * (out_own, out_other)[queries][:128, :]
        for part in range(2):
            head = 2 * queries + part
            at = slice(part * 64, (part + 1) * 64)
            delta = jnp.sum(dots[at, :], axis=0, keepdims=True)
            lse = (out_other[128 + part : 129 + part, :] if queries else lse_own[part : part + 1, :])
            extra = three_rows(row, -lse, 0)
            extra = extra + jnp.where(row == 3, bias_ref[queries : queries + 1, :], 0.0)
            q_t[head, :64, :] = across[at, :].astype(BF16)
            q_t[head, 64:, :] = extra.astype(BF16)
            do_t[head, :64, :] = three_rows(row, -delta, 0).astype(BF16)
            do_t[head, 64:, :] = do_turned[at, :].astype(BF16)
            q_head = pltpu.roll(q, 64, 1) if part else q
            do_head = do if part else pltpu.roll(do, 64, 1)
            q_pad[head] = jnp.where(low_half, q_head, 0.0).astype(BF16)
            do_pad[head] = jnp.where(low_half, 0.0, do_head).astype(BF16)


def ready(*given):
    return pl.pallas_call(
        ready_kernel,
        in_specs=vmem_specs(len(given)),
        out_specs=vmem_specs(4),
        out_shape=[shape((QPK, 128, ROWS), BF16)] * 2 + [shape((QPK, ROWS, 128), BF16)] * 2,
        compiler_params=params(),
        name="ready",
        cost_estimate=takes(2.5),
    )(*given)


def backward_kernel(
    blk_ref, q_t, do_t, q_pad, do_pad, kv_all, kinfo_ref, qinfo_ref, own_ref, other_ref, u_ref, v_ref, dq_t, total
):
    dq_t[...] = jnp.zeros_like(dq_t)
    keep_k, keep_v = lane_masks()
    keep_v_masked = jnp.where(lane_of((1, 128)) == 67, 0.0, keep_v.astype(F32)).astype(BF16)

    def step(slot, carry):
        total[...] = jnp.zeros_like(total)

        def work(queries, masked, is_own):
            kv = kv_all[slot]
            keys = kv * keep_k + (keep_v_masked if masked else keep_v)
            vals = kv * keep_v + keep_k
            keys_turned = kv.astype(F32).T[:64, :].astype(BF16)
            if masked:
                allowed = allowed_keys(queries, is_own, 0, ROWS, kinfo_ref, qinfo_ref)
            for head in (2 * queries, 2 * queries + 1):
                scores = jnp.dot(keys, q_t[head], preferred_element_type=F32)
                probs = jnp.exp(scores)
                if masked:
                    probs = jnp.where(allowed, probs, 0.0)
                grads = jnp.dot(vals, do_t[head], preferred_element_type=F32)
                grads = (probs * grads).astype(BF16)
                term = jnp.dot(probs.astype(BF16), do_pad[head], preferred_element_type=F32)
                total[...] += term + jnp.dot(grads, q_pad[head], preferred_element_type=F32)
                dq_t[head * 64 : (head + 1) * 64, :] += jnp.dot(
                    keys_turned, grads, preferred_element_type=F32
                )

        for_queries(blk_ref, slot, 16, 2, work)
        u_ref[slot // 4, slot % 4] = total[:256].astype(BF16)
        v_ref[slot % 4, slot // 4] = total[256:].astype(BF16)
        return carry

    lax.fori_loop(0, 16, step, 0)
    dq = (dq_t[...].T * 0.125).astype(BF16)
    own_ref[...] = dq[:, :128]
    other_ref[...] = dq[:, 128:]


def attend_back(blocks, operands, kv, kinfo, qinfo):
    pair = shape((ROWS, 128), BF16)
    half = shape((4, 4, 256, 128), BF16)
    return pl.pallas_call(
        backward_kernel,
        in_specs=[pl.BlockSpec(memory_space=pltpu.SMEM)] + vmem_specs(7),
        out_specs=vmem_specs(4),
        out_shape=[pair, pair, half, half],
        scratch_shapes=[pltpu.VMEM((256, ROWS), F32), pltpu.VMEM((ROWS, 128), F32)],
        compiler_params=params(VMEM_LARGE),
        name="attend_back",
        cost_estimate=takes(36),
    )(blocks, *operands, kv, kinfo, qinfo)


def heads_back_kernel(pairs, proj_ref, *refs):
    grads = refs[: len(pairs)]
    cos_ref, sin_ref, gain_ref, out_ref, sum_ref = refs[len(pairs) :]
    lane = lane_of((proj_ref.shape[0], 128))
    low_half = lane < 64
    first = (lane & 63) < 32
    cosine = cos_ref[...]
    sine = jnp.where(first, sin_ref[...], -sin_ref[...])
    sums = None
    for index, pair in enumerate(pairs):
        u = proj_ref[:, pair * 128 : (pair + 1) * 128]
        grad = grads[index][...].astype(F32)
        scale = lax.rsqrt(head_sums(u * u, low_half) * (1.0 / HD) + EPS_NORM)
        hat = u * scale
        turned = grad * cosine + turn(grad, first) * sine
        part = jnp.sum(turned * hat, axis=0, keepdims=True)
        sums = part if sums is None else sums + part
        grad_hat = turned * gain_ref[pair // 2 : pair // 2 + 1, :]
        mean = head_sums(grad_hat * hat, low_half) * (1.0 / HD)
        back = scale * (grad_hat - hat * mean)
        if pair == 2:
            back = jnp.where(low_half, back, grad)
        out_ref[:, index * 128 : (index + 1) * 128] = back.astype(BF16)

    @pl.when(pl.program_id(0) == 0)
    def _():
        sum_ref[...] = jnp.zeros_like(sum_ref)

    sum_ref[0:1, :] += sums


def heads_back(pairs, proj, grads, cosine, sine, gains):
    tile = 128
    row = lambda width: pl.BlockSpec((tile, width), lambda i: (i, 0))
    whole = pl.BlockSpec((8, 128), lambda i: (0, 0))
    wide = 128 * len(pairs)
    return pl.pallas_call(
        functools.partial(heads_back_kernel, pairs),
        grid=(ROWS // tile,),
        in_specs=[row(384)] + [row(128)] * (len(pairs) + 2) + [whole],
        out_specs=[row(wide), whole],
        out_shape=[shape((ROWS, wide), BF16), shape((8, 128), F32)],
        compiler_params=params(),
        name="heads_back",
        cost_estimate=takes(len(pairs)),
    )(proj, *grads, cosine, sine, gains)


def out_kernel(mixed_ref, w_ref, out_ref):
    out_ref[...] = dot_cols(mixed_ref[...], w_ref[...]).astype(out_ref.dtype)


def out_project(half, mixed, down_out, kind):
    return pl.pallas_call(
        out_kernel,
        grid=(1,),
        in_specs=[
            pl.BlockSpec((256, 256), lambda i: (half, 0)),
            pl.BlockSpec((D, 256), lambda i: (0, 4)),
        ],
        out_specs=pl.BlockSpec((256, D), lambda i: (0, 0)),
        out_shape=shape((256, D), kind),
        compiler_params=params(),
        name="out_project",
        cost_estimate=takes(1.8),
    )(mixed, down_out)


def ffn_kernel(
    near_ref, far_ref, grad_ref, w_in, act_ref, gate_ref, up_ref, near_out, far_out, w, x_all, both, sems
):
    tiles = []
    for tile in range(4):
        at = (slice(tile * 256, (tile + 1) * 256), slice(1024 + tile * 256, 1024 + (tile + 1) * 256))
        pair = [
            pltpu.make_async_copy(w_in.at[:, part], w.at[:, part], sems.at[2 * tile + i])
            for i, part in enumerate(at)
        ]
        for copy in pair:
            copy.start()
        tiles.append((at, pair))
    x_all[:256] = near_ref[...]
    x_all[256:] = far_ref[...]
    for (gate_at, up_at), pair in tiles:
        for copy in pair:
            copy.wait()
        x = x_all[...]
        gate = jnp.dot(x, w[:, gate_at], preferred_element_type=F32)
        up = jnp.dot(x, w[:, up_at], preferred_element_type=F32)
        inner = grad_ref[:, gate_at]
        sigmoid = jax.nn.sigmoid(gate)
        activated = gate * sigmoid
        act_ref[:, gate_at] = (activated * up).astype(BF16)
        grad_gate = (inner * up * sigmoid * (1.0 + gate * (1.0 - sigmoid))).astype(BF16)
        grad_up = (inner * activated).astype(BF16)
        gate_ref[:, gate_at] = grad_gate
        up_ref[:, gate_at] = grad_up
        both[:, gate_at] = grad_gate
        both[:, up_at] = grad_up
    for tile in range(4):
        at = slice(tile * 512, (tile + 1) * 512)
        part = dot_cols(both[...], w[at, :])
        near_out[:, at] = part[:256]
        far_out[:, at] = part[256:].astype(BF16)


def feed_forward(near, far, grad_inner, gate_up):
    return pl.pallas_call(
        ffn_kernel,
        in_specs=vmem_specs(3) + [pl.BlockSpec(memory_space=pl.ANY)],
        out_specs=vmem_specs(5),
        out_shape=[shape((ROWS, 1024), BF16)] * 3 + [shape((256, D), F32), shape((256, D), BF16)],
        scratch_shapes=[
            pltpu.VMEM((D, 2048), BF16),
            pltpu.VMEM((ROWS, D), BF16),
            pltpu.VMEM((ROWS, 2048), BF16),
            pltpu.SemaphoreType.DMA((8,)),
        ],
        compiler_params=params(VMEM_LARGE),
        name="feed_forward",
        cost_estimate=takes(13),
    )(near, far, grad_inner, gate_up)


def inner_grad_kernel(dy_ref, w_ref, out_ref):
    out_ref[...] = jnp.dot(dy_ref[...], w_ref[...], preferred_element_type=F32)


def inner_grad(dy, down_out):
    return pl.pallas_call(
        inner_grad_kernel,
        grid=(4,),
        in_specs=[
            pl.BlockSpec((ROWS, D), lambda j: (0, 0)),
            pl.BlockSpec((D, 256), lambda j: (0, j)),
        ],
        out_specs=pl.BlockSpec((ROWS, 256), lambda j: (0, j)),
        out_shape=shape((ROWS, 1024), F32),
        compiler_params=params(),
        name="inner_grad",
        cost_estimate=takes(5.5),
    )(dy, down_out)


def ffn_out_kernel(act_ref, w_ref, near_ref, far_ref, acc):
    step = pl.program_id(0)
    term = dot_cols(act_ref[...], w_ref[...])

    @pl.when(step == 0)
    def _():
        acc[...] = term

    @pl.when(step > 0)
    def _():
        acc[...] += term

    @pl.when(step == pl.num_programs(0) - 1)
    def _():
        near_ref[...] = acc[:256]
        far_ref[...] = acc[256:].astype(BF16)


def ffn_out(act, down_out):
    whole = lambda dims: pl.BlockSpec(dims, lambda j: (0, 0))
    return pl.pallas_call(
        ffn_out_kernel,
        grid=(4,),
        in_specs=[
            pl.BlockSpec((ROWS, 256), lambda j: (0, j)),
            pl.BlockSpec((D, 256), lambda j: (0, j)),
        ],
        out_specs=[whole((256, D)), whole((256, D))],
        out_shape=[shape((256, D), F32), shape((256, D), BF16)],
        scratch_shapes=[pltpu.VMEM((ROWS, D), F32)],
        compiler_params=params(),
        name="ffn_out",
        cost_estimate=takes(6.5),
    )(act, down_out)


def out_grad_kernel(blk_ref, near_ref, far_ref, mixed_ref, out_ref, turned):
    turned[:, :256] = near_ref[...].astype(F32).T.astype(BF16)
    turned[:, 256:] = far_ref[...].astype(F32).T.astype(BF16)
    mixed = mixed_ref[...]
    for slot in range(16):
        at = pl.ds(pl.multiple_of(blk_ref[slot] * 128, 128), 128)
        out = jnp.dot(turned[at, :], mixed, preferred_element_type=F32)
        out_ref[slot // 4, slot % 4] = out.astype(BF16)


def out_grad(blocks, near, far, mixed):
    return pl.pallas_call(
        out_grad_kernel,
        in_specs=[pl.BlockSpec(memory_space=pltpu.SMEM)] + vmem_specs(3),
        out_specs=vmem_specs(1)[0],
        out_shape=shape((4, 4, 128, 256), BF16),
        scratch_shapes=[pltpu.VMEM((D, ROWS), BF16)],
        compiler_params=params(),
        name="out_grad",
        cost_estimate=takes(2),
    )(blocks, near, far, mixed)


def query_out_grad_kernel(blk_ref, across_ref, grad_ref, parts_ref, out_ref):
    grad = grad_ref[...]
    for slot in range(16):
        at = pl.ds(pl.multiple_of(blk_ref[slot] * 128, 128), 128)
        part = jnp.dot(across_ref[at, :], grad, preferred_element_type=F32)
        out_ref[slot // 4, slot % 4, :, :256] = part.astype(BF16)
        out_ref[slot // 4, slot % 4, :, 256:] = parts_ref[slot // 4, slot % 4]


def query_out_grad(blocks, across, grad, out_parts):
    return pl.pallas_call(
        query_out_grad_kernel,
        in_specs=[pl.BlockSpec(memory_space=pltpu.SMEM)] + vmem_specs(3),
        out_specs=vmem_specs(1)[0],
        out_shape=shape((4, 4, 128, 512), BF16),
        compiler_params=params(),
        name="query_out_grad",
        cost_estimate=takes(2),
    )(blocks, across, grad, out_parts)


def key_grad_kernel(blk_ref, across_ref, grad_ref, parts_ref, u_ref, v_ref):
    grad = grad_ref[...]
    for slot in range(16):
        at_y, at_x = slot // 4, slot % 4
        at = pl.ds(pl.multiple_of(blk_ref[slot] * 128, 128), 128)
        part = jnp.dot(across_ref[at, :], grad, preferred_element_type=F32).astype(BF16)
        u_ref[at_y, at_x, :, :512] = parts_ref[at_y, at_x, :64]
        u_ref[at_y, at_x, :, 512:] = part[:64]
        v_ref[at_x, at_y, :, :512] = parts_ref[at_y, at_x, 64:]
        v_ref[at_x, at_y, :, 512:] = part[64:]


def key_grad(blocks, across, grad, parts):
    return pl.pallas_call(
        key_grad_kernel,
        in_specs=[pl.BlockSpec(memory_space=pltpu.SMEM)] + vmem_specs(3),
        out_specs=vmem_specs(2),
        out_shape=[shape((4, 4, 64, 640), BF16)] * 2,
        compiler_params=params(),
        name="key_grad",
        cost_estimate=takes(2),
    )(blocks, across, grad, parts)


def attn_back_kernel(grad_ref, w_ref, x_ref, part_ref, gain_ref):
    step = pl.program_id(0)
    part = dot_cols(grad_ref[...], w_ref[...])
    part_ref[...] = part.astype(BF16)
    x = x_ref[...].astype(F32)
    sums = jnp.sum(part * (x * inverse_rms(x)), axis=0, keepdims=True)

    @pl.when(step == 0)
    def _():
        gain_ref[...] = sums

    @pl.when(step > 0)
    def _():
        gain_ref[...] += sums


def attn_back(grad, w, x):
    tile = 128
    row = lambda width: pl.BlockSpec((tile, width), lambda i: (i, 0))
    return pl.pallas_call(
        attn_back_kernel,
        grid=(4,),
        in_specs=[row(256), pl.BlockSpec((D, 256), lambda i: (0, 0)), row(D)],
        out_specs=[row(D), pl.BlockSpec((1, D), lambda i: (0, 0))],
        out_shape=[shape((ROWS, D), BF16), shape((1, D), F32)],
        compiler_params=params(),
        name="attn_back",
        cost_estimate=takes(5),
    )(grad, w, x)


def attn_back_rest_kernel(row_ref, grad_ref, w_ref, x_ref, part_ref, out_ref, gain_ref):
    step = pl.program_id(0)
    part = dot_cols(grad_ref[...], w_ref[...])
    x = x_ref[...].astype(F32)
    sums = jnp.sum(part * (x * inverse_rms(x)), axis=0, keepdims=True)
    part = (part + part_ref[...].astype(F32)).astype(BF16)

    @pl.when(step == 0)
    def _():
        gain_ref[...] = sums

    @pl.when(step > 0)
    def _():
        gain_ref[...] += sums

    for half in range(2):
        at = pl.multiple_of(row_ref[2 * step + half] * CH, CH)
        out_ref[pl.ds(at, CH), :] = part[half * CH : (half + 1) * CH]


def attn_back_rest(row_table, grad, w, x, part):
    tile = 128
    row = lambda width: pl.BlockSpec((tile, width), lambda i, r: (i, 0))
    return pl.pallas_call(
        attn_back_rest_kernel,
        grid_spec=pltpu.PrefetchScalarGridSpec(
            num_scalar_prefetch=1,
            grid=(4,),
            in_specs=[row(128), pl.BlockSpec((D, 128), lambda i, r: (0, 2)), row(D), row(D)],
            out_specs=[
                pl.BlockSpec((ROWS, D), lambda i, r: (0, 0)),
                pl.BlockSpec((1, D), lambda i, r: (0, 0)),
            ],
        ),
        out_shape=[shape((ROWS, D), BF16), shape((1, D), F32)],
        compiler_params=params(),
        name="attn_back_rest",
        cost_estimate=takes(4),
    )(row_table, grad, w, x, part)


def weight_grad_kernel(parts, wide, *refs):
    lhs, rhs = refs[:parts], refs[parts : parts + len(wide)]
    out_ref, turned = refs[-2:]
    step = pl.program_id(0)

    @pl.when(step == 0)
    def _():
        rows = ROWS // parts
        for index, ref in enumerate(lhs):
            turned[:, index * rows : (index + 1) * rows] = ref[...].astype(F32).T.astype(BF16)

    start = 0
    for ref, count in zip(rhs, wide, strict=True):

        @pl.when((step >= start) & (step < start + count))
        def _(ref=ref):
            out_ref[...] = jnp.dot(turned[...], ref[...], preferred_element_type=F32).astype(BF16)

        start += count


def weight_grad(lhs, rhs, at, flat=None):
    wide = [a.shape[1] // 256 for a in rhs]
    starts = [sum(wide[:i]) for i in range(len(wide))]
    given = [*lhs, *rhs] + ([] if flat is None else [flat])
    specs = [pl.BlockSpec(a.shape, lambda i: (0, 0)) for a in lhs]
    for start, count in zip(starts, wide, strict=True):
        specs.append(
            pl.BlockSpec(
                (ROWS, 256),
                lambda i, start=start, count=count: (0, jnp.clip(i - start, 0, count - 1)),
            )
        )
    if flat is not None:
        specs.append(pl.BlockSpec(memory_space=pl.ANY))
    return pl.pallas_call(
        functools.partial(weight_grad_kernel, len(lhs), wide),
        grid=(sum(wide),),
        in_specs=specs,
        out_specs=pl.BlockSpec((D, 256), lambda i: (0, at + i)),
        out_shape=shape((D, FLAT_GRAD), BF16),
        scratch_shapes=[pltpu.VMEM((D, ROWS), BF16)],
        input_output_aliases={} if flat is None else {len(given) - 1: 0},
        compiler_params=params(),
        name="weight_grad",
        cost_estimate=takes(1.25 * sum(wide)),
    )(*given)


def keep_kernel(in_ref, out_ref):
    out_ref[...] = in_ref[...]


def keep(a):
    block = pl.BlockSpec((128, D), lambda i: (i, 0))
    return pl.pallas_call(
        keep_kernel,
        grid=(4,),
        in_specs=[block],
        out_specs=block,
        out_shape=shape((ROWS, D), BF16),
        compiler_params=params(),
        name="keep",
        cost_estimate=takes(2),
    )(a)


def step_kernel(wide, *refs):
    count = len(wide)
    squares = []
    for index, (given, start, columns, turned, row) in enumerate(wide):
        weight, first, second = refs[at_of(wide) + 3 * index : at_of(wide) + 3 * index + 3]
        base = at_of(wide) + 3 * count + 3 * index
        first_out, second_out, direction_out = refs[base : base + 3]
        total = None
        for part in range(2 if len(weight.shape) == 3 else 1):
            grad = refs[given][:, start : start + columns].astype(F32)
            start += columns
            if turned:
                grad = grad.T
            pick = (part,) if len(weight.shape) == 3 else (slice(None),)
            first_new, second_new, direction = adapt(weight[pick], first[pick], second[pick], grad)
            first_out[pick] = first_new
            second_out[pick] = second_new
            direction_out[pick] = direction
            sums = column_squares(direction)
            total = sums if total is None else total + sums
        squares.append((row, total))
    refs[-1][...] = eight_rows([dict(squares).get(row) for row in range(8)])


def at_of(wide):
    return 1 + max(entry[0] for entry in wide)


def take_step(grads, matrices, wide):
    given = [*grads, *[a for matrix in matrices for a in matrix]]
    outs = [shape(matrix[0].shape, F32) for matrix in matrices for _ in range(3)]
    out = pl.pallas_call(
        functools.partial(step_kernel, wide),
        grid=(1,),
        in_specs=whole_specs(given),
        out_specs=whole_specs(outs + [shape((8, 128), F32)]),
        out_shape=outs + [shape((8, 128), F32)],
        compiler_params=params(),
        name="take_step",
        cost_estimate=takes(4),
    )(*given)
    return [out[3 * i : 3 * i + 3] for i in range(len(matrices))], out[-1]


def finish_kernel(*refs):
    sums = refs[0]
    weights, directions = refs[1:5], refs[5:9]
    gains = (refs[9:12], refs[12:15])
    outs = refs[15:19]
    gain_outs = (refs[19:22], refs[22:25])
    stats_ref = refs[25]
    row = lax.broadcasted_iota(jnp.int32, (3, 6), 0)
    column = lax.broadcasted_iota(jnp.int32, (3, 6), 1)
    stats = jnp.zeros((3, 6), F32)

    def total(a):
        return jnp.sum(jnp.sum(a, axis=1, keepdims=True), axis=0, keepdims=True)

    def keep(stats, index, weight_norm, step_norm):
        ratio = weight_norm / (step_norm + EPS_ADAM)
        values = jnp.where(row == 0, weight_norm, jnp.where(row == 1, step_norm, ratio))
        return jnp.where(column == index, values, stats), ratio

    for index in range(4):
        weight_norm = jnp.sqrt(total(sums[2:3, 256 + index * 128 : 384 + index * 128]))
        step_norm = jnp.sqrt(total(sums[2:3, 768 + index * 128 : 896 + index * 128]))
        stats, ratio = keep(stats, index, weight_norm, step_norm)
        weight, direction, out = weights[index], directions[index], outs[index]
        if len(weight.shape) == 3:
            for part in range(2):
                out[part] = weight[part] - RATE * ratio * direction[part]
        else:
            out[...] = weight[...] - RATE * ratio * direction[...]
    query_gain = sums[2:3, 0:64] + sums[2:3, 64:128]
    head_grad = jnp.concatenate([query_gain, sums[2:3, 128:192]], axis=0)
    for index, grad in enumerate((sums[0:2, :], head_grad)):
        weight, first, second = (ref[...] for ref in gains[index])
        first_new, second_new, direction = adapt(weight, first, second, grad)
        weight_norm = jnp.sqrt(total(weight * weight))
        step_norm = jnp.sqrt(total(direction * direction))
        stats, ratio = keep(stats, 4 + index, weight_norm, step_norm)
        new_out, first_out, second_out = gain_outs[index]
        new_out[...] = weight - RATE * ratio * direction
        first_out[...] = first_new
        second_out[...] = second_new
    stats_ref[...] = stats


def finish(sums, weights, directions, norm_set, head_set):
    outs = [shape(w.shape, F32) for w in weights]
    outs += [shape(norm_set[0].shape, F32)] * 3 + [shape(head_set[0].shape, F32)] * 3
    outs += [shape((3, 6), F32)]
    given = (sums, *weights, *directions, *norm_set, *head_set)
    return pl.pallas_call(
        finish_kernel,
        grid=(1,),
        in_specs=whole_specs(given),
        out_specs=whole_specs(outs),
        out_shape=outs,
        compiler_params=params(),
        name="finish",
        cost_estimate=takes(3),
    )(*given)


def norm_back(grad_in, normed, inv_scale, gain):
    grad_hat = grad_in * gain
    return inv_scale * (grad_hat - normed * jnp.mean(grad_hat * normed, axis=-1, keepdims=True))


def dot_cols(a, b):
    return lax.dot_general(a, b, (((1,), (1,)), ((), ())), preferred_element_type=F32)


def in_order(a, row_table):
    chunks = a.reshape(8, CH)
    pick = row_table[:, None, None] == jnp.arange(8, dtype=jnp.int32)[None, :, None]
    return jnp.sum(jnp.where(pick, chunks[None], 0), axis=1).reshape(ROWS)


def local(
    tokens,
    segments,
    weight_qkv,
    weight_out,
    weight_gate_up,
    weight_down,
    norm_gains,
    head_gains,
    first_qkv,
    first_out,
    first_gate_up,
    first_down,
    first_norm,
    first_head,
    second_qkv,
    second_out,
    second_gate_up,
    second_down,
    second_norm,
    second_head,
    cotangent,
):
    seg_low = jnp.concatenate([segments >> 6, segments & 63]).astype(BF16).reshape(4, 256)
    seg_low = jnp.pad(seg_low, ((0, 12), (0, 128)))
    qkv_low = weight_qkv.astype(BF16)
    w_first, w_second = gather_both(jnp.concatenate([qkv_low[:64], seg_low], axis=0), qkv_low[64:])

    dp = lax.axis_index("dp")
    tensor = lax.axis_index("tensor")
    y, x = dp >> 2, dp & 3
    z, core = tensor >> 1, tensor & 1
    slots = jnp.arange(8, dtype=jnp.int32)
    row_table = 2 * ((z + slots) & 3) + (core ^ (slots >> 2))
    sixteen = jnp.arange(16, dtype=jnp.int32)
    blocks = ((((sixteen >> 2) + y) & 3) << 2) + ((sixteen + x) & 3)
    blocks_turned = ((((sixteen) + y) & 3) << 2) + (((sixteen >> 2) + x) & 3)
    own_blocks = jnp.stack([dp, 15 - dp])
    zero_slot = ((-y & 3) << 2) + (-x & 3)
    partner_slot = (((3 - 2 * y) & 3) << 2) + ((3 - 2 * x) & 3)

    down_out, gate_up, weight_squares = pack(weight_qkv, weight_out, weight_gate_up, weight_down)
    down_out = lax.all_gather(down_out, "dp", axis=0, tiled=True)
    gate_up = lax.all_gather(gate_up, "dp", axis=0, tiled=True)

    attn_in = prepare(row_table, tokens, norm_gains[0:1])
    token_ids = (row_table[:, None] * CH + jnp.arange(CH, dtype=jnp.int32)[None, :]).reshape(ROWS)
    frequency = ROPE_BASE ** (-(jnp.arange(HD // 2, dtype=F32) * 2.0 / HD))
    angles = (dp * ROWS + token_ids).astype(F32)[:, None] * jnp.tile(frequency, 4)[None, :]
    cosine, sine = jnp.cos(angles), jnp.sin(angles)
    gain_rows = jnp.concatenate(
        [
            jnp.concatenate([head_gains[0:1], head_gains[0:1]], axis=1),
            jnp.concatenate([head_gains[1:2], jnp.ones((1, HD), F32)], axis=1),
            jnp.zeros((6, 128), F32),
        ]
    )
    projected, q_own, q_send, local_kv, full_qkv, all_segs = project(
        blocks, attn_in, w_first, w_second, cosine, sine, gain_rows
    )
    kv_groups, (all_segs, tokens, cotangent) = gather_dp(local_kv, (all_segs, tokens, cotangent))
    kv_groups, (across, x_rows, dy) = beside(
        kv_groups, arrange(row_table, tokens, cotangent, attn_in)
    )

    def block_segs(slot):
        pick = (sixteen == slot)[:, None, None]
        got = jnp.sum(jnp.where(pick, all_segs[:, :4, :256].astype(jnp.int32), 0), axis=0)
        got = got.reshape(2, ROWS)
        return got[0] * 64 + got[1]

    partner_segs = block_segs(partner_slot)
    seg_rows = in_order(segments, row_table)
    first_rows = in_order(block_segs(zero_slot), row_table)
    partner_rows = in_order(partner_segs, row_table)
    kinfo = jnp.stack([seg_rows, partner_rows, first_rows, token_ids], axis=1)
    qinfo = jnp.concatenate(
        [seg_rows[None], partner_rows[None], token_ids[None], jnp.zeros((5, ROWS), jnp.int32)]
    )
    bias = jnp.concatenate(
        [
            jnp.where(seg_rows == segments[0], 0.0, OFF).astype(F32)[None],
            jnp.where(partner_rows == partner_segs[0], 0.0, OFF).astype(F32)[None],
            jnp.zeros((6, ROWS), F32),
        ]
    )
    block_info = jnp.concatenate([blocks, own_blocks])
    mixed, out_own, log_own, out_send, kv_all = attend(
        block_info, q_own, q_send, kv_groups, kinfo, qinfo, bias
    )

    far = out_project(1, mixed, down_out, BF16)
    near = out_project(0, mixed, down_out, F32)
    own_tokens = x_rows[:CH].astype(F32)
    attn_rows, grad_inner = scatter_tensor(near, far, inner_grad(dy, down_out))
    hidden_one = own_tokens + attn_rows
    scale_two = inverse_rms(hidden_one)
    normed_two = hidden_one * scale_two
    ffn_in, out_other = gather_tensor(
        (normed_two * norm_gains[1]).astype(BF16), from_partner(out_send)
    )
    inner_act, grad_gate, grad_up, near, far = feed_forward(*ffn_in, grad_inner, gate_up)

    grads = weight_grad([dy], [inner_act], 8)
    grads = weight_grad(ffn_in, [grad_gate, grad_up], 0, grads)
    grad_ffn_in, grads = scatter_tensor(near, far, grads)
    grads = lax.psum_scatter(grads, "dp", scatter_dimension=0, tiled=True)
    gain_ffn = jnp.sum(grad_ffn_in * normed_two, axis=0)
    grad_hidden = dy[:CH].astype(F32) + norm_back(grad_ffn_in, normed_two, scale_two, norm_gains[1])
    ffn_parts = ffn_out(inner_act, down_out)
    grad_attn, (ffn_near, ffn_far) = gather_tensor(grad_hidden.astype(BF16), ffn_parts)

    do_own, do_send = mixed_grad(*grad_attn, down_out)
    do_other = from_partner(do_send)
    out_parts = out_grad(blocks, *grad_attn, mixed)
    (do_other, ffn_far), out_parts = beside((do_other, from_core(ffn_far)), out_parts)
    ffn_near = (ffn_near + ffn_far.astype(F32)).reshape(4, CH, D)
    ffn_low = ffn_near.astype(BF16)
    ffn_got = {k: from_z(ffn_low[k], -k) for k in (2, 1, 3)}
    operands = ready(do_own, do_other, out_own, log_own, out_other, q_own, bias)
    dq_own, dq_send, part_u, part_v = attend_back(block_info, operands, kv_all, kinfo, qinfo)
    dq_send, ffn_got = beside(dq_send, ffn_got)
    dq_other = from_partner(dq_send)
    part_v, dq_other = beside(part_v, dq_other)
    got_u, got_v = send(part_u, from_y), send(part_v, from_x)
    grad_query, gain_query = heads_back(
        (0, 1), projected, [dq_own, dq_other], cosine, sine, gain_rows
    )
    parts = query_out_grad(blocks, across, grad_query, out_parts)
    attn_part, gain_attn = attn_back(grad_query, full_qkv, x_rows)
    (got_u, got_v), (parts, attn_part) = beside((got_u, got_v), (parts, attn_part))
    block_rows = (hidden_one + sum_four(ffn_near[0], ffn_got)).astype(BF16)
    line_u, line_v = sum_four(part_u[0], got_u), sum_four(part_v[0], got_v)
    low_u, low_v = line_u.astype(BF16), line_v.astype(BF16)
    got_u = {k: from_x(low_u[k], -k) for k in (2, 1, 3)}
    got_v = {k: from_y(low_v[k], -k) for k in (2, 1, 3)}
    grad_kv = jnp.concatenate([sum_four(line_u[0], got_u), sum_four(line_v[0], got_v)]).astype(BF16)
    grad_kv, gain_key = heads_back((2,), projected, [grad_kv], cosine, sine, gain_rows)
    parts_u, parts_v = key_grad(blocks, across, grad_kv, parts)
    got_u, got_v = send(parts_u, from_y), send(parts_v, from_x)

    grad_kv, _ = beside(grad_kv, (parts_u, parts_v))
    block_out = keep(lax.all_gather(block_rows, "tensor", axis=0, tiled=True))
    partial, gain_rest = attn_back_rest(row_table, grad_kv, full_qkv, x_rows, attn_part)
    partial, grads = beside(partial, grads)
    grad_attn_in = lax.psum_scatter(partial, "tensor", scatter_dimension=0, tiled=True).astype(F32)
    (gate_up_step, down_step), later_squares = take_step(
        [grads],
        [(weight_gate_up, first_gate_up, second_gate_up), (weight_down, first_down, second_down)],
        ((0, 0, 1024, False, 2), (0, 2048, 1024, True, 3)),
    )
    (got_u, got_v), (later_squares, block_out) = beside((got_u, got_v), (later_squares, block_out))
    late_u = scatter_rest(parts_u[0], got_u, from_x)
    late_v = scatter_rest(parts_v[0], got_v, from_y)
    grad_attn_in, _ = beside(grad_attn_in, (late_u, late_v))
    late_grad = jnp.concatenate([late_u, late_v])
    scale_one = inverse_rms(own_tokens)
    normed_one = own_tokens * scale_one
    input_grad = (
        grad_hidden + norm_back(grad_attn_in, normed_one, scale_one, norm_gains[0])
    ).astype(BF16)
    input_grad = keep(lax.all_gather(input_grad, "tensor", axis=0, tiled=True))

    (qkv_step, out_step), qkv_squares = take_step(
        [jnp.concatenate([late_grad[:, :256], late_grad[:, 512:]], axis=1), late_grad],
        [(weight_qkv, first_qkv, second_qkv), (weight_out, first_out, second_out)],
        ((0, 0, 384, False, 0), (1, 256, 256, True, 1)),
    )
    squares = jnp.concatenate(
        [
            gain_query[0:1],
            gain_key[0:1],
            weight_squares[:4].reshape(1, 512),
            (later_squares + qkv_squares)[:4].reshape(1, 512),
            jnp.zeros((1, D - 1280), F32),
        ],
        axis=1,
    )
    sums = jnp.concatenate([gain_attn + gain_rest, gain_ffn[None], squares, jnp.zeros((1, D), F32)])
    sums = sum_all(sums)
    steps = (qkv_step, out_step, gate_up_step, down_step)
    done = finish(
        sums,
        (weight_qkv, weight_out, weight_gate_up, weight_down),
        [step[2] for step in steps],
        (norm_gains, first_norm, second_norm),
        (head_gains, first_head, second_head),
    )
    return (
        block_out,
        input_grad,
        *done[:4],
        done[4],
        done[7],
        *[step[0] for step in steps],
        done[5],
        done[8],
        *[step[1] for step in steps],
        done[6],
        done[9],
        done[10],
    )


def solution(mesh):
    matrix_specs = (P("dp", "tensor"), P("tensor", "dp"), P(None, "dp", "tensor"), P("tensor", "dp"), P(), P())
    in_specs = (P("dp", None), P("dp"), *matrix_specs, *matrix_specs, *matrix_specs, P("dp", None))
    out_specs = (P("dp", None), P("dp", None), *matrix_specs, *matrix_specs, *matrix_specs, P())
    return jax.shard_map(local, mesh=mesh, in_specs=in_specs, out_specs=out_specs, check_vma=False)
```
